128 devices in a mesh: dp: 4 (over y_hi, core), mp: 32 (over y_lo, z, x).
Axes of the slice: x: 4, y: 4 (y_hi: 2, y_lo: 2; y = y_hi * 2 + y_lo), z: 4, core: 2. Of those that a mesh axis runs over, the one named last changes fastest.
Arguments:
- gradients: bfloat16 [4, 6, 6144, 1408], P('dp', None, 'mp'), may hold values from -500 to 500
- errors: float32 [4, 6, 6144, 1408], P('dp', None, 'mp'), may hold values from -3 to 3
- previous_q: float32 [6, 64, 1408], replicated, may hold values from -1 to 1, as said below
Outputs:
- new_errors: float32 [4, 6, 6144, 1408], P('dp', None, 'mp')
- new_q: float32 [6, 64, 1408], replicated
The draws below stay inside these ranges and needn't reach their ends.
Inputs may be any that keep to these rules, and one draw needn't show every extreme that they name: `previous_q`: entries of the previous Q factors, within 5 / sqrt(1408).
All inputs are finite; a program needn't handle non-finite values.
Results may differ from the reference program's by a relative error of at most 0.0003.
Values sent between devices are 32-bit elements; how exact they have to be, the bound alone decides.
A program may use at most 128 MiB of HBM per device.

```python
import jax
import jax.numpy as jnp
from jax import lax

D = 1408
FF = 6144
R = 64
MATS = 6
N_DP = 4


def draw_gradients(key, part):
    key = jax.random.fold_in(key, 11)
    key_base, key_rows, key_cols = jax.random.split(key, 3)
    shape = (N_DP, MATS, FF, D)
    row_scale = jnp.exp(jax.random.uniform(key_rows, (1, MATS, FF, 1), jnp.float32) * jnp.log(10.0))
    col_scale = jnp.exp(jax.random.uniform(key_cols, (1, MATS, 1, D), jnp.float32) * jnp.log(10.0))
    ramp = jnp.exp(jnp.log(3.0) * jnp.arange(FF, dtype=jnp.float32) / FF).reshape(1, 1, FF, 1)
    base = jnp.clip(jax.random.normal(key_base, shape, jnp.float32), -5.0, 5.0)
    return (0.2 * base * row_scale * col_scale * ramp).astype(jnp.bfloat16)


def draw_previous_q(key, part):
    key = jax.random.fold_in(key, 23)
    key_own, key_shared = jax.random.split(key, 2)
    unit = 1.0 / jnp.sqrt(jnp.float32(D))
    own = jax.random.normal(key_own, (MATS, R, D), jnp.float32)
    shared = jax.random.normal(key_shared, (MATS, 1, D), jnp.float32)
    values = (0.75 * own + 0.35 * shared) * unit
    return jnp.clip(values, -5.0 * unit, 5.0 * unit).astype(jnp.float32)


def block_scale(rng, extent, pieces, low, high):
    factor_of = 1.0
    for dim, parts in pieces:
        draws = jax.random.uniform(jax.random.fold_in(jax.random.fold_in(rng, 6), dim), (parts,), jnp.float32, low / len(pieces), high / len(pieces))
        factor_of = factor_of * jnp.repeat(jnp.exp(draws), extent[dim] // parts).reshape((-1,) + (1,) * (len(extent) - 1 - dim))
    return factor_of


def bell_draw(rng, dims, spread, reach, pieces=(), held_as=jnp.bfloat16):
    drawn = jax.random.normal(rng, dims, jnp.float32) * spread
    if len(pieces) > 0:
        drawn = block_scale(rng, dims, pieces, -0.22, 0.18) * drawn
    return jnp.clip(drawn, min=-reach, max=reach).astype(held_as)


def setup_inputs(seed: int = 0) -> dict:
    splits = jax.random.split(jax.random.key(seed), 4)
    gradients = draw_gradients(jax.random.fold_in(splits[3], 71), 0)
    errors = bell_draw(splits[1], (N_DP, MATS, FF, D), 0.5, 3.0, ((0, 4), (2, 32)), jnp.float32)
    previous_q = draw_previous_q(jax.random.fold_in(splits[3], 71), 0)
    return dict(gradients=gradients, errors=errors, previous_q=previous_q)


exact_mode = lax.Precision.HIGHEST

def compress(grads, errs, prev):
    merged = grads.astype(jnp.float32) + errs
    replicas = merged.shape[0]
    p_mat = jnp.einsum('rfd,kd->fk', merged, prev, precision=exact_mode) / replicas
    gram_mat = jnp.dot(p_mat.T, p_mat, precision=exact_mode)
    factor = jnp.linalg.cholesky(gram_mat)
    ortho = jax.scipy.linalg.solve_triangular(factor, p_mat.T, lower=True).T
    fresh = jnp.einsum('rfd,fk->kd', merged, ortho, precision=exact_mode) / replicas
    approx = jnp.dot(ortho, fresh, precision=exact_mode)
    return (merged - approx[None], fresh)

def reference(gradients, errors, previous_q):
    results = lax.map(lambda items: compress(items[0], items[1], items[2]), (jnp.moveaxis(gradients, 1, 0), jnp.moveaxis(errors, 1, 0), previous_q))
    return (jnp.moveaxis(results[0], 0, 1), results[1])
```

```python
import functools

import jax
import jax.numpy as jnp
from jax import lax
from jax.experimental import pallas as pl
from jax.experimental.pallas import tpu as pltpu
from jax.sharding import PartitionSpec as P

MESH = pl.DeviceIdType.MESH
MATS, ROWS, D, R = 6, 192, 1408, 64
HALF = ROWS // 2
BLOCK = 384
COLS = ((0, 512), (512, 512), (1024, 384))
f32, bf16 = jnp.float32, jnp.bfloat16
NT = (((1,), (1,)), ((), ()))


def dot(a, b):
    return jnp.dot(a, b, preferred_element_type=f32)


def dot_nt(a, b):
    return lax.dot_general(a, b, NT, preferred_element_type=f32)


def split(x):
    hi = x.astype(bf16)
    return hi, (x - hi.astype(f32)).astype(bf16)


def eliminate(grams, y_ref):
    row = lax.broadcasted_iota(jnp.int32, (R, 2 * R), 0)
    lane = lax.broadcasted_iota(jnp.int32, (R, 2 * R), 1)
    eye = jnp.where(lane == row + 64, 1.0, 0.0)
    unit = jnp.where(lane == row, 1.0, 0.0)
    for m in range(8):
        if m < MATS:
            gram = grams[m // 2]
            gram = pltpu.roll(gram, 64, axis=1) if m % 2 else gram
        else:
            gram = unit
        y_ref[pl.ds(m, R, stride=8), :] = jnp.where(lane < 64, gram, eye)
    rows = [y_ref[8 * i : 8 * i + 8] for i in range(R)]

    def at(r, k):
        return jnp.broadcast_to(r[:, k : k + 1], (8, 128))

    for k in range(0, R, 4):
        r0, r1, r2, r3 = rows[k : k + 4]
        s00, s01, s02, s03 = (at(r0, k + i) for i in range(4))
        s11, s12, s13 = (at(r1, k + i) for i in range(1, 4))
        s22, s23, s33 = at(r2, k + 2), at(r2, k + 3), at(r3, k + 3)
        i0 = 1.0 / s00
        l10, l20, l30 = s01 * i0, s02 * i0, s03 * i0
        d1 = s11 - l10 * s01
        t12, t13 = s12 - l10 * s02, s13 - l10 * s03
        i1 = 1.0 / d1
        l21, l31 = t12 * i1, t13 * i1
        d2 = s22 - l20 * s02 - l21 * t12
        t23 = s23 - l20 * s03 - l21 * t13
        i2 = 1.0 / d2
        l32 = t23 * i2
        d3 = s33 - l30 * s03 - l31 * t13 - l32 * t23
        i3 = 1.0 / d3
        r1 = r1 - l10 * r0
        r2 = r2 - l20 * r0 - l21 * r1
        r3 = r3 - l30 * r0 - l31 * r1 - l32 * r2
        q0, q1, q2, q3 = r0 * i0, r1 * i1, r2 * i2, r3 * i3
        for i in range(k + 4, R):
            if i < k + 8:
                c0, c1, c2, c3 = (at(rows[i], k + j) for j in range(4))
                c1 = c1 - l10 * c0
                c2 = c2 - l20 * c0 - l21 * c1
                c3 = c3 - l30 * c0 - l31 * c1 - l32 * c2
            else:
                c0, c1, c2, c3 = at(r0, i), at(r1, i), at(r2, i), at(r3, i)
            rows[i] = rows[i] - (c0 * q0 + c1 * q1) - (c2 * q2 + c3 * q3)
        for i, (r, d) in enumerate(((r0, s00), (r1, d1), (r2, d2), (r3, d3))):
            y_ref[8 * (k + i) : 8 * (k + i) + 8] = r * (1.0 / jnp.sqrt(d))
        yield


def comm_kernel(
    g_hbm, e_hbm, q_hbm, g_sum, p_out, y_out, m_hbm,
    gbuf, ebuf, qbuf, mh, ml, qst, p_own, p_recv, p_chip, p_far, g_acc,
    core_recv, recv0, recv1, q_acc, x_acc, recv2, recv3, gram_own, gram_half, gram_recv, gram_out,
    load_sem, p_send, p_arrive, c_send, c_arrive, a_send, a_arrive, b_send, b_arrive,
    gram_send, gram_arrive, store_sem,
):
    dp, mp = lax.axis_index("dp"), lax.axis_index("mp")
    y_hi, core = lax.div(dp, 2), lax.rem(dp, 2)
    x = lax.rem(mp, 4)
    z = lax.rem(lax.div(mp, 4), 4)
    y = y_hi * 2 + lax.div(mp, 16)

    def device(xx, yy, zz, cc):
        return (lax.div(yy, 2) * 2 + cc, lax.rem(yy, 2) * 16 + zz * 4 + xx)

    def flip(v):
        return v + 1 - 2 * lax.rem(v, 2)

    def side0(v):
        hi = lax.div(v, 2)
        lo = lax.rem(v, 2)
        return hi + lo - 2 * hi * lo

    def side1(v):
        return lax.div(v, 2)

    def over(*links):
        xx, yy, zz = x, y, z
        for link in links:
            if link % 3 == 0:
                xx = flip(x) if link == 0 else 3 - x
            elif link % 3 == 1:
                yy = flip(y) if link == 1 else 3 - y
            else:
                zz = flip(z) if link == 2 else 3 - z
        return device(xx, yy, zz, core)

    near = tuple(over(link) for link in range(6))
    corner = tuple(over(link, (link + 1) % 6) for link in range(6))
    sides = (side0(x), side0(y), side0(z), side1(x), side1(y), side1(z))
    twin = device(x, y, z, 1 - core)
    far = device(x, lax.rem(y + 2, 4), z, core)

    loads = []
    for m in range(MATS):
        loads.append((
            pltpu.make_async_copy(q_hbm.at[m], qbuf.at[m], load_sem.at[m, 0]),
            pltpu.make_async_copy(g_hbm.at[0, m], gbuf.at[m], load_sem.at[m, 1]),
            pltpu.make_async_copy(e_hbm.at[0, m], ebuf.at[m], load_sem.at[m, 2]),
        ))
        for copy in loads[-1]:
            copy.start()

    barrier = pltpu.get_barrier_semaphore()
    everyone = near + corner + (twin, far)
    for other in everyone:
        pl.semaphore_signal(barrier, inc=1, device_id=other, device_id_type=MESH)

    def remote(src, dst, send, arrive, target):
        copy = pltpu.make_async_remote_copy(
            src_ref=src, dst_ref=dst, send_sem=send, recv_sem=arrive,
            device_id=target, device_id_type=MESH,
        )
        copy.start()
        return copy

    mine = pl.multiple_of(core * HALF, 8)
    theirs = pl.multiple_of((1 - core) * HALF, 8)
    stores = []
    qst[...] = jnp.zeros_like(qst)
    q_acc[...] = jnp.zeros_like(q_acc)

    def local_p(j):
        total = None
        for b in range(2):
            m = 2 * j + b
            for copy in loads[m]:
                copy.wait()

            def merge(i, _, m=m):
                rows = pl.ds(pl.multiple_of(i * 16, 16), 16)
                merged = gbuf[m, rows].astype(f32) + ebuf[m, rows]
                ebuf[m, rows] = merged
                hi, lo = split(merged)
                mh[m, rows] = hi
                ml[m, rows] = lo
                return 0

            lax.fori_loop(0, ROWS // 16, merge, 0)
            store = pltpu.make_async_copy(ebuf.at[m], m_hbm.at[m], store_sem.at[m])
            store.start()
            stores.append(store)
            hi, lo = split(qbuf[m])
            qst[b, 64 * b : 64 * b + 64] = hi
            qst[b, 128 + 64 * b : 192 + 64 * b] = lo
            wide = dot_nt(mh[m], qst[b])
            part = wide[:, :128] + wide[:, 128:] + dot_nt(ml[m], qst[b, :128])
            total = part if total is None else total + part
        p_own[j] = total

    def p_chain(j):
        copy = remote(p_own.at[j, pl.ds(theirs, HALF)], p_recv.at[j], p_send.at[0, j], p_arrive.at[0, j], twin)
        yield
        copy.wait()
        p_chip[j] = p_own[j, pl.ds(mine, HALF)] + p_recv[j]
        copy = remote(p_chip.at[j], p_far.at[j], p_send.at[1, j], p_arrive.at[1, j], far)
        yield
        copy.wait()
        p_out[j, pl.ds(mine, HALF)] = (p_chip[j] + p_far[j]) * 0.25
        part = p_out.at[j, pl.ds(mine, HALF)]
        copy = remote(part, part, p_send.at[2, j], p_arrive.at[2, j], twin)
        yield
        copy.wait()
        yield

    halves = {}

    def three(src, dst, send, arrive, link):
        targets = (near[(link + 1) % 6], near[link], corner[link])
        return [remote(src(f), dst.at[f], send.at[f], arrive.at[f], targets[f]) for f in range(3)]

    def gram_chain(j):
        halves[j] = hi, lo = split(p_out[j].T)
        square = dot_nt(hi, hi) + (dot_nt(hi, lo) + dot_nt(lo, hi))
        lane = lax.broadcasted_iota(jnp.int32, (R, 2 * R), 1)
        gram_own[j] = jnp.where(lane < 64, square[:64], square[64:])
        rows = pl.ds(pl.multiple_of(core * 32, 32), 32)
        gram_half[j, 0] = gram_own[j, rows]
        for s, link in enumerate((2, 5) if j % 2 == 0 else (5, 2)):
            copies = three(
                lambda f: gram_half.at[j, s], gram_recv.at[j, s], gram_send.at[j, s], gram_arrive.at[j, s], link,
            )
            yield
            for copy in copies:
                copy.wait()
            got = gram_recv.at[j, s]
            gram_half[j, s + 1] = (gram_half[j, s] + got[1]) + (got[0] + got[2])
        copy = remote(
            gram_half.at[j, 2], gram_recv.at[j, 2, 0], gram_send.at[j, 2, 0], gram_arrive.at[j, 2, 0], near[1],
        )
        yield
        copy.wait()
        gram_out[j, rows] = gram_half[j, 2] + gram_recv[j, 2, 0]
        part = gram_out.at[j, rows]
        copy = remote(part, part, gram_send.at[j, 2, 1], gram_arrive.at[j, 2, 1], twin)
        yield
        copy.wait()

    def local_g(m):
        j, b = divmod(m, 2)
        hi, lo = halves[j]
        top = hi[64 * b : 64 * b + 64]
        both = jnp.concatenate([top, lo[64 * b : 64 * b + 64]], axis=0)
        for start, size in COLS:
            cols = slice(start, start + size)
            wide = dot(both, mh[m, :, cols])
            g_acc[m, :, cols] = wide[:64] + wide[64:] + dot(top, ml[m, :, cols])

    def g_chain(m):
        link = [(m + s) % 6 for s in range(6)]
        keep = pl.multiple_of(core * 32, 32)
        give = pl.multiple_of((1 - core) * 32, 32)
        kept0 = pl.multiple_of(core * 32 + 16 * sides[link[0]], 16)
        gone0 = pl.multiple_of(core * 32 + 16 - 16 * sides[link[0]], 16)
        kept1 = pl.multiple_of(kept0 + 8 * sides[link[1]], 8)
        gone1 = pl.multiple_of(kept0 + 8 - 8 * sides[link[1]], 8)
        hi, lo = sides[link[2]], sides[link[3]]

        def block(h, l):
            return pl.ds(pl.multiple_of((2 * h + l) * BLOCK, 128), BLOCK)

        own = block(hi, lo)
        others = (block(hi, 1 - lo), block(1 - hi, lo), block(1 - hi, 1 - lo))

        def send(s, src, dst, i):
            return remote(src, dst, a_send.at[s, m], a_arrive.at[s, m], near[link[i]])

        def forward(i, row, size):
            part = g_sum.at[m, pl.ds(row, size), pl.ds(0, D)]
            return remote(part, part, c_send.at[i, m], c_arrive.at[i, m], twin)

        copy = remote(g_acc.at[m, pl.ds(give, 32)], core_recv.at[m], c_send.at[0, m], c_arrive.at[0, m], twin)
        yield
        copy.wait()
        g_acc[m, pl.ds(keep, 32)] += core_recv[m]
        copy = send(0, g_acc.at[m, pl.ds(gone0, 16)], recv0.at[m], 0)
        yield
        copy.wait()
        g_acc[m, pl.ds(kept0, 16)] += recv0[m]
        copy = send(1, g_acc.at[m, pl.ds(gone1, 8)], recv1.at[m], 1)
        yield
        copy.wait()
        q_acc[m, :, :D] = g_acc[m, pl.ds(kept1, 8)] + recv1[m]
        copies = three(lambda f: q_acc.at[m, :, others[f]], recv2.at[m], b_send.at[0, m], b_arrive.at[0, m], link[2])
        yield
        for copy in copies:
            copy.wait()
        x_acc[m] = (q_acc[m, :, own] + recv2[m, 1]) + (recv2[m, 0] + recv2[m, 2])
        copies = three(lambda f: x_acc.at[m], recv3.at[m], b_send.at[1, m], b_arrive.at[1, m], link[4])
        yield
        for copy in copies:
            copy.wait()
        g_sum[m, pl.ds(kept1, 8), own] = (x_acc[m] + recv3[m, 1]) + (recv3[m, 0] + recv3[m, 2])
        part = g_sum.at[m, pl.ds(kept1, 8), own]
        targets = (near[link[3]], near[link[2]], corner[link[2]])
        copies = [remote(part, part, b_send.at[2, m, f], b_arrive.at[2, m, f], targets[f]) for f in range(3)]
        yield
        for copy in copies:
            copy.wait()
        part = g_sum.at[m, pl.ds(kept1, 8), pl.ds(0, D)]
        copy = send(2, part, part, 1)
        passed = [forward(1, kept1, 8)]
        yield
        copy.wait()
        part = g_sum.at[m, pl.ds(kept0, 16), pl.ds(0, D)]
        copy = send(3, part, part, 0)
        passed.append(forward(2, gone1, 8))
        yield
        copy.wait()
        passed.append(forward(3, gone0, 16))
        yield
        for copy in passed:
            copy.wait()

    pc = [p_chain(j) for j in range(3)]
    gc = [gram_chain(j) for j in range(3)]
    ac = [g_chain(m) for m in range(MATS)]
    factor = None

    def behind():
        nonlocal factor
        if factor is None:
            if all([next(chain, 1) for chain in gc]):
                factor = eliminate([gram_out[j] for j in range(3)], y_out)
        if factor is not None:
            next(factor, None)

    local_p(0)
    pl.semaphore_wait(barrier, len(everyone))
    next(pc[0])
    local_p(1)
    next(pc[1])
    next(pc[0])
    local_p(2)
    next(pc[2])
    next(pc[1])
    next(pc[0])
    next(pc[2])
    next(pc[0])
    next(gc[0])
    local_g(0)
    next(ac[0])
    next(pc[1])
    local_g(1)
    next(ac[1])
    next(pc[2])
    next(pc[1])
    next(gc[1])
    next(gc[0])
    local_g(2)
    next(ac[2])
    next(ac[0])
    local_g(3)
    next(ac[3])
    next(ac[1])
    next(pc[2])
    next(gc[2])
    next(gc[1])
    next(gc[0])
    local_g(4)
    next(ac[4])
    next(ac[2])
    local_g(5)
    next(ac[5])
    next(ac[3])
    next(gc[2])
    next(gc[1])
    next(gc[0])
    next(ac[4])
    next(ac[5])
    for s in range(8):
        for m in range(MATS):
            next(ac[m], None)
            if factor is not None or m in (2, 5):
                behind()
    for _ in factor:
        pass
    for store in stores:
        store.wait()


def finish_kernel(
    g_sum, p_ref, y_ref, m_hbm, err_hbm, q_out, mbuf, new_q, wst, load_sem, store_sem, q_sem,
):
    loads = [pltpu.make_async_copy(m_hbm.at[m], mbuf.at[m], load_sem.at[m]) for m in range(MATS)]
    for copy in loads:
        copy.start()
    lane = lax.broadcasted_iota(jnp.int32, (R, 2 * R), 1)
    wide_lane = lax.broadcasted_iota(jnp.int32, (ROWS, 2 * R), 1)
    stores = []
    for m in range(MATS):
        b = m % 2
        side = jnp.where(lane >= 64, y_ref[pl.ds(m, R, stride=8), :], 0.0)
        other = pltpu.roll(side, 64, axis=1)
        inverse = side if b else other
        bh, bl = split(jnp.concatenate([inverse, inverse], axis=0))
        ph, pl_ = split(p_ref[m // 2])
        ortho = dot_nt(ph, bh) + (dot_nt(ph, bl) + dot_nt(pl_, bh))
        oh, ol = split(ortho)
        lhs = jnp.concatenate([jnp.where(wide_lane < 64, oh, ol), oh[:, :64]], axis=1)
        lh, ll = split(side + other)
        lhs_q = jnp.concatenate([jnp.where(lane < 64, lh, ll), lh[:, :64]], axis=1)
        gh, gl = split(g_sum[m, :, :D] * 0.25)
        wst[0, 0:64] = gh
        wst[0, 64:128] = gh
        wst[0, 128:192] = gl
        fresh = dot(lhs_q, wst[0])
        new_q[m] = fresh
        store = pltpu.make_async_copy(new_q.at[m], q_out.at[m], q_sem.at[m])
        store.start()
        stores.append(store)
        nh, nl = split(fresh)
        wst[1, 0:64] = nh
        wst[1, 64:128] = nh
        wst[1, 128:192] = nl
        loads[m].wait()
        for start, size in COLS:
            cols = slice(start, start + size)
            mbuf[m, :, cols] = mbuf[m, :, cols] - dot(lhs, wst[1, :, cols])
        store = pltpu.make_async_copy(mbuf.at[m], err_hbm.at[0, m], store_sem.at[m])
        store.start()
        stores.append(store)
    for store in stores:
        store.wait()


def body(gradients, errors, previous_q):
    vmem, hbm = pl.BlockSpec(memory_space=pltpu.VMEM), pl.BlockSpec(memory_space=pl.ANY)
    far_hbm = pl.BlockSpec(memory_space=pltpu.HBM)
    sem = pltpu.SemaphoreType.DMA
    g_sum, p_mat, y_mat, merged = pl.pallas_call(
        comm_kernel,
        out_shape=(
            jax.ShapeDtypeStruct((MATS, R, 4 * BLOCK), f32),
            jax.ShapeDtypeStruct((MATS // 2, ROWS, 2 * R), f32),
            jax.ShapeDtypeStruct((8 * R, 2 * R), f32),
            jax.ShapeDtypeStruct((MATS, ROWS, D), f32),
        ),
        in_specs=[far_hbm, far_hbm, far_hbm],
        out_specs=(vmem, vmem, vmem, hbm),
        scratch_shapes=[
            pltpu.VMEM((MATS, ROWS, D), bf16),
            pltpu.VMEM((MATS, ROWS, D), f32),
            pltpu.VMEM((MATS, R, D), f32),
            pltpu.VMEM((MATS, ROWS, D), bf16),
            pltpu.VMEM((MATS, ROWS, D), bf16),
            pltpu.VMEM((2, 256, D), bf16),
            pltpu.VMEM((MATS // 2, ROWS, 128), f32),
            pltpu.VMEM((MATS // 2, HALF, 128), f32),
            pltpu.VMEM((MATS // 2, HALF, 128), f32),
            pltpu.VMEM((MATS // 2, HALF, 128), f32),
            pltpu.VMEM((MATS, R, D), f32),
            pltpu.VMEM((MATS, 32, D), f32),
            pltpu.VMEM((MATS, 16, D), f32),
            pltpu.VMEM((MATS, 8, D), f32),
            pltpu.VMEM((MATS, 8, 4 * BLOCK), f32),
            pltpu.VMEM((MATS, 8, BLOCK), f32),
            pltpu.VMEM((MATS, 3, 8, BLOCK), f32),
            pltpu.VMEM((MATS, 3, 8, BLOCK), f32),
            pltpu.VMEM((MATS // 2, R, 2 * R), f32),
            pltpu.VMEM((MATS // 2, 3, R // 2, 2 * R), f32),
            pltpu.VMEM((MATS // 2, 3, 3, R // 2, 2 * R), f32),
            pltpu.VMEM((MATS // 2, R, 2 * R), f32),
            sem((MATS, 3)),
            sem((3, 3)),
            sem((3, 3)),
            sem((4, MATS)),
            sem((4, MATS)),
            sem((4, MATS)),
            sem((4, MATS)),
            sem((3, MATS, 3)),
            sem((3, MATS, 3)),
            sem((3, 3, 3)),
            sem((3, 3, 3)),
            sem((MATS,)),
        ],
        compiler_params=pltpu.CompilerParams(
            collective_id=0, has_side_effects=True, vmem_limit_bytes=40 * 2**20
        ),
        name="compress_and_sum",
    )(*[pltpu.with_memory_space_constraint(v, pltpu.HBM) for v in (gradients, errors, previous_q)])
    return pl.pallas_call(
        finish_kernel,
        out_shape=(
            jax.ShapeDtypeStruct((1, MATS, ROWS, D), f32),
            jax.ShapeDtypeStruct((MATS, R, D), f32),
        ),
        in_specs=[vmem, vmem, vmem, hbm],
        out_specs=(far_hbm, far_hbm),
        scratch_shapes=[
            pltpu.VMEM((MATS, ROWS, D), f32),
            pltpu.VMEM((MATS, R, D), f32),
            pltpu.VMEM((2, ROWS, D), bf16),
            sem((MATS,)),
            sem((MATS,)),
            sem((MATS,)),
        ],
        compiler_params=pltpu.CompilerParams(vmem_limit_bytes=24 * 2**20),
        name="new_q_and_errors",
    )(g_sum, p_mat, y_mat, merged)


def solution(mesh):
    in_specs = (P("dp", None, "mp", None), P("dp", None, "mp", None), P())
    out_specs = (P("dp", None, "mp", None), P())
    return jax.shard_map(body, mesh=mesh, in_specs=in_specs, out_specs=out_specs, check_vma=False)
```

```python
import functools

import jax
import jax.numpy as jnp
from jax import lax
from jax.experimental import pallas as pl
from jax.experimental.pallas import tpu as pltpu
from jax.sharding import PartitionSpec as P

MESH = pl.DeviceIdType.MESH
MATS, ROWS, D, R = 6, 192, 1408, 64
HALF = ROWS // 2
BLOCK = 384
COLS = ((0, 512), (512, 512), (1024, 384))
f32, bf16 = jnp.float32, jnp.bfloat16
NT = (((1,), (1,)), ((), ()))


def dot(a, b):
    return jnp.dot(a, b, preferred_element_type=f32)


def dot_nt(a, b):
    return lax.dot_general(a, b, NT, preferred_element_type=f32)


def split(x):
    hi = x.astype(bf16)
    return hi, (x - hi.astype(f32)).astype(bf16)


def eliminate(grams, y_ref):
    row = lax.broadcasted_iota(jnp.int32, (R, 2 * R), 0)
    lane = lax.broadcasted_iota(jnp.int32, (R, 2 * R), 1)
    eye = jnp.where(lane == row + 64, 1.0, 0.0)
    unit = jnp.where(lane == row, 1.0, 0.0)
    for m in range(8):
        if m < MATS:
            gram = grams[m // 2]
            gram = pltpu.roll(gram, 64, axis=1) if m % 2 else gram
        else:
            gram = unit
        y_ref[pl.ds(m, R, stride=8), :] = jnp.where(lane < 64, gram, eye)
    rows = [y_ref[8 * i : 8 * i + 8] for i in range(R)]

    def at(r, k):
        return jnp.broadcast_to(r[:, k : k + 1], (8, 128))

    for k in range(0, R, 4):
        r0, r1, r2, r3 = rows[k : k + 4]
        s00, s01, s02, s03 = (at(r0, k + i) for i in range(4))
        s11, s12, s13 = (at(r1, k + i) for i in range(1, 4))
        s22, s23, s33 = at(r2, k + 2), at(r2, k + 3), at(r3, k + 3)
        i0 = 1.0 / s00
        l10, l20, l30 = s01 * i0, s02 * i0, s03 * i0
        d1 = s11 - l10 * s01
        t12, t13 = s12 - l10 * s02, s13 - l10 * s03
        i1 = 1.0 / d1
        l21, l31 = t12 * i1, t13 * i1
        d2 = s22 - l20 * s02 - l21 * t12
        t23 = s23 - l20 * s03 - l21 * t13
        i2 = 1.0 / d2
        l32 = t23 * i2
        d3 = s33 - l30 * s03 - l31 * t13 - l32 * t23
        i3 = 1.0 / d3
        r1 = r1 - l10 * r0
        r2 = r2 - l20 * r0 - l21 * r1
        r3 = r3 - l30 * r0 - l31 * r1 - l32 * r2
        q0, q1, q2, q3 = r0 * i0, r1 * i1, r2 * i2, r3 * i3
        for i in range(k + 4, R):
            if i < k + 8:
                c0, c1, c2, c3 = (at(rows[i], k + j) for j in range(4))
                c1 = c1 - l10 * c0
                c2 = c2 - l20 * c0 - l21 * c1
                c3 = c3 - l30 * c0 - l31 * c1 - l32 * c2
            else:
                c0, c1, c2, c3 = at(r0, i), at(r1, i), at(r2, i), at(r3, i)
            rows[i] = rows[i] - (c0 * q0 + c1 * q1) - (c2 * q2 + c3 * q3)
        for i, (r, d) in enumerate(((r0, s00), (r1, d1), (r2, d2), (r3, d3))):
            y_ref[8 * (k + i) : 8 * (k + i) + 8] = r * (1.0 / jnp.sqrt(d))
        yield


def comm_kernel(
    g_hbm, e_hbm, q_hbm, g_sum, p_out, y_out, m_hbm,
    gbuf, ebuf, qbuf, mh, ml, qst, p_own, p_recv, p_chip, p_far, g_acc,
    core_recv, recv0, recv1, q_acc, x_acc, recv2, recv3, gram_own, gram_half, gram_recv, gram_out,
    load_sem, p_send, p_arrive, c_send, c_arrive, a_send, a_arrive, b_send, b_arrive,
    gram_send, gram_arrive, store_sem,
):
    dp, mp = lax.axis_index("dp"), lax.axis_index("mp")
    y_hi, core = lax.div(dp, 2), lax.rem(dp, 2)
    x = lax.rem(mp, 4)
    z = lax.rem(lax.div(mp, 4), 4)
    y = y_hi * 2 + lax.div(mp, 16)

    def device(xx, yy, zz, cc):
        return (lax.div(yy, 2) * 2 + cc, lax.rem(yy, 2) * 16 + zz * 4 + xx)

    def flip(v):
        return v + 1 - 2 * lax.rem(v, 2)

    def side0(v):
        hi = lax.div(v, 2)
        lo = lax.rem(v, 2)
        return hi + lo - 2 * hi * lo

    def side1(v):
        return lax.div(v, 2)

    def over(*links):
        xx, yy, zz = x, y, z
        for link in links:
            if link % 3 == 0:
                xx = flip(x) if link == 0 else 3 - x
            elif link % 3 == 1:
                yy = flip(y) if link == 1 else 3 - y
            else:
                zz = flip(z) if link == 2 else 3 - z
        return device(xx, yy, zz, core)

    near = tuple(over(link) for link in range(6))
    corner = tuple(over(link, (link + 1) % 6) for link in range(6))
    sides = (side0(x), side0(y), side0(z), side1(x), side1(y), side1(z))
    twin = device(x, y, z, 1 - core)
    far = device(x, lax.rem(y + 2, 4), z, core)

    def loads(m):
        return (
            pltpu.make_async_copy(q_hbm.at[m], qbuf.at[m], load_sem.at[m, 0]),
            pltpu.make_async_copy(g_hbm.at[0, m], gbuf.at[m], load_sem.at[m, 1]),
            pltpu.make_async_copy(e_hbm.at[0, m], ebuf.at[m], load_sem.at[m, 2]),
        )

    def store(m):
        return pltpu.make_async_copy(ebuf.at[m], m_hbm.at[m], store_sem.at[m])

    def begin(m, _):
        for copy in loads(m):
            copy.start()
        return 0

    lax.fori_loop(0, MATS, begin, 0)
    barrier = pltpu.get_barrier_semaphore()
    everyone = near + corner + (twin, far)
    for other in everyone:
        pl.semaphore_signal(barrier, inc=1, device_id=other, device_id_type=MESH)

    def remote(src, dst, send, arrive, target):
        copy = pltpu.make_async_remote_copy(
            src_ref=src, dst_ref=dst, send_sem=send, recv_sem=arrive,
            device_id=target, device_id_type=MESH,
        )
        copy.start()
        return copy

    mine = pl.multiple_of(core * HALF, 8)
    theirs = pl.multiple_of((1 - core) * HALF, 8)
    p_own[...] = jnp.zeros_like(p_own)
    qst[...] = jnp.zeros_like(qst)
    q_acc[...] = jnp.zeros_like(q_acc)

    def local_p(m):
        b = lax.rem(m, 2)
        for copy in loads(m):
            copy.wait()

        def merge(i, _):
            rows = pl.ds(pl.multiple_of(i * 32, 32), 32)
            merged = gbuf[m, rows].astype(f32) + ebuf[m, rows]
            ebuf[m, rows] = merged
            hi, lo = split(merged)
            mh[m, rows] = hi
            ml[m, rows] = lo
            return 0

        lax.fori_loop(0, ROWS // 32, merge, 0)
        store(m).start()
        hi, lo = split(qbuf[m])
        at = pl.multiple_of(64 * b, 64)
        qst[b, pl.ds(at, 64)] = hi
        qst[b, pl.ds(at + 128, 64)] = lo
        wide = dot_nt(mh[m], qst[b])
        p_own[lax.div(m, 2)] += wide[:, :128] + wide[:, 128:] + dot_nt(ml[m], qst[b, :128])

    def p_copy(s, j):
        if s == 0:
            src, dst, target = p_own.at[j, pl.ds(theirs, HALF)], p_recv.at[j], twin
        elif s == 1:
            src, dst, target = p_chip.at[j], p_far.at[j], far
        else:
            src = dst = p_out.at[j, pl.ds(mine, HALF)]
            target = twin
        return pltpu.make_async_remote_copy(
            src_ref=src, dst_ref=dst, send_sem=p_send.at[s, j], recv_sem=p_arrive.at[s, j],
            device_id=target, device_id_type=MESH,
        )

    def p_step(s, j):
        if s > 0:
            p_copy(s - 1, j).wait()
        if s == 1:
            p_chip[j] = p_own[j, pl.ds(mine, HALF)] + p_recv[j]
        if s == 2:
            p_out[j, pl.ds(mine, HALF)] = (p_chip[j] + p_far[j]) * 0.25
        if s < 3:
            p_copy(s, j).start()

    def p_loop(m, _):
        local_p(m)

        @pl.when(m == 1)
        def _():
            pl.semaphore_wait(barrier, len(everyone))
            p_step(0, 0)

        @pl.when(m == 3)
        def _():
            p_step(0, 1)
            p_step(1, 0)

        @pl.when(m == 5)
        def _():
            p_step(0, 2)
            p_step(1, 1)
            p_step(2, 0)

        return 0

    halves = {}

    def three(src, dst, send, arrive, link):
        targets = (near[(link + 1) % 6], near[link], corner[link])
        return [remote(src(f), dst.at[f], send.at[f], arrive.at[f], targets[f]) for f in range(3)]

    def gram_chain(j):
        halves[j] = hi, lo = split(p_out[j].T)
        square = dot_nt(hi, hi) + (dot_nt(hi, lo) + dot_nt(lo, hi))
        lane = lax.broadcasted_iota(jnp.int32, (R, 2 * R), 1)
        gram_own[j] = jnp.where(lane < 64, square[:64], square[64:])
        rows = pl.ds(pl.multiple_of(core * 32, 32), 32)
        gram_half[j, 0] = gram_own[j, rows]
        for s, link in enumerate((2, 5) if j % 2 == 0 else (5, 2)):
            copies = three(
                lambda f: gram_half.at[j, s], gram_recv.at[j, s], gram_send.at[j, s], gram_arrive.at[j, s], link,
            )
            yield
            for copy in copies:
                copy.wait()
            got = gram_recv.at[j, s]
            gram_half[j, s + 1] = (gram_half[j, s] + got[1]) + (got[0] + got[2])
        copy = remote(
            gram_half.at[j, 2], gram_recv.at[j, 2, 0], gram_send.at[j, 2, 0], gram_arrive.at[j, 2, 0], near[1],
        )
        yield
        copy.wait()
        gram_out[j, rows] = gram_half[j, 2] + gram_recv[j, 2, 0]
        part = gram_out.at[j, rows]
        copy = remote(part, part, gram_send.at[j, 2, 1], gram_arrive.at[j, 2, 1], twin)
        yield
        copy.wait()

    def local_g(m):
        j, b = divmod(m, 2)
        hi, lo = halves[j]
        top = hi[64 * b : 64 * b + 64]
        both = jnp.concatenate([top, lo[64 * b : 64 * b + 64]], axis=0)
        for start, size in COLS:
            cols = slice(start, start + size)
            wide = dot(both, mh[m, :, cols])
            g_acc[m, :, cols] = wide[:64] + wide[64:] + dot(top, ml[m, :, cols])

    def g_chain(m):
        link = [(m + s) % 6 for s in range(6)]
        keep = pl.multiple_of(core * 32, 32)
        give = pl.multiple_of((1 - core) * 32, 32)
        kept0 = pl.multiple_of(core * 32 + 16 * sides[link[0]], 16)
        gone0 = pl.multiple_of(core * 32 + 16 - 16 * sides[link[0]], 16)
        kept1 = pl.multiple_of(kept0 + 8 * sides[link[1]], 8)
        gone1 = pl.multiple_of(kept0 + 8 - 8 * sides[link[1]], 8)
        hi, lo = sides[link[2]], sides[link[3]]

        def block(h, l):
            return pl.ds(pl.multiple_of((2 * h + l) * BLOCK, 128), BLOCK)

        own = block(hi, lo)
        others = (block(hi, 1 - lo), block(1 - hi, lo), block(1 - hi, 1 - lo))

        def send(s, src, dst, i):
            return remote(src, dst, a_send.at[s, m], a_arrive.at[s, m], near[link[i]])

        def forward(i, row, size):
            part = g_sum.at[m, pl.ds(row, size), pl.ds(0, D)]
            return remote(part, part, c_send.at[i, m], c_arrive.at[i, m], twin)

        copy = remote(g_acc.at[m, pl.ds(give, 32)], core_recv.at[m], c_send.at[0, m], c_arrive.at[0, m], twin)
        yield
        copy.wait()
        g_acc[m, pl.ds(keep, 32)] += core_recv[m]
        copy = send(0, g_acc.at[m, pl.ds(gone0, 16)], recv0.at[m], 0)
        yield
        copy.wait()
        g_acc[m, pl.ds(kept0, 16)] += recv0[m]
        copy = send(1, g_acc.at[m, pl.ds(gone1, 8)], recv1.at[m], 1)
        yield
        copy.wait()
        q_acc[m, :, :D] = g_acc[m, pl.ds(kept1, 8)] + recv1[m]
        copies = three(lambda f: q_acc.at[m, :, others[f]], recv2.at[m], b_send.at[0, m], b_arrive.at[0, m], link[2])
        yield
        for copy in copies:
            copy.wait()
        x_acc[m] = (q_acc[m, :, own] + recv2[m, 1]) + (recv2[m, 0] + recv2[m, 2])
        copies = three(lambda f: x_acc.at[m], recv3.at[m], b_send.at[1, m], b_arrive.at[1, m], link[4])
        yield
        for copy in copies:
            copy.wait()
        g_sum[m, pl.ds(kept1, 8), own] = (x_acc[m] + recv3[m, 1]) + (recv3[m, 0] + recv3[m, 2])
        part = g_sum.at[m, pl.ds(kept1, 8), own]
        targets = (near[link[3]], near[link[2]], corner[link[2]])
        copies = [remote(part, part, b_send.at[2, m, f], b_arrive.at[2, m, f], targets[f]) for f in range(3)]
        yield
        for copy in copies:
            copy.wait()
        part = g_sum.at[m, pl.ds(kept1, 8), pl.ds(0, D)]
        copy = send(2, part, part, 1)
        passed = [forward(1, kept1, 8)]
        yield
        copy.wait()
        part = g_sum.at[m, pl.ds(kept0, 16), pl.ds(0, D)]
        copy = send(3, part, part, 0)
        passed.append(forward(2, gone1, 8))
        yield
        copy.wait()
        passed.append(forward(3, gone0, 16))
        yield
        for copy in passed:
            copy.wait()

    gc = [gram_chain(j) for j in range(3)]
    ac = [g_chain(m) for m in range(MATS)]
    factor = None

    def behind():
        nonlocal factor
        if factor is None:
            if all([next(chain, 1) for chain in gc]):
                factor = eliminate([gram_out[j] for j in range(3)], y_out)
        if factor is not None:
            next(factor, None)

    lax.fori_loop(0, MATS, p_loop, 0)
    p_step(1, 2)
    p_step(3, 0)
    next(gc[0])
    local_g(0)
    next(ac[0])
    p_step(2, 1)
    local_g(1)
    next(ac[1])
    p_step(2, 2)
    p_step(3, 1)
    next(gc[1])
    next(gc[0])
    local_g(2)
    next(ac[2])
    next(ac[0])
    local_g(3)
    next(ac[3])
    next(ac[1])
    p_step(3, 2)
    next(gc[2])
    next(gc[1])
    next(gc[0])
    local_g(4)
    next(ac[4])
    next(ac[2])
    local_g(5)
    next(ac[5])
    next(ac[3])
    next(gc[2])
    next(gc[1])
    next(gc[0])
    next(ac[4])
    next(ac[5])
    for s in range(8):
        for m in range(MATS):
            next(ac[m], None)
            if factor is not None or m in (2, 5):
                behind()
    for _ in factor:
        pass
    for m in range(MATS):
        store(m).wait()


def finish_kernel(
    g_sum, p_ref, y_ref, m_hbm, err_hbm, q_out, mbuf, new_q, wst, load_sem, store_sem, q_sem,
):
    def load(m):
        return pltpu.make_async_copy(m_hbm.at[m], mbuf.at[m], load_sem.at[m])

    def store_q(m):
        return pltpu.make_async_copy(new_q.at[m], q_out.at[m], q_sem.at[m])

    def store_err(m):
        return pltpu.make_async_copy(mbuf.at[m], err_hbm.at[0, m], store_sem.at[m])

    def begin(m, _):
        load(m).start()
        return 0

    def end(m, _):
        store_q(m).wait()
        store_err(m).wait()
        return 0

    lane = lax.broadcasted_iota(jnp.int32, (R, 2 * R), 1)
    wide_lane = lax.broadcasted_iota(jnp.int32, (ROWS, 2 * R), 1)

    def step(m, _):
        b = lax.rem(m, 2)
        side = jnp.where(lane >= 64, y_ref[pl.ds(m, R, stride=8), :], 0.0)
        both = side + pltpu.roll(side, 64, axis=1)
        inverse = jnp.where((lane >= 64) == (b == 1), both, 0.0)
        bh, bl = split(jnp.concatenate([inverse, inverse], axis=0))
        ph, pl_ = split(p_ref[lax.div(m, 2)])
        ortho = dot_nt(ph, bh) + (dot_nt(ph, bl) + dot_nt(pl_, bh))
        oh, ol = split(ortho)
        lhs = jnp.concatenate([jnp.where(wide_lane < 64, oh, ol), oh[:, :64]], axis=1)
        lh, ll = split(both)
        lhs_q = jnp.concatenate([jnp.where(lane < 64, lh, ll), lh[:, :64]], axis=1)
        gh, gl = split(g_sum[m, :, :D] * 0.25)
        wst[0, 0:64] = gh
        wst[0, 64:128] = gh
        wst[0, 128:192] = gl
        fresh = dot(lhs_q, wst[0])
        new_q[m] = fresh
        store_q(m).start()
        nh, nl = split(fresh)
        wst[1, 0:64] = nh
        wst[1, 64:128] = nh
        wst[1, 128:192] = nl
        load(m).wait()
        for start, size in COLS:
            cols = slice(start, start + size)
            mbuf[m, :, cols] = mbuf[m, :, cols] - dot(lhs, wst[1, :, cols])
        store_err(m).start()
        return 0

    lax.fori_loop(0, MATS, begin, 0)
    lax.fori_loop(0, MATS, step, 0)
    lax.fori_loop(0, MATS, end, 0)


def body(gradients, errors, previous_q):
    vmem, hbm = pl.BlockSpec(memory_space=pltpu.VMEM), pl.BlockSpec(memory_space=pl.ANY)
    far_hbm = pl.BlockSpec(memory_space=pltpu.HBM)
    sem = pltpu.SemaphoreType.DMA
    g_sum, p_mat, y_mat, merged = pl.pallas_call(
        comm_kernel,
        out_shape=(
            jax.ShapeDtypeStruct((MATS, R, 4 * BLOCK), f32),
            jax.ShapeDtypeStruct((MATS // 2, ROWS, 2 * R), f32),
            jax.ShapeDtypeStruct((8 * R, 2 * R), f32),
            jax.ShapeDtypeStruct((MATS, ROWS, D), f32),
        ),
        in_specs=[far_hbm, far_hbm, far_hbm],
        out_specs=(vmem, vmem, vmem, hbm),
        scratch_shapes=[
            pltpu.VMEM((MATS, ROWS, D), bf16),
            pltpu.VMEM((MATS, ROWS, D), f32),
            pltpu.VMEM((MATS, R, D), f32),
            pltpu.VMEM((MATS, ROWS, D), bf16),
            pltpu.VMEM((MATS, ROWS, D), bf16),
            pltpu.VMEM((2, 256, D), bf16),
            pltpu.VMEM((MATS // 2, ROWS, 128), f32),
            pltpu.VMEM((MATS // 2, HALF, 128), f32),
            pltpu.VMEM((MATS // 2, HALF, 128), f32),
            pltpu.VMEM((MATS // 2, HALF, 128), f32),
            pltpu.VMEM((MATS, R, D), f32),
            pltpu.VMEM((MATS, 32, D), f32),
            pltpu.VMEM((MATS, 16, D), f32),
            pltpu.VMEM((MATS, 8, D), f32),
            pltpu.VMEM((MATS, 8, 4 * BLOCK), f32),
            pltpu.VMEM((MATS, 8, BLOCK), f32),
            pltpu.VMEM((MATS, 3, 8, BLOCK), f32),
            pltpu.VMEM((MATS, 3, 8, BLOCK), f32),
            pltpu.VMEM((MATS // 2, R, 2 * R), f32),
            pltpu.VMEM((MATS // 2, 3, R // 2, 2 * R), f32),
            pltpu.VMEM((MATS // 2, 3, 3, R // 2, 2 * R), f32),
            pltpu.VMEM((MATS // 2, R, 2 * R), f32),
            sem((MATS, 3)),
            sem((3, 3)),
            sem((3, 3)),
            sem((4, MATS)),
            sem((4, MATS)),
            sem((4, MATS)),
            sem((4, MATS)),
            sem((3, MATS, 3)),
            sem((3, MATS, 3)),
            sem((3, 3, 3)),
            sem((3, 3, 3)),
            sem((MATS,)),
        ],
        compiler_params=pltpu.CompilerParams(
            collective_id=0, has_side_effects=True, vmem_limit_bytes=40 * 2**20
        ),
        name="compress_and_sum",
    )(*[pltpu.with_memory_space_constraint(v, pltpu.HBM) for v in (gradients, errors, previous_q)])
    return pl.pallas_call(
        finish_kernel,
        out_shape=(
            jax.ShapeDtypeStruct((1, MATS, ROWS, D), f32),
            jax.ShapeDtypeStruct((MATS, R, D), f32),
        ),
        in_specs=[vmem, vmem, vmem, hbm],
        out_specs=(far_hbm, far_hbm),
        scratch_shapes=[
            pltpu.VMEM((MATS, ROWS, D), f32),
            pltpu.VMEM((MATS, R, D), f32),
            pltpu.VMEM((2, ROWS, D), bf16),
            sem((MATS,)),
            sem((MATS,)),
            sem((MATS,)),
        ],
        compiler_params=pltpu.CompilerParams(vmem_limit_bytes=24 * 2**20),
        name="new_q_and_errors",
    )(g_sum, p_mat, y_mat, merged)


def solution(mesh):
    in_specs = (P("dp", None, "mp", None), P("dp", None, "mp", None), P())
    out_specs = (P("dp", None, "mp", None), P())
    return jax.shard_map(body, mesh=mesh, in_specs=in_specs, out_specs=out_specs, check_vma=False)
```

```python
import functools

import jax
import jax.numpy as jnp
from jax import lax
from jax.experimental import pallas as pl
from jax.experimental.pallas import tpu as pltpu
from jax.sharding import PartitionSpec as P

MESH = pl.DeviceIdType.MESH
MATS, ROWS, D, R = 6, 192, 1408, 64
HALF = ROWS // 2
BLOCK = 384
COLS = ((0, 512), (512, 512), (1024, 384))
f32, bf16 = jnp.float32, jnp.bfloat16
NT = (((1,), (1,)), ((), ()))


def dot(a, b):
    return jnp.dot(a, b, preferred_element_type=f32)


def dot_nt(a, b):
    return lax.dot_general(a, b, NT, preferred_element_type=f32)


def split(x):
    hi = x.astype(bf16)
    return hi, (x - hi.astype(f32)).astype(bf16)


def eliminate(grams, y_ref):
    row = lax.broadcasted_iota(jnp.int32, (R, 2 * R), 0)
    lane = lax.broadcasted_iota(jnp.int32, (R, 2 * R), 1)
    eye = jnp.where(lane == row + 64, 1.0, 0.0)
    unit = jnp.where(lane == row, 1.0, 0.0)
    for m in range(8):
        if m < MATS:
            gram = grams[m // 2]
            gram = pltpu.roll(gram, 64, axis=1) if m % 2 else gram
        else:
            gram = unit
        y_ref[pl.ds(m, R, stride=8), :] = jnp.where(lane < 64, gram, eye)
    rows = [y_ref[8 * i : 8 * i + 8] for i in range(R)]

    def at(r, k):
        return jnp.broadcast_to(r[:, k : k + 1], (8, 128))

    for k in range(0, R, 4):
        r0, r1, r2, r3 = rows[k : k + 4]
        s00, s01, s02, s03 = (at(r0, k + i) for i in range(4))
        s11, s12, s13 = (at(r1, k + i) for i in range(1, 4))
        s22, s23, s33 = at(r2, k + 2), at(r2, k + 3), at(r3, k + 3)
        i0 = 1.0 / s00
        l10, l20, l30 = s01 * i0, s02 * i0, s03 * i0
        d1 = s11 - l10 * s01
        t12, t13 = s12 - l10 * s02, s13 - l10 * s03
        i1 = 1.0 / d1
        l21, l31 = t12 * i1, t13 * i1
        d2 = s22 - l20 * s02 - l21 * t12
        t23 = s23 - l20 * s03 - l21 * t13
        i2 = 1.0 / d2
        l32 = t23 * i2
        d3 = s33 - l30 * s03 - l31 * t13 - l32 * t23
        i3 = 1.0 / d3
        r1 = r1 - l10 * r0
        r2 = r2 - l20 * r0 - l21 * r1
        r3 = r3 - l30 * r0 - l31 * r1 - l32 * r2
        q0, q1, q2, q3 = r0 * i0, r1 * i1, r2 * i2, r3 * i3
        for i in range(k + 4, R):
            if i < k + 8:
                c0, c1, c2, c3 = (at(rows[i], k + j) for j in range(4))
                c1 = c1 - l10 * c0
                c2 = c2 - l20 * c0 - l21 * c1
                c3 = c3 - l30 * c0 - l31 * c1 - l32 * c2
            else:
                c0, c1, c2, c3 = at(r0, i), at(r1, i), at(r2, i), at(r3, i)
            rows[i] = rows[i] - (c0 * q0 + c1 * q1) - (c2 * q2 + c3 * q3)
        for i, (r, d) in enumerate(((r0, s00), (r1, d1), (r2, d2), (r3, d3))):
            y_ref[8 * (k + i) : 8 * (k + i) + 8] = r * (1.0 / jnp.sqrt(d))
        yield


def comm_kernel(
    g_hbm, e_hbm, q_hbm, g_sum, p_out, y_out, ebuf,
    gbuf, qbuf, mh, ml, qst, p_own, p_recv, p_chip, p_far, g_acc,
    core_recv, recv0, recv1, q_acc, x_acc, recv2, recv3, gram_own, gram_half, gram_recv, gram_out,
    load_sem, p_send, p_arrive, c_send, c_arrive, a_send, a_arrive, b_send, b_arrive,
    gram_send, gram_arrive,
):
    dp, mp = lax.axis_index("dp"), lax.axis_index("mp")
    y_hi, core = lax.div(dp, 2), lax.rem(dp, 2)
    x = lax.rem(mp, 4)
    z = lax.rem(lax.div(mp, 4), 4)
    y = y_hi * 2 + lax.div(mp, 16)

    def device(xx, yy, zz, cc):
        return (lax.div(yy, 2) * 2 + cc, lax.rem(yy, 2) * 16 + zz * 4 + xx)

    def flip(v):
        return v + 1 - 2 * lax.rem(v, 2)

    def side0(v):
        hi = lax.div(v, 2)
        lo = lax.rem(v, 2)
        return hi + lo - 2 * hi * lo

    def side1(v):
        return lax.div(v, 2)

    def over(*links):
        xx, yy, zz = x, y, z
        for link in links:
            if link % 3 == 0:
                xx = flip(x) if link == 0 else 3 - x
            elif link % 3 == 1:
                yy = flip(y) if link == 1 else 3 - y
            else:
                zz = flip(z) if link == 2 else 3 - z
        return device(xx, yy, zz, core)

    near = tuple(over(link) for link in range(6))
    corner = tuple(over(link, (link + 1) % 6) for link in range(6))
    sides = (side0(x), side0(y), side0(z), side1(x), side1(y), side1(z))
    twin = device(x, y, z, 1 - core)
    far = device(x, lax.rem(y + 2, 4), z, core)

    def loads(m):
        return (
            pltpu.make_async_copy(q_hbm.at[m], qbuf.at[m], load_sem.at[m, 0]),
            pltpu.make_async_copy(g_hbm.at[0, m], gbuf.at[m], load_sem.at[m, 1]),
            pltpu.make_async_copy(e_hbm.at[0, m], ebuf.at[m], load_sem.at[m, 2]),
        )

    def begin(m, _):
        for copy in loads(m):
            copy.start()
        return 0

    lax.fori_loop(0, MATS, begin, 0)
    barrier = pltpu.get_barrier_semaphore()
    everyone = near + corner + (twin, far)
    for other in everyone:
        pl.semaphore_signal(barrier, inc=1, device_id=other, device_id_type=MESH)

    def remote(src, dst, send, arrive, target):
        copy = pltpu.make_async_remote_copy(
            src_ref=src, dst_ref=dst, send_sem=send, recv_sem=arrive,
            device_id=target, device_id_type=MESH,
        )
        copy.start()
        return copy

    mine = pl.multiple_of(core * HALF, 8)
    theirs = pl.multiple_of((1 - core) * HALF, 8)
    p_own[...] = jnp.zeros_like(p_own)
    qst[...] = jnp.zeros_like(qst)
    q_acc[...] = jnp.zeros_like(q_acc)

    def local_p(m):
        b = lax.rem(m, 2)
        for copy in loads(m):
            copy.wait()

        def merge(i, _):
            rows = pl.ds(pl.multiple_of(i * 32, 32), 32)
            merged = gbuf[m, rows].astype(f32) + ebuf[m, rows]
            ebuf[m, rows] = merged
            hi, lo = split(merged)
            mh[m, rows] = hi
            ml[m, rows] = lo
            return 0

        lax.fori_loop(0, ROWS // 32, merge, 0)
        hi, lo = split(qbuf[m])
        at = pl.multiple_of(64 * b, 64)
        qst[b, pl.ds(at, 64)] = hi
        qst[b, pl.ds(at + 128, 64)] = lo
        wide = dot_nt(mh[m], qst[b])
        p_own[lax.div(m, 2)] += wide[:, :128] + wide[:, 128:] + dot_nt(ml[m], qst[b, :128])

    def p_copy(s, j):
        if s == 0:
            src, dst, target = p_own.at[j, pl.ds(theirs, HALF)], p_recv.at[j], twin
        elif s == 1:
            src, dst, target = p_chip.at[j], p_far.at[j], far
        else:
            src = dst = p_out.at[j, pl.ds(mine, HALF)]
            target = twin
        return pltpu.make_async_remote_copy(
            src_ref=src, dst_ref=dst, send_sem=p_send.at[s, j], recv_sem=p_arrive.at[s, j],
            device_id=target, device_id_type=MESH,
        )

    def p_step(s, j):
        if s > 0:
            p_copy(s - 1, j).wait()
        if s == 1:
            p_chip[j] = p_own[j, pl.ds(mine, HALF)] + p_recv[j]
        if s == 2:
            p_out[j, pl.ds(mine, HALF)] = (p_chip[j] + p_far[j]) * 0.25
        if s < 3:
            p_copy(s, j).start()

    def p_loop(m, _):
        local_p(m)

        @pl.when(m == 1)
        def _():
            pl.semaphore_wait(barrier, len(everyone))
            p_step(0, 0)

        @pl.when(m == 3)
        def _():
            p_step(0, 1)
            p_step(1, 0)

        @pl.when(m == 5)
        def _():
            p_step(0, 2)
            p_step(1, 1)
            p_step(2, 0)

        return 0

    halves = {}

    def three(src, dst, send, arrive, link):
        targets = (near[(link + 1) % 6], near[link], corner[link])
        return [remote(src(f), dst.at[f], send.at[f], arrive.at[f], targets[f]) for f in range(3)]

    def gram_chain(j):
        halves[j] = hi, lo = split(p_out[j].T)
        square = dot_nt(hi, hi) + (dot_nt(hi, lo) + dot_nt(lo, hi))
        lane = lax.broadcasted_iota(jnp.int32, (R, 2 * R), 1)
        gram_own[j] = jnp.where(lane < 64, square[:64], square[64:])
        rows = pl.ds(pl.multiple_of(core * 32, 32), 32)
        gram_half[j, 0] = gram_own[j, rows]
        for s, link in enumerate((2, 5) if j % 2 == 0 else (5, 2)):
            copies = three(
                lambda f: gram_half.at[j, s], gram_recv.at[j, s], gram_send.at[j, s], gram_arrive.at[j, s], link,
            )
            yield
            for copy in copies:
                copy.wait()
            got = gram_recv.at[j, s]
            gram_half[j, s + 1] = (gram_half[j, s] + got[1]) + (got[0] + got[2])
        copy = remote(
            gram_half.at[j, 2], gram_recv.at[j, 2, 0], gram_send.at[j, 2, 0], gram_arrive.at[j, 2, 0], near[1],
        )
        yield
        copy.wait()
        gram_out[j, rows] = gram_half[j, 2] + gram_recv[j, 2, 0]
        part = gram_out.at[j, rows]
        copy = remote(part, part, gram_send.at[j, 2, 1], gram_arrive.at[j, 2, 1], twin)
        yield
        copy.wait()

    def local_g(m):
        j, b = divmod(m, 2)
        hi, lo = halves[j]
        top = hi[64 * b : 64 * b + 64]
        both = jnp.concatenate([top, lo[64 * b : 64 * b + 64]], axis=0)
        for start, size in COLS:
            cols = slice(start, start + size)
            wide = dot(both, mh[m, :, cols])
            g_acc[m, :, cols] = wide[:64] + wide[64:] + dot(top, ml[m, :, cols])

    def g_chain(m):
        link = [(m + s) % 6 for s in range(6)]
        keep = pl.multiple_of(core * 32, 32)
        give = pl.multiple_of((1 - core) * 32, 32)
        kept0 = pl.multiple_of(core * 32 + 16 * sides[link[0]], 16)
        gone0 = pl.multiple_of(core * 32 + 16 - 16 * sides[link[0]], 16)
        kept1 = pl.multiple_of(kept0 + 8 * sides[link[1]], 8)
        gone1 = pl.multiple_of(kept0 + 8 - 8 * sides[link[1]], 8)
        hi, lo = sides[link[2]], sides[link[3]]

        def block(h, l):
            return pl.ds(pl.multiple_of((2 * h + l) * BLOCK, 128), BLOCK)

        own = block(hi, lo)
        others = (block(hi, 1 - lo), block(1 - hi, lo), block(1 - hi, 1 - lo))

        def send(s, src, dst, i):
            return remote(src, dst, a_send.at[s, m], a_arrive.at[s, m], near[link[i]])

        def forward(i, row, size):
            part = g_sum.at[m, pl.ds(row, size), pl.ds(0, D)]
            return remote(part, part, c_send.at[i, m], c_arrive.at[i, m], twin)

        copy = remote(g_acc.at[m, pl.ds(give, 32)], core_recv.at[m], c_send.at[0, m], c_arrive.at[0, m], twin)
        yield
        copy.wait()
        g_acc[m, pl.ds(keep, 32)] += core_recv[m]
        copy = send(0, g_acc.at[m, pl.ds(gone0, 16)], recv0.at[m], 0)
        yield
        copy.wait()
        g_acc[m, pl.ds(kept0, 16)] += recv0[m]
        copy = send(1, g_acc.at[m, pl.ds(gone1, 8)], recv1.at[m], 1)
        yield
        copy.wait()
        q_acc[m, :, :D] = g_acc[m, pl.ds(kept1, 8)] + recv1[m]
        copies = three(lambda f: q_acc.at[m, :, others[f]], recv2.at[m], b_send.at[0, m], b_arrive.at[0, m], link[2])
        yield
        for copy in copies:
            copy.wait()
        x_acc[m] = (q_acc[m, :, own] + recv2[m, 1]) + (recv2[m, 0] + recv2[m, 2])
        copies = three(lambda f: x_acc.at[m], recv3.at[m], b_send.at[1, m], b_arrive.at[1, m], link[4])
        yield
        for copy in copies:
            copy.wait()
        g_sum[m, pl.ds(kept1, 8), own] = (x_acc[m] + recv3[m, 1]) + (recv3[m, 0] + recv3[m, 2])
        part = g_sum.at[m, pl.ds(kept1, 8), own]
        targets = (near[link[3]], near[link[2]], corner[link[2]])
        copies = [remote(part, part, b_send.at[2, m, f], b_arrive.at[2, m, f], targets[f]) for f in range(3)]
        yield
        for copy in copies:
            copy.wait()
        part = g_sum.at[m, pl.ds(kept1, 8), pl.ds(0, D)]
        copy = send(2, part, part, 1)
        passed = [forward(1, kept1, 8)]
        yield
        copy.wait()
        part = g_sum.at[m, pl.ds(kept0, 16), pl.ds(0, D)]
        copy = send(3, part, part, 0)
        passed.append(forward(2, gone1, 8))
        yield
        copy.wait()
        passed.append(forward(3, gone0, 16))
        yield
        for copy in passed:
            copy.wait()

    gc = [gram_chain(j) for j in range(3)]
    ac = [g_chain(m) for m in range(MATS)]
    factor = None

    def behind():
        nonlocal factor
        if factor is None:
            if all([next(chain, 1) for chain in gc]):
                factor = eliminate([gram_out[j] for j in range(3)], y_out)
        if factor is not None:
            next(factor, None)

    lax.fori_loop(0, MATS, p_loop, 0)
    p_step(1, 2)
    p_step(3, 0)
    next(gc[0])
    local_g(0)
    next(ac[0])
    p_step(2, 1)
    local_g(1)
    next(ac[1])
    p_step(2, 2)
    p_step(3, 1)
    next(gc[1])
    next(gc[0])
    local_g(2)
    next(ac[2])
    next(ac[0])
    local_g(3)
    next(ac[3])
    next(ac[1])
    p_step(3, 2)
    next(gc[2])
    next(gc[1])
    next(gc[0])
    local_g(4)
    next(ac[4])
    next(ac[2])
    local_g(5)
    next(ac[5])
    next(ac[3])
    next(gc[2])
    next(gc[1])
    next(gc[0])
    next(ac[4])
    next(ac[5])
    for s in range(8):
        for m in range(MATS):
            next(ac[m], None)
            if factor is not None or m in (2, 5):
                behind()
    for _ in factor:
        pass


def finish_kernel(
    g_sum, p_ref, y_ref, m_ref, err_hbm, q_out, mbuf, new_q, wst, store_sem, q_sem,
):
    lane = lax.broadcasted_iota(jnp.int32, (R, 2 * R), 1)
    wide_lane = lax.broadcasted_iota(jnp.int32, (ROWS, 2 * R), 1)
    stores = []
    for m in range(MATS):
        b = m % 2
        side = jnp.where(lane >= 64, y_ref[pl.ds(m, R, stride=8), :], 0.0)
        other = pltpu.roll(side, 64, axis=1)
        inverse = side if b else other
        bh, bl = split(jnp.concatenate([inverse, inverse], axis=0))
        ph, pl_ = split(p_ref[m // 2])
        ortho = dot_nt(ph, bh) + (dot_nt(ph, bl) + dot_nt(pl_, bh))
        oh, ol = split(ortho)
        lhs = jnp.concatenate([jnp.where(wide_lane < 64, oh, ol), oh[:, :64]], axis=1)
        lh, ll = split(side + other)
        lhs_q = jnp.concatenate([jnp.where(lane < 64, lh, ll), lh[:, :64]], axis=1)
        gh, gl = split(g_sum[m, :, :D] * 0.25)
        wst[0, 0:64] = gh
        wst[0, 64:128] = gh
        wst[0, 128:192] = gl
        fresh = dot(lhs_q, wst[0])
        new_q[m] = fresh
        store = pltpu.make_async_copy(new_q.at[m], q_out.at[m], q_sem.at[m])
        store.start()
        stores.append(store)
        nh, nl = split(fresh)
        wst[1, 0:64] = nh
        wst[1, 64:128] = nh
        wst[1, 128:192] = nl
        for start, size in COLS:
            cols = slice(start, start + size)
            mbuf[m, :, cols] = m_ref[m, :, cols] - dot(lhs, wst[1, :, cols])
        store = pltpu.make_async_copy(mbuf.at[m], err_hbm.at[0, m], store_sem.at[m])
        store.start()
        stores.append(store)
    for store in stores:
        store.wait()


def body(gradients, errors, previous_q):
    vmem = pl.BlockSpec(memory_space=pltpu.VMEM)
    far_hbm = pl.BlockSpec(memory_space=pltpu.HBM)
    sem = pltpu.SemaphoreType.DMA
    g_sum, p_mat, y_mat, merged = pl.pallas_call(
        comm_kernel,
        out_shape=(
            jax.ShapeDtypeStruct((MATS, R, 4 * BLOCK), f32),
            jax.ShapeDtypeStruct((MATS // 2, ROWS, 2 * R), f32),
            jax.ShapeDtypeStruct((8 * R, 2 * R), f32),
            jax.ShapeDtypeStruct((MATS, ROWS, D), f32),
        ),
        in_specs=[far_hbm, far_hbm, far_hbm],
        out_specs=(vmem, vmem, vmem, vmem),
        scratch_shapes=[
            pltpu.VMEM((MATS, ROWS, D), bf16),
            pltpu.VMEM((MATS, R, D), f32),
            pltpu.VMEM((MATS, ROWS, D), bf16),
            pltpu.VMEM((MATS, ROWS, D), bf16),
            pltpu.VMEM((2, 256, D), bf16),
            pltpu.VMEM((MATS // 2, ROWS, 128), f32),
            pltpu.VMEM((MATS // 2, HALF, 128), f32),
            pltpu.VMEM((MATS // 2, HALF, 128), f32),
            pltpu.VMEM((MATS // 2, HALF, 128), f32),
            pltpu.VMEM((MATS, R, D), f32),
            pltpu.VMEM((MATS, 32, D), f32),
            pltpu.VMEM((MATS, 16, D), f32),
            pltpu.VMEM((MATS, 8, D), f32),
            pltpu.VMEM((MATS, 8, 4 * BLOCK), f32),
            pltpu.VMEM((MATS, 8, BLOCK), f32),
            pltpu.VMEM((MATS, 3, 8, BLOCK), f32),
            pltpu.VMEM((MATS, 3, 8, BLOCK), f32),
            pltpu.VMEM((MATS // 2, R, 2 * R), f32),
            pltpu.VMEM((MATS // 2, 3, R // 2, 2 * R), f32),
            pltpu.VMEM((MATS // 2, 3, 3, R // 2, 2 * R), f32),
            pltpu.VMEM((MATS // 2, R, 2 * R), f32),
            sem((MATS, 3)),
            sem((3, 3)),
            sem((3, 3)),
            sem((4, MATS)),
            sem((4, MATS)),
            sem((4, MATS)),
            sem((4, MATS)),
            sem((3, MATS, 3)),
            sem((3, MATS, 3)),
            sem((3, 3, 3)),
            sem((3, 3, 3)),
        ],
        compiler_params=pltpu.CompilerParams(
            collective_id=0, has_side_effects=True, vmem_limit_bytes=40 * 2**20
        ),
        name="compress_and_sum",
    )(*[pltpu.with_memory_space_constraint(v, pltpu.HBM) for v in (gradients, errors, previous_q)])
    return pl.pallas_call(
        finish_kernel,
        out_shape=(
            jax.ShapeDtypeStruct((1, MATS, ROWS, D), f32),
            jax.ShapeDtypeStruct((MATS, R, D), f32),
        ),
        in_specs=[vmem, vmem, vmem, vmem],
        out_specs=(far_hbm, far_hbm),
        scratch_shapes=[
            pltpu.VMEM((MATS, ROWS, D), f32),
            pltpu.VMEM((MATS, R, D), f32),
            pltpu.VMEM((2, ROWS, D), bf16),
            sem((MATS,)),
            sem((MATS,)),
        ],
        compiler_params=pltpu.CompilerParams(vmem_limit_bytes=24 * 2**20),
        name="new_q_and_errors",
    )(g_sum, p_mat, y_mat, merged)


def solution(mesh):
    in_specs = (P("dp", None, "mp", None), P("dp", None, "mp", None), P())
    out_specs = (P("dp", None, "mp", None), P())
    return jax.shard_map(body, mesh=mesh, in_specs=in_specs, out_specs=out_specs, check_vma=False)
```

```python
import functools

import jax
import jax.numpy as jnp
from jax import lax
from jax.experimental import pallas as pl
from jax.experimental.pallas import tpu as pltpu
from jax.sharding import PartitionSpec as P

MESH = pl.DeviceIdType.MESH
MATS, ROWS, D, R = 6, 192, 1408, 64
HALF = ROWS // 2
BLOCK = 384
COLS = ((0, 512), (512, 512), (1024, 384))
f32, bf16 = jnp.float32, jnp.bfloat16
NT = (((1,), (1,)), ((), ()))


def dot(a, b):
    return jnp.dot(a, b, preferred_element_type=f32)


def dot_nt(a, b):
    return lax.dot_general(a, b, NT, preferred_element_type=f32)


def split(x):
    hi = x.astype(bf16)
    return hi, (x - hi.astype(f32)).astype(bf16)


def eliminate(grams, y_ref):
    row = lax.broadcasted_iota(jnp.int32, (R, 2 * R), 0)
    lane = lax.broadcasted_iota(jnp.int32, (R, 2 * R), 1)
    eye = jnp.where(lane == row + 64, 1.0, 0.0)
    unit = jnp.where(lane == row, 1.0, 0.0)
    for m in range(8):
        if m < MATS:
            gram = grams[m // 2]
            gram = pltpu.roll(gram, 64, axis=1) if m % 2 else gram
        else:
            gram = unit
        y_ref[pl.ds(m, R, stride=8), :] = jnp.where(lane < 64, gram, eye)
    rows = [y_ref[8 * i : 8 * i + 8] for i in range(R)]

    def at(r, k):
        return jnp.broadcast_to(r[:, k : k + 1], (8, 128))

    for k in range(0, R, 4):
        r0, r1, r2, r3 = rows[k : k + 4]
        s00, s01, s02, s03 = (at(r0, k + i) for i in range(4))
        s11, s12, s13 = (at(r1, k + i) for i in range(1, 4))
        s22, s23, s33 = at(r2, k + 2), at(r2, k + 3), at(r3, k + 3)
        i0 = 1.0 / s00
        l10, l20, l30 = s01 * i0, s02 * i0, s03 * i0
        d1 = s11 - l10 * s01
        t12, t13 = s12 - l10 * s02, s13 - l10 * s03
        i1 = 1.0 / d1
        l21, l31 = t12 * i1, t13 * i1
        d2 = s22 - l20 * s02 - l21 * t12
        t23 = s23 - l20 * s03 - l21 * t13
        i2 = 1.0 / d2
        l32 = t23 * i2
        d3 = s33 - l30 * s03 - l31 * t13 - l32 * t23
        i3 = 1.0 / d3
        r1 = r1 - l10 * r0
        r2 = r2 - l20 * r0 - l21 * r1
        r3 = r3 - l30 * r0 - l31 * r1 - l32 * r2
        q0, q1, q2, q3 = r0 * i0, r1 * i1, r2 * i2, r3 * i3
        for i in range(k + 4, R):
            if i < k + 8:
                c0, c1, c2, c3 = (at(rows[i], k + j) for j in range(4))
                c1 = c1 - l10 * c0
                c2 = c2 - l20 * c0 - l21 * c1
                c3 = c3 - l30 * c0 - l31 * c1 - l32 * c2
            else:
                c0, c1, c2, c3 = at(r0, i), at(r1, i), at(r2, i), at(r3, i)
            rows[i] = rows[i] - (c0 * q0 + c1 * q1) - (c2 * q2 + c3 * q3)
        for i, (r, d) in enumerate(((r0, s00), (r1, d1), (r2, d2), (r3, d3))):
            y_ref[8 * (k + i) : 8 * (k + i) + 8] = r * (1.0 / jnp.sqrt(d))
        yield


def comm_kernel(
    g_hbm, e_hbm, q_hbm, g_sum, p_out, y_out, ebuf,
    gbuf, qbuf, mh, ml, qst, p_own, p_recv, p_chip, p_far, g_acc,
    core_recv, recv0, recv1, q_acc, x_acc, recv2, recv3, gram_own, gram_half, gram_recv, gram_out,
    load_sem, p_send, p_arrive, c_send, c_arrive, a_send, a_arrive, b_send, b_arrive,
    gram_send, gram_arrive,
):
    dp, mp = lax.axis_index("dp"), lax.axis_index("mp")
    y_hi, core = lax.div(dp, 2), lax.rem(dp, 2)
    x = lax.rem(mp, 4)
    z = lax.rem(lax.div(mp, 4), 4)
    y = y_hi * 2 + lax.div(mp, 16)

    def device(xx, yy, zz, cc):
        return (lax.div(yy, 2) * 2 + cc, lax.rem(yy, 2) * 16 + zz * 4 + xx)

    def flip(v):
        return v + 1 - 2 * lax.rem(v, 2)

    def side0(v):
        hi = lax.div(v, 2)
        lo = lax.rem(v, 2)
        return hi + lo - 2 * hi * lo

    def side1(v):
        return lax.div(v, 2)

    def over(*links):
        xx, yy, zz = x, y, z
        for link in links:
            if link % 3 == 0:
                xx = flip(x) if link == 0 else 3 - x
            elif link % 3 == 1:
                yy = flip(y) if link == 1 else 3 - y
            else:
                zz = flip(z) if link == 2 else 3 - z
        return device(xx, yy, zz, core)

    near = tuple(over(link) for link in range(6))
    corner = tuple(over(link, (link + 1) % 6) for link in range(6))

    def by_core(values):
        first = core == 0
        return tuple(
            jax.tree.map(lambda a, b: jnp.where(first, a, b), values[i], values[(i + 3) % 6]) for i in range(6)
        )
    sides = (side0(x), side0(y), side0(z), side1(x), side1(y), side1(z))
    twin = device(x, y, z, 1 - core)
    far = device(x, lax.rem(y + 2, 4), z, core)

    def loads(m):
        return (
            pltpu.make_async_copy(q_hbm.at[m], qbuf.at[m], load_sem.at[m, 0]),
            pltpu.make_async_copy(g_hbm.at[0, m], gbuf.at[m], load_sem.at[m, 1]),
            pltpu.make_async_copy(e_hbm.at[0, m], ebuf.at[m], load_sem.at[m, 2]),
        )

    def begin(m, _):
        for copy in loads(m):
            copy.start()
        return 0

    lax.fori_loop(0, MATS, begin, 0)
    barrier = pltpu.get_barrier_semaphore()
    everyone = near + corner + (twin, far)
    for other in everyone:
        pl.semaphore_signal(barrier, inc=1, device_id=other, device_id_type=MESH)

    def remote(src, dst, send, arrive, target):
        copy = pltpu.make_async_remote_copy(
            src_ref=src, dst_ref=dst, send_sem=send, recv_sem=arrive,
            device_id=target, device_id_type=MESH,
        )
        copy.start()
        return copy

    mine = pl.multiple_of(core * HALF, 8)
    theirs = pl.multiple_of((1 - core) * HALF, 8)
    p_own[...] = jnp.zeros_like(p_own)
    qst[...] = jnp.zeros_like(qst)
    q_acc[...] = jnp.zeros_like(q_acc)

    def local_p(m):
        b = lax.rem(m, 2)
        for copy in loads(m):
            copy.wait()

        def merge(i, _):
            rows = pl.ds(pl.multiple_of(i * 32, 32), 32)
            merged = gbuf[m, rows].astype(f32) + ebuf[m, rows]
            ebuf[m, rows] = merged
            hi, lo = split(merged)
            mh[m, rows] = hi
            ml[m, rows] = lo
            return 0

        lax.fori_loop(0, ROWS // 32, merge, 0)
        hi, lo = split(qbuf[m])
        at = pl.multiple_of(64 * b, 64)
        qst[b, pl.ds(at, 64)] = hi
        qst[b, pl.ds(at + 128, 64)] = lo
        wide = dot_nt(mh[m], qst[b])
        p_own[lax.div(m, 2)] += wide[:, :128] + wide[:, 128:] + dot_nt(ml[m], qst[b, :128])

    def p_copy(s, j):
        if s == 0:
            src, dst, target = p_own.at[j, pl.ds(theirs, HALF)], p_recv.at[j], twin
        elif s == 1:
            src, dst, target = p_chip.at[j], p_far.at[j], far
        else:
            src = dst = p_out.at[j, pl.ds(mine, HALF)]
            target = twin
        return pltpu.make_async_remote_copy(
            src_ref=src, dst_ref=dst, send_sem=p_send.at[s, j], recv_sem=p_arrive.at[s, j],
            device_id=target, device_id_type=MESH,
        )

    def p_step(s, j):
        if s > 0:
            p_copy(s - 1, j).wait()
        if s == 1:
            p_chip[j] = p_own[j, pl.ds(mine, HALF)] + p_recv[j]
        if s == 2:
            p_out[j, pl.ds(mine, HALF)] = (p_chip[j] + p_far[j]) * 0.25
        if s < 3:
            p_copy(s, j).start()

    def p_loop(m, _):
        local_p(m)

        @pl.when(m == 1)
        def _():
            pl.semaphore_wait(barrier, len(everyone))
            p_step(0, 0)

        @pl.when(m == 3)
        def _():
            p_step(0, 1)
            p_step(1, 0)

        @pl.when(m == 5)
        def _():
            p_step(0, 2)
            p_step(1, 1)
            p_step(2, 0)

        return 0

    near_of, corner_of, side_of = by_core(near), by_core(corner), by_core(sides)

    def three(src, dst, send, arrive, link):
        targets = (near_of[(link + 1) % 6], near_of[link], corner_of[link])
        return [remote(src(f), dst(f), send.at[f], arrive.at[f], targets[f]) for f in range(3)]

    halves = {}

    def local_g(m):
        j, b = divmod(m, 2)
        if j not in halves:
            halves[j] = split(p_out[j].T)
        hi, lo = halves[j]
        top = hi[64 * b : 64 * b + 64]
        both = jnp.concatenate([top, lo[64 * b : 64 * b + 64]], axis=0)
        for start, size in COLS:
            cols = slice(start, start + size)
            wide = dot(both, mh[m, :, cols])
            g_acc[m, :, cols] = wide[:64] + wide[64:] + dot(top, ml[m, :, cols])

    def gram_chain():
        lane = lax.broadcasted_iota(jnp.int32, (R, 2 * R), 1)
        for j in range(3):
            hi, lo = halves[j]
            square = dot_nt(hi, hi) + (dot_nt(hi, lo) + dot_nt(lo, hi))
            gram_own[j] = jnp.where(lane < 64, square[:64], square[64:])
        rows = pl.ds(pl.multiple_of(core * 32, 32), 32)
        gram_half[0] = gram_own[:, rows]
        for s, link in enumerate((2, 5)):
            copies = three(
                lambda f: gram_half.at[s], lambda f: gram_recv.at[s, f], gram_send.at[s], gram_arrive.at[s], link,
            )
            yield
            for copy in copies:
                copy.wait()
            gram_half[s + 1] = (gram_half[s] + gram_recv[s, 1]) + (gram_recv[s, 0] + gram_recv[s, 2])
        copy = remote(gram_half.at[2], gram_recv.at[2, 0], gram_send.at[2, 0], gram_arrive.at[2, 0], near[1])
        yield
        copy.wait()
        gram_out[:, rows] = gram_half[2] + gram_recv[2, 0]
        part = gram_out.at[:, rows]
        copy = remote(part, part, gram_send.at[2, 1], gram_arrive.at[2, 1], twin)
        yield
        copy.wait()

    def g_chain(j):
        two = pl.ds(2 * j, 2)
        link = [(2 * j + s) % 6 for s in range(6)]
        keep = pl.multiple_of(core * 32, 32)
        give = pl.multiple_of((1 - core) * 32, 32)
        kept0 = pl.multiple_of(core * 32 + 16 * side_of[link[0]], 16)
        gone0 = pl.multiple_of(core * 32 + 16 - 16 * side_of[link[0]], 16)
        kept1 = pl.multiple_of(kept0 + 8 * side_of[link[1]], 8)
        gone1 = pl.multiple_of(kept0 + 8 - 8 * side_of[link[1]], 8)
        hi, lo = side_of[link[2]], side_of[link[3]]

        def block(h, l):
            return pl.ds(pl.multiple_of((2 * h + l) * BLOCK, 128), BLOCK)

        own = block(hi, lo)
        others = (block(hi, 1 - lo), block(1 - hi, lo), block(1 - hi, 1 - lo))

        def send(s, src, dst, i):
            return remote(src, dst, a_send.at[s, j], a_arrive.at[s, j], near_of[link[i]])

        def forward(i, row, size):
            part = g_sum.at[two, pl.ds(row, size), pl.ds(0, D)]
            return remote(part, part, c_send.at[i, j], c_arrive.at[i, j], twin)

        copy = remote(g_acc.at[two, pl.ds(give, 32)], core_recv.at[two], c_send.at[0, j], c_arrive.at[0, j], twin)
        yield
        copy.wait()
        g_acc[two, pl.ds(keep, 32)] += core_recv[two]
        copy = send(0, g_acc.at[two, pl.ds(gone0, 16)], recv0.at[two], 0)
        yield
        copy.wait()
        g_acc[two, pl.ds(kept0, 16)] += recv0[two]
        copy = send(1, g_acc.at[two, pl.ds(gone1, 8)], recv1.at[two], 1)
        yield
        copy.wait()
        q_acc[two, :, :D] = g_acc[two, pl.ds(kept1, 8)] + recv1[two]
        copies = three(
            lambda f: q_acc.at[two, :, others[f]], lambda f: recv2.at[f, two], b_send.at[0, j], b_arrive.at[0, j], link[2],
        )
        yield
        for copy in copies:
            copy.wait()
        x_acc[two] = (q_acc[two, :, own] + recv2[1, two]) + (recv2[0, two] + recv2[2, two])
        copies = three(
            lambda f: x_acc.at[two], lambda f: recv3.at[f, two], b_send.at[1, j], b_arrive.at[1, j], link[4],
        )
        yield
        for copy in copies:
            copy.wait()
        g_sum[two, pl.ds(kept1, 8), own] = (x_acc[two] + recv3[1, two]) + (recv3[0, two] + recv3[2, two])
        part = g_sum.at[two, pl.ds(kept1, 8), own]
        copies = three(lambda f: part, lambda f: part, b_send.at[2, j], b_arrive.at[2, j], link[2])
        yield
        for copy in copies:
            copy.wait()
        part = g_sum.at[two, pl.ds(kept1, 8), pl.ds(0, D)]
        copy = send(2, part, part, 1)
        passed = [forward(1, kept1, 8)]
        yield
        copy.wait()
        part = g_sum.at[two, pl.ds(kept0, 16), pl.ds(0, D)]
        copy = send(3, part, part, 0)
        passed.append(forward(2, gone1, 8))
        yield
        copy.wait()
        passed.append(forward(3, gone0, 16))
        yield
        for copy in passed:
            copy.wait()

    gram = gram_chain()
    ac = [g_chain(j) for j in range(3)]
    factor = None

    def behind(blocks):
        nonlocal factor
        if factor is None and next(gram, 1):
            factor = eliminate([gram_out[j] for j in range(3)], y_out)
        if factor is not None:
            for _ in range(blocks):
                next(factor, None)

    lax.fori_loop(0, MATS, p_loop, 0)
    p_step(1, 2)
    p_step(3, 0)
    local_g(0)
    p_step(2, 1)
    local_g(1)
    next(ac[0])
    p_step(2, 2)
    p_step(3, 1)
    local_g(2)
    local_g(3)
    next(ac[1])
    next(ac[0])
    p_step(3, 2)
    halves[2] = split(p_out[2].T)
    next(gram)
    local_g(4)
    local_g(5)
    next(ac[2])
    next(ac[1])
    behind(0)
    next(ac[0])
    next(ac[2])
    for s in range(8):
        for j in range(3):
            next(ac[j], None)
            if factor is not None or j != 1:
                behind(2)
    for _ in factor:
        pass


def finish_kernel(
    g_sum, p_ref, y_ref, m_ref, err_hbm, q_out, mbuf, new_q, wst, store_sem, q_sem,
):
    lane = lax.broadcasted_iota(jnp.int32, (R, 2 * R), 1)
    wide_lane = lax.broadcasted_iota(jnp.int32, (ROWS, 2 * R), 1)
    stores = []
    for m in range(MATS):
        b = m % 2
        side = jnp.where(lane >= 64, y_ref[pl.ds(m, R, stride=8), :], 0.0)
        other = pltpu.roll(side, 64, axis=1)
        inverse = side if b else other
        bh, bl = split(jnp.concatenate([inverse, inverse], axis=0))
        ph, pl_ = split(p_ref[m // 2])
        ortho = dot_nt(ph, bh) + (dot_nt(ph, bl) + dot_nt(pl_, bh))
        oh, ol = split(ortho)
        lhs = jnp.concatenate([jnp.where(wide_lane < 64, oh, ol), oh[:, :64]], axis=1)
        lh, ll = split(side + other)
        lhs_q = jnp.concatenate([jnp.where(lane < 64, lh, ll), lh[:, :64]], axis=1)
        gh, gl = split(g_sum[m, :, :D] * 0.25)
        wst[0, 0:64] = gh
        wst[0, 64:128] = gh
        wst[0, 128:192] = gl
        fresh = dot(lhs_q, wst[0])
        new_q[m] = fresh
        store = pltpu.make_async_copy(new_q.at[m], q_out.at[m], q_sem.at[m])
        store.start()
        stores.append(store)
        nh, nl = split(fresh)
        wst[1, 0:64] = nh
        wst[1, 64:128] = nh
        wst[1, 128:192] = nl
        for start, size in COLS:
            cols = slice(start, start + size)
            mbuf[m, :, cols] = m_ref[m, :, cols] - dot(lhs, wst[1, :, cols])
        store = pltpu.make_async_copy(mbuf.at[m], err_hbm.at[0, m], store_sem.at[m])
        store.start()
        stores.append(store)
    for store in stores:
        store.wait()


def body(gradients, errors, previous_q):
    vmem = pl.BlockSpec(memory_space=pltpu.VMEM)
    far_hbm = pl.BlockSpec(memory_space=pltpu.HBM)
    sem = pltpu.SemaphoreType.DMA
    g_sum, p_mat, y_mat, merged = pl.pallas_call(
        comm_kernel,
        out_shape=(
            jax.ShapeDtypeStruct((MATS, R, 4 * BLOCK), f32),
            jax.ShapeDtypeStruct((MATS // 2, ROWS, 2 * R), f32),
            jax.ShapeDtypeStruct((8 * R, 2 * R), f32),
            jax.ShapeDtypeStruct((MATS, ROWS, D), f32),
        ),
        in_specs=[far_hbm, far_hbm, far_hbm],
        out_specs=(vmem, vmem, vmem, vmem),
        scratch_shapes=[
            pltpu.VMEM((MATS, ROWS, D), bf16),
            pltpu.VMEM((MATS, R, D), f32),
            pltpu.VMEM((MATS, ROWS, D), bf16),
            pltpu.VMEM((MATS, ROWS, D), bf16),
            pltpu.VMEM((2, 256, D), bf16),
            pltpu.VMEM((MATS // 2, ROWS, 128), f32),
            pltpu.VMEM((MATS // 2, HALF, 128), f32),
            pltpu.VMEM((MATS // 2, HALF, 128), f32),
            pltpu.VMEM((MATS // 2, HALF, 128), f32),
            pltpu.VMEM((MATS, R, D), f32),
            pltpu.VMEM((MATS, 32, D), f32),
            pltpu.VMEM((MATS, 16, D), f32),
            pltpu.VMEM((MATS, 8, D), f32),
            pltpu.VMEM((MATS, 8, 4 * BLOCK), f32),
            pltpu.VMEM((MATS, 8, BLOCK), f32),
            pltpu.VMEM((3, MATS, 8, BLOCK), f32),
            pltpu.VMEM((3, MATS, 8, BLOCK), f32),
            pltpu.VMEM((MATS // 2, R, 2 * R), f32),
            pltpu.VMEM((3, MATS // 2, R // 2, 2 * R), f32),
            pltpu.VMEM((3, 3, MATS // 2, R // 2, 2 * R), f32),
            pltpu.VMEM((MATS // 2, R, 2 * R), f32),
            sem((MATS, 3)),
            sem((3, 3)),
            sem((3, 3)),
            sem((4, 3)),
            sem((4, 3)),
            sem((4, 3)),
            sem((4, 3)),
            sem((3, 3, 3)),
            sem((3, 3, 3)),
            sem((3, 3)),
            sem((3, 3)),
        ],
        compiler_params=pltpu.CompilerParams(
            collective_id=0, has_side_effects=True, vmem_limit_bytes=40 * 2**20
        ),
        name="compress_and_sum",
    )(*[pltpu.with_memory_space_constraint(v, pltpu.HBM) for v in (gradients, errors, previous_q)])
    return pl.pallas_call(
        finish_kernel,
        out_shape=(
            jax.ShapeDtypeStruct((1, MATS, ROWS, D), f32),
            jax.ShapeDtypeStruct((MATS, R, D), f32),
        ),
        in_specs=[vmem, vmem, vmem, vmem],
        out_specs=(far_hbm, far_hbm),
        scratch_shapes=[
            pltpu.VMEM((MATS, ROWS, D), f32),
            pltpu.VMEM((MATS, R, D), f32),
            pltpu.VMEM((2, ROWS, D), bf16),
            sem((MATS,)),
            sem((MATS,)),
        ],
        compiler_params=pltpu.CompilerParams(vmem_limit_bytes=24 * 2**20),
        name="new_q_and_errors",
    )(g_sum, p_mat, y_mat, merged)


def solution(mesh):
    in_specs = (P("dp", None, "mp", None), P("dp", None, "mp", None), P())
    out_specs = (P("dp", None, "mp", None), P())
    return jax.shard_map(body, mesh=mesh, in_specs=in_specs, out_specs=out_specs, check_vma=False)
```

```python
import functools

import jax
import jax.numpy as jnp
from jax import lax
from jax.experimental import pallas as pl
from jax.experimental.pallas import tpu as pltpu
from jax.sharding import PartitionSpec as P

MESH = pl.DeviceIdType.MESH
MATS, ROWS, D, R = 6, 192, 1408, 64
HALF = ROWS // 2
BLOCK = 384
COLS = ((0, 512), (512, 512), (1024, 384))
f32, bf16 = jnp.float32, jnp.bfloat16
NT = (((1,), (1,)), ((), ()))


def dot(a, b):
    return jnp.dot(a, b, preferred_element_type=f32)


def dot_nt(a, b):
    return lax.dot_general(a, b, NT, preferred_element_type=f32)


def split(x):
    hi = x.astype(bf16)
    return hi, (x - hi.astype(f32)).astype(bf16)


def eliminate(grams, y_ref):
    row = lax.broadcasted_iota(jnp.int32, (R, 2 * R), 0)
    lane = lax.broadcasted_iota(jnp.int32, (R, 2 * R), 1)
    eye = jnp.where(lane == row + 64, 1.0, 0.0)
    unit = jnp.where(lane == row, 1.0, 0.0)
    for m in range(8):
        if m < MATS:
            gram = grams[m // 2]
            gram = pltpu.roll(gram, 64, axis=1) if m % 2 else gram
        else:
            gram = unit
        y_ref[pl.ds(m, R, stride=8), :] = jnp.where(lane < 64, gram, eye)
    rows = [y_ref[8 * i : 8 * i + 8] for i in range(R)]

    def at(r, k):
        return jnp.broadcast_to(r[:, k : k + 1], (8, 128))

    for k in range(0, R, 4):
        r0, r1, r2, r3 = rows[k : k + 4]
        s00, s01, s02, s03 = (at(r0, k + i) for i in range(4))
        s11, s12, s13 = (at(r1, k + i) for i in range(1, 4))
        s22, s23, s33 = at(r2, k + 2), at(r2, k + 3), at(r3, k + 3)
        i0 = 1.0 / s00
        l10, l20, l30 = s01 * i0, s02 * i0, s03 * i0
        d1 = s11 - l10 * s01
        t12, t13 = s12 - l10 * s02, s13 - l10 * s03
        i1 = 1.0 / d1
        l21, l31 = t12 * i1, t13 * i1
        d2 = s22 - l20 * s02 - l21 * t12
        t23 = s23 - l20 * s03 - l21 * t13
        i2 = 1.0 / d2
        l32 = t23 * i2
        d3 = s33 - l30 * s03 - l31 * t13 - l32 * t23
        i3 = 1.0 / d3
        r1 = r1 - l10 * r0
        r2 = r2 - l20 * r0 - l21 * r1
        r3 = r3 - l30 * r0 - l31 * r1 - l32 * r2
        q0, q1, q2, q3 = r0 * i0, r1 * i1, r2 * i2, r3 * i3
        for i in range(k + 4, R):
            if i < k + 8:
                c0, c1, c2, c3 = (at(rows[i], k + j) for j in range(4))
                c1 = c1 - l10 * c0
                c2 = c2 - l20 * c0 - l21 * c1
                c3 = c3 - l30 * c0 - l31 * c1 - l32 * c2
            else:
                c0, c1, c2, c3 = at(r0, i), at(r1, i), at(r2, i), at(r3, i)
            rows[i] = rows[i] - (c0 * q0 + c1 * q1) - (c2 * q2 + c3 * q3)
        for i, (r, d) in enumerate(((r0, s00), (r1, d1), (r2, d2), (r3, d3))):
            y_ref[8 * (k + i) : 8 * (k + i) + 8] = r * (1.0 / jnp.sqrt(d))
        yield


def product_kernel(g_hbm, e_hbm, q_hbm, ebuf, mh, ml, p_own, gbuf, qbuf, qst, load_sem):
    def loads(m):
        return (
            pltpu.make_async_copy(q_hbm.at[m], qbuf.at[m], load_sem.at[m, 0]),
            pltpu.make_async_copy(g_hbm.at[0, m], gbuf.at[m], load_sem.at[m, 1]),
            pltpu.make_async_copy(e_hbm.at[0, m], ebuf.at[m], load_sem.at[m, 2]),
        )

    def begin(m, _):
        for copy in loads(m):
            copy.start()
        return 0

    lax.fori_loop(0, MATS, begin, 0)
    p_own[...] = jnp.zeros_like(p_own)
    qst[...] = jnp.zeros_like(qst)

    def local_p(m):
        b = lax.rem(m, 2)
        for copy in loads(m):
            copy.wait()

        def merge(i, _):
            rows = pl.ds(pl.multiple_of(i * 32, 32), 32)
            merged = gbuf[m, rows].astype(f32) + ebuf[m, rows]
            ebuf[m, rows] = merged
            hi, lo = split(merged)
            mh[m, rows] = hi
            ml[m, rows] = lo
            return 0

        lax.fori_loop(0, ROWS // 32, merge, 0)
        hi, lo = split(qbuf[m])
        at = pl.multiple_of(64 * b, 64)
        qst[b, pl.ds(at, 64)] = hi
        qst[b, pl.ds(at + 128, 64)] = lo
        wide = dot_nt(mh[m], qst[b])
        p_own[lax.div(m, 2)] += wide[:, :128] + wide[:, 128:] + dot_nt(ml[m], qst[b, :128])

    def p_loop(m, _):
        local_p(m)
        return 0

    lax.fori_loop(0, MATS, p_loop, 0)


def comm_kernel(
    mh, ml, p_own, g_sum, p_out, y_out,
    p_recv, p_chip, p_far, g_acc,
    core_recv, recv0, recv1, q_acc, x_acc, recv2, recv3, gram_own, gram_half, gram_recv, gram_out,
    p_send, p_arrive, c_send, c_arrive, a_send, a_arrive, b_send, b_arrive,
    gram_send, gram_arrive,
):
    dp, mp = lax.axis_index("dp"), lax.axis_index("mp")
    y_hi, core = lax.div(dp, 2), lax.rem(dp, 2)
    x = lax.rem(mp, 4)
    z = lax.rem(lax.div(mp, 4), 4)
    y = y_hi * 2 + lax.div(mp, 16)

    def device(xx, yy, zz, cc):
        return (lax.div(yy, 2) * 2 + cc, lax.rem(yy, 2) * 16 + zz * 4 + xx)

    def flip(v):
        return v + 1 - 2 * lax.rem(v, 2)

    def side0(v):
        hi = lax.div(v, 2)
        lo = lax.rem(v, 2)
        return hi + lo - 2 * hi * lo

    def side1(v):
        return lax.div(v, 2)

    def over(*links):
        xx, yy, zz = x, y, z
        for link in links:
            if link % 3 == 0:
                xx = flip(x) if link == 0 else 3 - x
            elif link % 3 == 1:
                yy = flip(y) if link == 1 else 3 - y
            else:
                zz = flip(z) if link == 2 else 3 - z
        return device(xx, yy, zz, core)

    near = tuple(over(link) for link in range(6))
    corner = tuple(over(link, (link + 1) % 6) for link in range(6))
    sides = (side0(x), side0(y), side0(z), side1(x), side1(y), side1(z))
    twin = device(x, y, z, 1 - core)
    far = device(x, lax.rem(y + 2, 4), z, core)

    barrier = pltpu.get_barrier_semaphore()
    everyone = near + corner + (twin, far)
    for other in everyone:
        pl.semaphore_signal(barrier, inc=1, device_id=other, device_id_type=MESH)

    def remote(src, dst, send, arrive, target):
        copy = pltpu.make_async_remote_copy(
            src_ref=src, dst_ref=dst, send_sem=send, recv_sem=arrive,
            device_id=target, device_id_type=MESH,
        )
        copy.start()
        return copy

    mine = pl.multiple_of(core * HALF, 8)
    theirs = pl.multiple_of((1 - core) * HALF, 8)
    q_acc[...] = jnp.zeros_like(q_acc)

    def p_copy(s, j):
        if s == 0:
            src, dst, target = p_own.at[j, pl.ds(theirs, HALF)], p_recv.at[j], twin
        elif s == 1:
            src, dst, target = p_chip.at[j], p_far.at[j], far
        else:
            src = dst = p_out.at[j, pl.ds(mine, HALF)]
            target = twin
        return pltpu.make_async_remote_copy(
            src_ref=src, dst_ref=dst, send_sem=p_send.at[s, j], recv_sem=p_arrive.at[s, j],
            device_id=target, device_id_type=MESH,
        )

    def p_step(s, j):
        if s > 0:
            p_copy(s - 1, j).wait()
        if s == 1:
            p_chip[j] = p_own[j, pl.ds(mine, HALF)] + p_recv[j]
        if s == 2:
            p_out[j, pl.ds(mine, HALF)] = (p_chip[j] + p_far[j]) * 0.25
        if s < 3:
            p_copy(s, j).start()

    halves = {}

    def three(src, dst, send, arrive, link):
        targets = (near[(link + 1) % 6], near[link], corner[link])
        return [remote(src(f), dst.at[f], send.at[f], arrive.at[f], targets[f]) for f in range(3)]

    def gram_chain(j):
        halves[j] = hi, lo = split(p_out[j].T)
        square = dot_nt(hi, hi) + (dot_nt(hi, lo) + dot_nt(lo, hi))
        lane = lax.broadcasted_iota(jnp.int32, (R, 2 * R), 1)
        gram_own[j] = jnp.where(lane < 64, square[:64], square[64:])
        rows = pl.ds(pl.multiple_of(core * 32, 32), 32)
        gram_half[j, 0] = gram_own[j, rows]
        for s, link in enumerate((2, 5) if j % 2 == 0 else (5, 2)):
            copies = three(
                lambda f: gram_half.at[j, s], gram_recv.at[j, s], gram_send.at[j, s], gram_arrive.at[j, s], link,
            )
            yield
            for copy in copies:
                copy.wait()
            got = gram_recv.at[j, s]
            gram_half[j, s + 1] = (gram_half[j, s] + got[1]) + (got[0] + got[2])
        copy = remote(
            gram_half.at[j, 2], gram_recv.at[j, 2, 0], gram_send.at[j, 2, 0], gram_arrive.at[j, 2, 0], near[1],
        )
        yield
        copy.wait()
        gram_out[j, rows] = gram_half[j, 2] + gram_recv[j, 2, 0]
        part = gram_out.at[j, rows]
        copy = remote(part, part, gram_send.at[j, 2, 1], gram_arrive.at[j, 2, 1], twin)
        yield
        copy.wait()

    def local_g(m):
        j, b = divmod(m, 2)
        hi, lo = halves[j]
        top = hi[64 * b : 64 * b + 64]
        both = jnp.concatenate([top, lo[64 * b : 64 * b + 64]], axis=0)
        for start, size in COLS:
            cols = slice(start, start + size)
            wide = dot(both, mh[m, :, cols])
            g_acc[m, :, cols] = wide[:64] + wide[64:] + dot(top, ml[m, :, cols])

    def g_chain(m):
        link = [(m + s) % 6 for s in range(6)]
        keep = pl.multiple_of(core * 32, 32)
        give = pl.multiple_of((1 - core) * 32, 32)
        kept0 = pl.multiple_of(core * 32 + 16 * sides[link[0]], 16)
        gone0 = pl.multiple_of(core * 32 + 16 - 16 * sides[link[0]], 16)
        kept1 = pl.multiple_of(kept0 + 8 * sides[link[1]], 8)
        gone1 = pl.multiple_of(kept0 + 8 - 8 * sides[link[1]], 8)
        hi, lo = sides[link[2]], sides[link[3]]

        def block(h, l):
            return pl.ds(pl.multiple_of((2 * h + l) * BLOCK, 128), BLOCK)

        own = block(hi, lo)
        others = (block(hi, 1 - lo), block(1 - hi, lo), block(1 - hi, 1 - lo))

        def send(s, src, dst, i):
            return remote(src, dst, a_send.at[s, m], a_arrive.at[s, m], near[link[i]])

        def forward(i, row, size):
            part = g_sum.at[m, pl.ds(row, size), pl.ds(0, D)]
            return remote(part, part, c_send.at[i, m], c_arrive.at[i, m], twin)

        copy = remote(g_acc.at[m, pl.ds(give, 32)], core_recv.at[m], c_send.at[0, m], c_arrive.at[0, m], twin)
        yield
        copy.wait()
        g_acc[m, pl.ds(keep, 32)] += core_recv[m]
        copy = send(0, g_acc.at[m, pl.ds(gone0, 16)], recv0.at[m], 0)
        yield
        copy.wait()
        g_acc[m, pl.ds(kept0, 16)] += recv0[m]
        copy = send(1, g_acc.at[m, pl.ds(gone1, 8)], recv1.at[m], 1)
        yield
        copy.wait()
        q_acc[m, :, :D] = g_acc[m, pl.ds(kept1, 8)] + recv1[m]
        copies = three(lambda f: q_acc.at[m, :, others[f]], recv2.at[m], b_send.at[0, m], b_arrive.at[0, m], link[2])
        yield
        for copy in copies:
            copy.wait()
        x_acc[m] = (q_acc[m, :, own] + recv2[m, 1]) + (recv2[m, 0] + recv2[m, 2])
        copies = three(lambda f: x_acc.at[m], recv3.at[m], b_send.at[1, m], b_arrive.at[1, m], link[4])
        yield
        for copy in copies:
            copy.wait()
        g_sum[m, pl.ds(kept1, 8), own] = (x_acc[m] + recv3[m, 1]) + (recv3[m, 0] + recv3[m, 2])
        part = g_sum.at[m, pl.ds(kept1, 8), own]
        targets = (near[link[3]], near[link[2]], corner[link[2]])
        copies = [remote(part, part, b_send.at[2, m, f], b_arrive.at[2, m, f], targets[f]) for f in range(3)]
        yield
        for copy in copies:
            copy.wait()
        part = g_sum.at[m, pl.ds(kept1, 8), pl.ds(0, D)]
        copy = send(2, part, part, 1)
        passed = [forward(1, kept1, 8)]
        yield
        copy.wait()
        part = g_sum.at[m, pl.ds(kept0, 16), pl.ds(0, D)]
        copy = send(3, part, part, 0)
        passed.append(forward(2, gone1, 8))
        yield
        copy.wait()
        passed.append(forward(3, gone0, 16))
        yield
        for copy in passed:
            copy.wait()

    gc = [gram_chain(j) for j in range(3)]
    ac = [g_chain(m) for m in range(MATS)]
    factor = None

    def behind():
        nonlocal factor
        if factor is None:
            if all([next(chain, 1) for chain in gc]):
                factor = eliminate([gram_out[j] for j in range(3)], y_out)
        if factor is not None:
            next(factor, None)

    pl.semaphore_wait(barrier, len(everyone))
    for i in range(3):
        for j in range(3):
            p_step(i, j)
    p_step(3, 0)
    next(gc[0])
    local_g(0)
    next(ac[0])
    local_g(1)
    next(ac[1])
    p_step(3, 1)
    next(gc[1])
    next(gc[0])
    local_g(2)
    next(ac[2])
    next(ac[0])
    local_g(3)
    next(ac[3])
    next(ac[1])
    p_step(3, 2)
    next(gc[2])
    next(gc[1])
    next(gc[0])
    local_g(4)
    next(ac[4])
    next(ac[2])
    local_g(5)
    next(ac[5])
    next(ac[3])
    next(gc[2])
    next(gc[1])
    next(gc[0])
    next(ac[4])
    next(ac[5])
    for s in range(8):
        for m in range(MATS):
            next(ac[m], None)
            if factor is not None or m in (2, 5):
                behind()
    for _ in factor:
        pass


def finish_kernel(
    g_sum, p_ref, y_ref, m_ref, err_hbm, q_out, mbuf, new_q, wst, store_sem, q_sem,
):
    lane = lax.broadcasted_iota(jnp.int32, (R, 2 * R), 1)
    wide_lane = lax.broadcasted_iota(jnp.int32, (ROWS, 2 * R), 1)
    stores = []
    for m in range(MATS):
        b = m % 2
        side = jnp.where(lane >= 64, y_ref[pl.ds(m, R, stride=8), :], 0.0)
        other = pltpu.roll(side, 64, axis=1)
        inverse = side if b else other
        bh, bl = split(jnp.concatenate([inverse, inverse], axis=0))
        ph, pl_ = split(p_ref[m // 2])
        ortho = dot_nt(ph, bh) + (dot_nt(ph, bl) + dot_nt(pl_, bh))
        oh, ol = split(ortho)
        lhs = jnp.concatenate([jnp.where(wide_lane < 64, oh, ol), oh[:, :64]], axis=1)
        lh, ll = split(side + other)
        lhs_q = jnp.concatenate([jnp.where(lane < 64, lh, ll), lh[:, :64]], axis=1)
        gh, gl = split(g_sum[m, :, :D] * 0.25)
        wst[0, 0:64] = gh
        wst[0, 64:128] = gh
        wst[0, 128:192] = gl
        fresh = dot(lhs_q, wst[0])
        new_q[m] = fresh
        store = pltpu.make_async_copy(new_q.at[m], q_out.at[m], q_sem.at[m])
        store.start()
        stores.append(store)
        nh, nl = split(fresh)
        wst[1, 0:64] = nh
        wst[1, 64:128] = nh
        wst[1, 128:192] = nl
        for start, size in COLS:
            cols = slice(start, start + size)
            mbuf[m, :, cols] = m_ref[m, :, cols] - dot(lhs, wst[1, :, cols])
        store = pltpu.make_async_copy(mbuf.at[m], err_hbm.at[0, m], store_sem.at[m])
        store.start()
        stores.append(store)
    for store in stores:
        store.wait()


def body(gradients, errors, previous_q):
    vmem = pl.BlockSpec(memory_space=pltpu.VMEM)
    far_hbm = pl.BlockSpec(memory_space=pltpu.HBM)
    sem = pltpu.SemaphoreType.DMA
    from_hbm = [pltpu.with_memory_space_constraint(v, pltpu.HBM) for v in (gradients, errors, previous_q)]
    merged, high, low, p_own = pl.pallas_call(
        product_kernel,
        out_shape=(
            jax.ShapeDtypeStruct((MATS, ROWS, D), f32),
            jax.ShapeDtypeStruct((MATS, ROWS, D), bf16),
            jax.ShapeDtypeStruct((MATS, ROWS, D), bf16),
            jax.ShapeDtypeStruct((MATS // 2, ROWS, 128), f32),
        ),
        in_specs=[far_hbm] * 3,
        out_specs=(vmem,) * 4,
        scratch_shapes=[
            pltpu.VMEM((MATS, ROWS, D), bf16),
            pltpu.VMEM((MATS, R, D), f32),
            pltpu.VMEM((2, 256, D), bf16),
            sem((MATS, 3)),
        ],
        compiler_params=pltpu.CompilerParams(vmem_limit_bytes=30 * 2**20),
        name="merge_and_product",
    )(*from_hbm)
    g_sum, p_mat, y_mat = pl.pallas_call(
        comm_kernel,
        out_shape=(
            jax.ShapeDtypeStruct((MATS, R, 4 * BLOCK), f32),
            jax.ShapeDtypeStruct((MATS // 2, ROWS, 2 * R), f32),
            jax.ShapeDtypeStruct((8 * R, 2 * R), f32),
        ),
        in_specs=[vmem] * 3,
        out_specs=(vmem,) * 3,
        scratch_shapes=[
            pltpu.VMEM((MATS // 2, HALF, 128), f32),
            pltpu.VMEM((MATS // 2, HALF, 128), f32),
            pltpu.VMEM((MATS // 2, HALF, 128), f32),
            pltpu.VMEM((MATS, R, D), f32),
            pltpu.VMEM((MATS, 32, D), f32),
            pltpu.VMEM((MATS, 16, D), f32),
            pltpu.VMEM((MATS, 8, D), f32),
            pltpu.VMEM((MATS, 8, 4 * BLOCK), f32),
            pltpu.VMEM((MATS, 8, BLOCK), f32),
            pltpu.VMEM((MATS, 3, 8, BLOCK), f32),
            pltpu.VMEM((MATS, 3, 8, BLOCK), f32),
            pltpu.VMEM((MATS // 2, R, 2 * R), f32),
            pltpu.VMEM((MATS // 2, 3, R // 2, 2 * R), f32),
            pltpu.VMEM((MATS // 2, 3, 3, R // 2, 2 * R), f32),
            pltpu.VMEM((MATS // 2, R, 2 * R), f32),
            sem((3, 3)),
            sem((3, 3)),
            sem((4, MATS)),
            sem((4, MATS)),
            sem((4, MATS)),
            sem((4, MATS)),
            sem((3, MATS, 3)),
            sem((3, MATS, 3)),
            sem((3, 3, 3)),
            sem((3, 3, 3)),
        ],
        compiler_params=pltpu.CompilerParams(
            collective_id=0, has_side_effects=True, vmem_limit_bytes=30 * 2**20
        ),
        name="exchange_and_sum",
    )(high, low, p_own)
    return pl.pallas_call(
        finish_kernel,
        out_shape=(
            jax.ShapeDtypeStruct((1, MATS, ROWS, D), f32),
            jax.ShapeDtypeStruct((MATS, R, D), f32),
        ),
        in_specs=[vmem, vmem, vmem, vmem],
        out_specs=(far_hbm, far_hbm),
        scratch_shapes=[
            pltpu.VMEM((MATS, ROWS, D), f32),
            pltpu.VMEM((MATS, R, D), f32),
            pltpu.VMEM((2, ROWS, D), bf16),
            sem((MATS,)),
            sem((MATS,)),
        ],
        compiler_params=pltpu.CompilerParams(vmem_limit_bytes=24 * 2**20),
        name="new_q_and_errors",
    )(g_sum, p_mat, y_mat, merged)


def solution(mesh):
    in_specs = (P("dp", None, "mp", None), P("dp", None, "mp", None), P())
    out_specs = (P("dp", None, "mp", None), P())
    return jax.shard_map(body, mesh=mesh, in_specs=in_specs, out_specs=out_specs, check_vma=False)
```

```python
import functools

import jax
import jax.numpy as jnp
from jax import lax
from jax.experimental import pallas as pl
from jax.experimental.pallas import tpu as pltpu
from jax.sharding import PartitionSpec as P

MESH = pl.DeviceIdType.MESH
MATS, ROWS, D, R = 6, 192, 1408, 64
HALF = ROWS // 2
BLOCK = 384
COLS = ((0, 512), (512, 512), (1024, 384))
f32, bf16 = jnp.float32, jnp.bfloat16
NT = (((1,), (1,)), ((), ()))


def dot(a, b):
    return jnp.dot(a, b, preferred_element_type=f32)


def dot_nt(a, b):
    return lax.dot_general(a, b, NT, preferred_element_type=f32)


def split(x):
    hi = x.astype(bf16)
    return hi, (x - hi.astype(f32)).astype(bf16)


def eliminate(grams, y_ref):
    row = lax.broadcasted_iota(jnp.int32, (R, 2 * R), 0)
    lane = lax.broadcasted_iota(jnp.int32, (R, 2 * R), 1)
    eye = jnp.where(lane == row + 64, 1.0, 0.0)
    unit = jnp.where(lane == row, 1.0, 0.0)
    for m in range(8):
        if m < MATS:
            gram = grams[m // 2]
            gram = pltpu.roll(gram, 64, axis=1) if m % 2 else gram
        else:
            gram = unit
        y_ref[pl.ds(m, R, stride=8), :] = jnp.where(lane < 64, gram, eye)
    rows = [y_ref[8 * i : 8 * i + 8] for i in range(R)]

    def at(r, k):
        return jnp.broadcast_to(r[:, k : k + 1], (8, 128))

    for k in range(0, R, 4):
        r0, r1, r2, r3 = rows[k : k + 4]
        s00, s01, s02, s03 = (at(r0, k + i) for i in range(4))
        s11, s12, s13 = (at(r1, k + i) for i in range(1, 4))
        s22, s23, s33 = at(r2, k + 2), at(r2, k + 3), at(r3, k + 3)
        i0 = 1.0 / s00
        l10, l20, l30 = s01 * i0, s02 * i0, s03 * i0
        d1 = s11 - l10 * s01
        t12, t13 = s12 - l10 * s02, s13 - l10 * s03
        i1 = 1.0 / d1
        l21, l31 = t12 * i1, t13 * i1
        d2 = s22 - l20 * s02 - l21 * t12
        t23 = s23 - l20 * s03 - l21 * t13
        i2 = 1.0 / d2
        l32 = t23 * i2
        d3 = s33 - l30 * s03 - l31 * t13 - l32 * t23
        i3 = 1.0 / d3
        r1 = r1 - l10 * r0
        r2 = r2 - l20 * r0 - l21 * r1
        r3 = r3 - l30 * r0 - l31 * r1 - l32 * r2
        q0, q1, q2, q3 = r0 * i0, r1 * i1, r2 * i2, r3 * i3
        for i in range(k + 4, R):
            if i < k + 8:
                c0, c1, c2, c3 = (at(rows[i], k + j) for j in range(4))
                c1 = c1 - l10 * c0
                c2 = c2 - l20 * c0 - l21 * c1
                c3 = c3 - l30 * c0 - l31 * c1 - l32 * c2
            else:
                c0, c1, c2, c3 = at(r0, i), at(r1, i), at(r2, i), at(r3, i)
            rows[i] = rows[i] - (c0 * q0 + c1 * q1) - (c2 * q2 + c3 * q3)
        for i, (r, d) in enumerate(((r0, s00), (r1, d1), (r2, d2), (r3, d3))):
            y_ref[8 * (k + i) : 8 * (k + i) + 8] = r * (1.0 / jnp.sqrt(d))
        yield


def comm_kernel(
    g_hbm, e_hbm, q_hbm, g_sum, p_out, y_out, ebuf,
    gbuf, qbuf, mh, ml, qst, p_own, p_recv, p_chip, p_far, g_acc,
    core_recv, recv0, recv1, q_acc, x_acc, recv2, recv3, gram_own, gram_half, gram_recv, gram_out,
    load_sem, p_send, p_arrive, c_send, c_arrive, a_send, a_arrive, b_send, b_arrive,
    gram_send, gram_arrive,
):
    dp, mp = lax.axis_index("dp"), lax.axis_index("mp")
    y_hi, core = lax.div(dp, 2), lax.rem(dp, 2)
    x = lax.rem(mp, 4)
    z = lax.rem(lax.div(mp, 4), 4)
    y = y_hi * 2 + lax.div(mp, 16)

    def device(xx, yy, zz, cc):
        return (lax.div(yy, 2) * 2 + cc, lax.rem(yy, 2) * 16 + zz * 4 + xx)

    def flip(v):
        return v + 1 - 2 * lax.rem(v, 2)

    def side0(v):
        hi = lax.div(v, 2)
        lo = lax.rem(v, 2)
        return hi + lo - 2 * hi * lo

    def side1(v):
        return lax.div(v, 2)

    def over(*links):
        xx, yy, zz = x, y, z
        for link in links:
            if link % 3 == 0:
                xx = flip(x) if link == 0 else 3 - x
            elif link % 3 == 1:
                yy = flip(y) if link == 1 else 3 - y
            else:
                zz = flip(z) if link == 2 else 3 - z
        return device(xx, yy, zz, core)

    near = tuple(over(link) for link in range(6))
    corner = tuple(over(link, (link + 1) % 6) for link in range(6))
    sides = (side0(x), side0(y), side0(z), side1(x), side1(y), side1(z))
    twin = device(x, y, z, 1 - core)
    far = device(x, lax.rem(y + 2, 4), z, core)

    def loads(m):
        return (
            pltpu.make_async_copy(q_hbm.at[m], qbuf.at[m], load_sem.at[m, 0]),
            pltpu.make_async_copy(g_hbm.at[0, m], gbuf.at[m], load_sem.at[m, 1]),
            pltpu.make_async_copy(e_hbm.at[0, m], ebuf.at[m], load_sem.at[m, 2]),
        )

    def begin(m, _):
        for copy in loads(m):
            copy.start()
        return 0

    lax.fori_loop(0, MATS, begin, 0)
    barrier = pltpu.get_barrier_semaphore()
    everyone = near + corner + (twin, far)
    for other in everyone:
        pl.semaphore_signal(barrier, inc=1, device_id=other, device_id_type=MESH)

    def remote(src, dst, send, arrive, target):
        copy = pltpu.make_async_remote_copy(
            src_ref=src, dst_ref=dst, send_sem=send, recv_sem=arrive,
            device_id=target, device_id_type=MESH,
        )
        copy.start()
        return copy

    mine = pl.multiple_of(core * HALF, 8)
    theirs = pl.multiple_of((1 - core) * HALF, 8)
    p_own[...] = jnp.zeros_like(p_own)
    qst[...] = jnp.zeros_like(qst)
    q_acc[...] = jnp.zeros_like(q_acc)

    def local_p(m):
        b = lax.rem(m, 2)
        for copy in loads(m):
            copy.wait()

        def merge(i, _):
            rows = pl.ds(pl.multiple_of(i * 32, 32), 32)
            merged = gbuf[m, rows].astype(f32) + ebuf[m, rows]
            ebuf[m, rows] = merged
            hi, lo = split(merged)
            mh[m, rows] = hi
            ml[m, rows] = lo
            return 0

        lax.fori_loop(0, ROWS // 32, merge, 0)
        hi, lo = split(qbuf[m])
        at = pl.multiple_of(64 * b, 64)
        qst[b, pl.ds(at, 64)] = hi
        qst[b, pl.ds(at + 128, 64)] = lo
        wide = dot_nt(mh[m], qst[b])
        p_own[lax.div(m, 2)] += wide[:, :128] + wide[:, 128:] + dot_nt(ml[m], qst[b, :128])

    def p_copy(s, j):
        if s == 0:
            src, dst, target = p_own.at[j, pl.ds(theirs, HALF)], p_recv.at[j], twin
        elif s == 1:
            src, dst, target = p_chip.at[j], p_far.at[j], far
        else:
            src = dst = p_out.at[j, pl.ds(mine, HALF)]
            target = twin
        return pltpu.make_async_remote_copy(
            src_ref=src, dst_ref=dst, send_sem=p_send.at[s, j], recv_sem=p_arrive.at[s, j],
            device_id=target, device_id_type=MESH,
        )

    def p_step(s, j):
        if s > 0:
            p_copy(s - 1, j).wait()
        if s == 1:
            p_chip[j] = p_own[j, pl.ds(mine, HALF)] + p_recv[j]
        if s == 2:
            p_out[j, pl.ds(mine, HALF)] = (p_chip[j] + p_far[j]) * 0.25
        if s < 3:
            p_copy(s, j).start()

    def p_loop(m, _):
        local_p(m)

        @pl.when(m == 1)
        def _():
            pl.semaphore_wait(barrier, len(everyone))
            p_step(0, 0)

        @pl.when(m == 3)
        def _():
            p_step(0, 1)
            p_step(1, 0)

        @pl.when(m == 5)
        def _():
            p_step(0, 2)
            p_step(1, 1)
            p_step(2, 0)

        return 0

    halves = {}

    def three(src, dst, send, arrive, link):
        targets = (near[(link + 1) % 6], near[link], corner[link])
        return [remote(src(f), dst.at[f], send.at[f], arrive.at[f], targets[f]) for f in range(3)]

    def gram_chain(j):
        halves[j] = hi, lo = split(p_out[j].T)
        square = dot_nt(hi, hi) + (dot_nt(hi, lo) + dot_nt(lo, hi))
        lane = lax.broadcasted_iota(jnp.int32, (R, 2 * R), 1)
        gram_own[j] = jnp.where(lane < 64, square[:64], square[64:])
        rows = pl.ds(pl.multiple_of(core * 32, 32), 32)
        gram_half[j, 0] = gram_own[j, rows]
        for s, link in enumerate((2, 5) if j % 2 == 0 else (5, 2)):
            copies = three(
                lambda f: gram_half.at[j, s], gram_recv.at[j, s], gram_send.at[j, s], gram_arrive.at[j, s], link,
            )
            yield
            for copy in copies:
                copy.wait()
            got = gram_recv.at[j, s]
            gram_half[j, s + 1] = (gram_half[j, s] + got[1]) + (got[0] + got[2])
        copy = remote(
            gram_half.at[j, 2], gram_recv.at[j, 2, 0], gram_send.at[j, 2, 0], gram_arrive.at[j, 2, 0], near[1],
        )
        yield
        copy.wait()
        gram_out[j, rows] = gram_half[j, 2] + gram_recv[j, 2, 0]
        part = gram_out.at[j, rows]
        copy = remote(part, part, gram_send.at[j, 2, 1], gram_arrive.at[j, 2, 1], twin)
        yield
        copy.wait()

    def local_g(m):
        j, b = divmod(m, 2)
        hi, lo = halves[j]
        top = hi[64 * b : 64 * b + 64]
        both = jnp.concatenate([top, lo[64 * b : 64 * b + 64]], axis=0)
        for start, size in COLS:
            cols = slice(start, start + size)
            wide = dot(both, mh[m, :, cols])
            g_acc[m, :, cols] = wide[:64] + wide[64:] + dot(top, ml[m, :, cols])

    def g_chain(m):
        link = [(m + s) % 6 for s in range(6)]
        keep = pl.multiple_of(core * 32, 32)
        give = pl.multiple_of((1 - core) * 32, 32)
        kept0 = pl.multiple_of(core * 32 + 16 * sides[link[0]], 16)
        gone0 = pl.multiple_of(core * 32 + 16 - 16 * sides[link[0]], 16)
        kept1 = pl.multiple_of(kept0 + 8 * sides[link[1]], 8)
        gone1 = pl.multiple_of(kept0 + 8 - 8 * sides[link[1]], 8)
        hi, lo = sides[link[2]], sides[link[3]]

        def block(h, l):
            return pl.ds(pl.multiple_of((2 * h + l) * BLOCK, 128), BLOCK)

        own = block(hi, lo)
        others = (block(hi, 1 - lo), block(1 - hi, lo), block(1 - hi, 1 - lo))

        def pieces(src, first, dst, place, size, send, arrive, target):
            return [
                remote(
                    src.at[m, pl.ds(pl.multiple_of(first + r, 8), 8), pl.ds(0, D)],
                    dst.at[m, pl.ds(pl.multiple_of(place + r, 8), 8), pl.ds(0, D)],
                    send.at[m, r // 8], arrive.at[m, r // 8], target,
                )
                for r in range(0, size, 8)
            ]

        def send(s, src, first, dst, place, size, i):
            return pieces(src, first, dst, place, size, a_send.at[s], a_arrive.at[s], near[link[i]])

        def forward(i, row, size):
            return pieces(g_sum, row, g_sum, row, size, c_send.at[i], c_arrive.at[i], twin)

        def wait(copies):
            for copy in copies:
                copy.wait()

        copy = pieces(g_acc, give, core_recv, 0, 32, c_send.at[0], c_arrive.at[0], twin)
        yield
        wait(copy)
        g_acc[m, pl.ds(keep, 32)] += core_recv[m]
        copy = send(0, g_acc, gone0, recv0, 0, 16, 0)
        yield
        wait(copy)
        g_acc[m, pl.ds(kept0, 16)] += recv0[m]
        copy = send(1, g_acc, gone1, recv1, 0, 8, 1)
        yield
        wait(copy)
        q_acc[m, :, :D] = g_acc[m, pl.ds(kept1, 8)] + recv1[m]
        copies = three(lambda f: q_acc.at[m, :, others[f]], recv2.at[m], b_send.at[0, m], b_arrive.at[0, m], link[2])
        yield
        for copy in copies:
            copy.wait()
        x_acc[m] = (q_acc[m, :, own] + recv2[m, 1]) + (recv2[m, 0] + recv2[m, 2])
        copies = three(lambda f: x_acc.at[m], recv3.at[m], b_send.at[1, m], b_arrive.at[1, m], link[4])
        yield
        for copy in copies:
            copy.wait()
        g_sum[m, pl.ds(kept1, 8), own] = (x_acc[m] + recv3[m, 1]) + (recv3[m, 0] + recv3[m, 2])
        part = g_sum.at[m, pl.ds(kept1, 8), own]
        targets = (near[link[3]], near[link[2]], corner[link[2]])
        copies = [remote(part, part, b_send.at[2, m, f], b_arrive.at[2, m, f], targets[f]) for f in range(3)]
        yield
        for copy in copies:
            copy.wait()
        copy = send(2, g_sum, kept1, g_sum, kept1, 8, 1)
        passed = [forward(1, kept1, 8)]
        yield
        wait(copy)
        copy = send(3, g_sum, kept0, g_sum, kept0, 16, 0)
        passed.append(forward(2, gone1, 8))
        yield
        wait(copy)
        passed.append(forward(3, gone0, 16))
        yield
        for copy in passed:
            wait(copy)

    gc = [gram_chain(j) for j in range(3)]
    ac = [g_chain(m) for m in range(MATS)]
    factor = None

    def behind():
        nonlocal factor
        if factor is None:
            if all([next(chain, 1) for chain in gc]):
                factor = eliminate([gram_out[j] for j in range(3)], y_out)
        if factor is not None:
            next(factor, None)

    lax.fori_loop(0, MATS, p_loop, 0)
    p_step(1, 2)
    p_step(3, 0)
    next(gc[0])
    local_g(0)
    next(ac[0])
    p_step(2, 1)
    local_g(1)
    next(ac[1])
    p_step(2, 2)
    p_step(3, 1)
    next(gc[1])
    next(gc[0])
    local_g(2)
    next(ac[2])
    next(ac[0])
    local_g(3)
    next(ac[3])
    next(ac[1])
    p_step(3, 2)
    next(gc[2])
    next(gc[1])
    next(gc[0])
    local_g(4)
    next(ac[4])
    next(ac[2])
    local_g(5)
    next(ac[5])
    next(ac[3])
    next(gc[2])
    next(gc[1])
    next(gc[0])
    next(ac[4])
    next(ac[5])
    for s in range(8):
        for m in range(MATS):
            next(ac[m], None)
            if factor is not None or m in (2, 5):
                behind()
    for _ in factor:
        pass


def finish_kernel(
    g_sum, p_ref, y_ref, m_ref, err_hbm, q_out, mbuf, new_q, wst, store_sem, q_sem,
):
    lane = lax.broadcasted_iota(jnp.int32, (R, 2 * R), 1)
    wide_lane = lax.broadcasted_iota(jnp.int32, (ROWS, 2 * R), 1)
    stores = []
    for m in range(MATS):
        b = m % 2
        side = jnp.where(lane >= 64, y_ref[pl.ds(m, R, stride=8), :], 0.0)
        other = pltpu.roll(side, 64, axis=1)
        inverse = side if b else other
        bh, bl = split(jnp.concatenate([inverse, inverse], axis=0))
        ph, pl_ = split(p_ref[m // 2])
        ortho = dot_nt(ph, bh) + (dot_nt(ph, bl) + dot_nt(pl_, bh))
        oh, ol = split(ortho)
        lhs = jnp.concatenate([jnp.where(wide_lane < 64, oh, ol), oh[:, :64]], axis=1)
        lh, ll = split(side + other)
        lhs_q = jnp.concatenate([jnp.where(lane < 64, lh, ll), lh[:, :64]], axis=1)
        gh, gl = split(g_sum[m, :, :D] * 0.25)
        wst[0, 0:64] = gh
        wst[0, 64:128] = gh
        wst[0, 128:192] = gl
        fresh = dot(lhs_q, wst[0])
        new_q[m] = fresh
        store = pltpu.make_async_copy(new_q.at[m], q_out.at[m], q_sem.at[m])
        store.start()
        stores.append(store)
        nh, nl = split(fresh)
        wst[1, 0:64] = nh
        wst[1, 64:128] = nh
        wst[1, 128:192] = nl
        for start, size in COLS:
            cols = slice(start, start + size)
            mbuf[m, :, cols] = m_ref[m, :, cols] - dot(lhs, wst[1, :, cols])
        store = pltpu.make_async_copy(mbuf.at[m], err_hbm.at[0, m], store_sem.at[m])
        store.start()
        stores.append(store)
    for store in stores:
        store.wait()


def body(gradients, errors, previous_q):
    vmem = pl.BlockSpec(memory_space=pltpu.VMEM)
    far_hbm = pl.BlockSpec(memory_space=pltpu.HBM)
    sem = pltpu.SemaphoreType.DMA
    g_sum, p_mat, y_mat, merged = pl.pallas_call(
        comm_kernel,
        out_shape=(
            jax.ShapeDtypeStruct((MATS, R, 4 * BLOCK), f32),
            jax.ShapeDtypeStruct((MATS // 2, ROWS, 2 * R), f32),
            jax.ShapeDtypeStruct((8 * R, 2 * R), f32),
            jax.ShapeDtypeStruct((MATS, ROWS, D), f32),
        ),
        in_specs=[far_hbm, far_hbm, far_hbm],
        out_specs=(vmem, vmem, vmem, vmem),
        scratch_shapes=[
            pltpu.VMEM((MATS, ROWS, D), bf16),
            pltpu.VMEM((MATS, R, D), f32),
            pltpu.VMEM((MATS, ROWS, D), bf16),
            pltpu.VMEM((MATS, ROWS, D), bf16),
            pltpu.VMEM((2, 256, D), bf16),
            pltpu.VMEM((MATS // 2, ROWS, 128), f32),
            pltpu.VMEM((MATS // 2, HALF, 128), f32),
            pltpu.VMEM((MATS // 2, HALF, 128), f32),
            pltpu.VMEM((MATS // 2, HALF, 128), f32),
            pltpu.VMEM((MATS, R, D), f32),
            pltpu.VMEM((MATS, 32, D), f32),
            pltpu.VMEM((MATS, 16, D), f32),
            pltpu.VMEM((MATS, 8, D), f32),
            pltpu.VMEM((MATS, 8, 4 * BLOCK), f32),
            pltpu.VMEM((MATS, 8, BLOCK), f32),
            pltpu.VMEM((MATS, 3, 8, BLOCK), f32),
            pltpu.VMEM((MATS, 3, 8, BLOCK), f32),
            pltpu.VMEM((MATS // 2, R, 2 * R), f32),
            pltpu.VMEM((MATS // 2, 3, R // 2, 2 * R), f32),
            pltpu.VMEM((MATS // 2, 3, 3, R // 2, 2 * R), f32),
            pltpu.VMEM((MATS // 2, R, 2 * R), f32),
            sem((MATS, 3)),
            sem((3, 3)),
            sem((3, 3)),
            sem((4, MATS, 4)),
            sem((4, MATS, 4)),
            sem((4, MATS, 2)),
            sem((4, MATS, 2)),
            sem((3, MATS, 3)),
            sem((3, MATS, 3)),
            sem((3, 3, 3)),
            sem((3, 3, 3)),
        ],
        compiler_params=pltpu.CompilerParams(
            collective_id=0, has_side_effects=True, vmem_limit_bytes=40 * 2**20
        ),
        name="compress_and_sum",
    )(*[pltpu.with_memory_space_constraint(v, pltpu.HBM) for v in (gradients, errors, previous_q)])
    return pl.pallas_call(
        finish_kernel,
        out_shape=(
            jax.ShapeDtypeStruct((1, MATS, ROWS, D), f32),
            jax.ShapeDtypeStruct((MATS, R, D), f32),
        ),
        in_specs=[vmem, vmem, vmem, vmem],
        out_specs=(far_hbm, far_hbm),
        scratch_shapes=[
            pltpu.VMEM((MATS, ROWS, D), f32),
            pltpu.VMEM((MATS, R, D), f32),
            pltpu.VMEM((2, ROWS, D), bf16),
            sem((MATS,)),
            sem((MATS,)),
        ],
        compiler_params=pltpu.CompilerParams(vmem_limit_bytes=24 * 2**20),
        name="new_q_and_errors",
    )(g_sum, p_mat, y_mat, merged)


def solution(mesh):
    in_specs = (P("dp", None, "mp", None), P("dp", None, "mp", None), P())
    out_specs = (P("dp", None, "mp", None), P())
    return jax.shard_map(body, mesh=mesh, in_specs=in_specs, out_specs=out_specs, check_vma=False)
```

```python
import functools

import jax
import jax.numpy as jnp
from jax import lax
from jax.experimental import pallas as pl
from jax.experimental.pallas import tpu as pltpu
from jax.sharding import PartitionSpec as P

MESH = pl.DeviceIdType.MESH
MATS, ROWS, D, R = 6, 192, 1408, 64
HALF = ROWS // 2
BLOCK = 384
COLS = ((0, 512), (512, 512), (1024, 384))
f32, bf16 = jnp.float32, jnp.bfloat16
NT = (((1,), (1,)), ((), ()))


def dot(a, b):
    return jnp.dot(a, b, preferred_element_type=f32)


def dot_nt(a, b):
    return lax.dot_general(a, b, NT, preferred_element_type=f32)


def split(x):
    hi = x.astype(bf16)
    return hi, (x - hi.astype(f32)).astype(bf16)


def eliminate(grams, y_ref):
    row = lax.broadcasted_iota(jnp.int32, (R, 2 * R), 0)
    lane = lax.broadcasted_iota(jnp.int32, (R, 2 * R), 1)
    eye = jnp.where(lane == row + 64, 1.0, 0.0)
    unit = jnp.where(lane == row, 1.0, 0.0)
    for m in range(8):
        if m < MATS:
            gram = grams[m // 2]
            gram = pltpu.roll(gram, 64, axis=1) if m % 2 else gram
        else:
            gram = unit
        y_ref[pl.ds(m, R, stride=8), :] = jnp.where(lane < 64, gram, eye)
    rows = [y_ref[8 * i : 8 * i + 8] for i in range(R)]

    def at(r, k):
        return jnp.broadcast_to(r[:, k : k + 1], (8, 128))

    for k in range(0, R, 4):
        r0, r1, r2, r3 = rows[k : k + 4]
        s00, s01, s02, s03 = (at(r0, k + i) for i in range(4))
        s11, s12, s13 = (at(r1, k + i) for i in range(1, 4))
        s22, s23, s33 = at(r2, k + 2), at(r2, k + 3), at(r3, k + 3)
        i0 = 1.0 / s00
        l10, l20, l30 = s01 * i0, s02 * i0, s03 * i0
        d1 = s11 - l10 * s01
        t12, t13 = s12 - l10 * s02, s13 - l10 * s03
        i1 = 1.0 / d1
        l21, l31 = t12 * i1, t13 * i1
        d2 = s22 - l20 * s02 - l21 * t12
        t23 = s23 - l20 * s03 - l21 * t13
        i2 = 1.0 / d2
        l32 = t23 * i2
        d3 = s33 - l30 * s03 - l31 * t13 - l32 * t23
        i3 = 1.0 / d3
        r1 = r1 - l10 * r0
        r2 = r2 - l20 * r0 - l21 * r1
        r3 = r3 - l30 * r0 - l31 * r1 - l32 * r2
        q0, q1, q2, q3 = r0 * i0, r1 * i1, r2 * i2, r3 * i3
        for i in range(k + 4, R):
            if i < k + 8:
                c0, c1, c2, c3 = (at(rows[i], k + j) for j in range(4))
                c1 = c1 - l10 * c0
                c2 = c2 - l20 * c0 - l21 * c1
                c3 = c3 - l30 * c0 - l31 * c1 - l32 * c2
            else:
                c0, c1, c2, c3 = at(r0, i), at(r1, i), at(r2, i), at(r3, i)
            rows[i] = rows[i] - (c0 * q0 + c1 * q1) - (c2 * q2 + c3 * q3)
        for i, (r, d) in enumerate(((r0, s00), (r1, d1), (r2, d2), (r3, d3))):
            y_ref[8 * (k + i) : 8 * (k + i) + 8] = r * (1.0 / jnp.sqrt(d))
        yield


def comm_kernel(
    g_hbm, e_hbm, q_hbm, g_sum, p_out, y_out, ebuf,
    gbuf, qbuf, mh, ml, qst, p_own, p_recv, p_chip, p_far, g_acc,
    core_recv, recv0, recv1, q_acc, x_acc, recv2, recv3, gram_own, gram_half, gram_recv, gram_out,
    load_sem, p_send, p_arrive, c_send, c_arrive, a_send, a_arrive, b_send, b_arrive,
    gram_send, gram_arrive,
):
    dp, mp = lax.axis_index("dp"), lax.axis_index("mp")
    y_hi, core = lax.div(dp, 2), lax.rem(dp, 2)
    x = lax.rem(mp, 4)
    z = lax.rem(lax.div(mp, 4), 4)
    y = y_hi * 2 + lax.div(mp, 16)

    def device(xx, yy, zz, cc):
        return (lax.div(yy, 2) * 2 + cc, lax.rem(yy, 2) * 16 + zz * 4 + xx)

    def flip(v):
        return v + 1 - 2 * lax.rem(v, 2)

    def side0(v):
        hi = lax.div(v, 2)
        lo = lax.rem(v, 2)
        return hi + lo - 2 * hi * lo

    def side1(v):
        return lax.div(v, 2)

    def over(*links):
        xx, yy, zz = x, y, z
        for link in links:
            if link % 3 == 0:
                xx = flip(x) if link == 0 else 3 - x
            elif link % 3 == 1:
                yy = flip(y) if link == 1 else 3 - y
            else:
                zz = flip(z) if link == 2 else 3 - z
        return device(xx, yy, zz, core)

    near = tuple(over(link) for link in range(6))
    corner = tuple(over(link, (link + 1) % 6) for link in range(6))
    sides = (side0(x), side0(y), side0(z), side1(x), side1(y), side1(z))
    twin = device(x, y, z, 1 - core)
    far = device(x, lax.rem(y + 2, 4), z, core)

    def loads(m):
        return (
            pltpu.make_async_copy(q_hbm.at[m], qbuf.at[m], load_sem.at[m, 0]),
            pltpu.make_async_copy(g_hbm.at[0, m], gbuf.at[m], load_sem.at[m, 1]),
            pltpu.make_async_copy(e_hbm.at[0, m], ebuf.at[m], load_sem.at[m, 2]),
        )

    def begin(m, _):
        for copy in loads(m):
            copy.start()
        return 0

    lax.fori_loop(0, MATS, begin, 0)
    barrier = pltpu.get_barrier_semaphore()
    everyone = near + corner + (twin, far)
    for other in everyone:
        pl.semaphore_signal(barrier, inc=1, device_id=other, device_id_type=MESH)

    sent = []

    def remote(src, dst, send, arrive, target):
        copy = pltpu.make_async_remote_copy(
            src_ref=src, dst_ref=dst, send_sem=send, recv_sem=arrive,
            device_id=target, device_id_type=MESH,
        )
        copy.start()
        sent.append(copy)
        return copy

    mine = pl.multiple_of(core * HALF, 8)
    theirs = pl.multiple_of((1 - core) * HALF, 8)
    p_own[...] = jnp.zeros_like(p_own)
    qst[...] = jnp.zeros_like(qst)
    q_acc[...] = jnp.zeros_like(q_acc)

    def local_p(m):
        b = lax.rem(m, 2)
        for copy in loads(m):
            copy.wait()

        def merge(i, _):
            rows = pl.ds(pl.multiple_of(i * 32, 32), 32)
            merged = gbuf[m, rows].astype(f32) + ebuf[m, rows]
            ebuf[m, rows] = merged
            hi, lo = split(merged)
            mh[m, rows] = hi
            ml[m, rows] = lo
            return 0

        lax.fori_loop(0, ROWS // 32, merge, 0)
        hi, lo = split(qbuf[m])
        at = pl.multiple_of(64 * b, 64)
        qst[b, pl.ds(at, 64)] = hi
        qst[b, pl.ds(at + 128, 64)] = lo
        wide = dot_nt(mh[m], qst[b])
        p_own[lax.div(m, 2)] += wide[:, :128] + wide[:, 128:] + dot_nt(ml[m], qst[b, :128])

    def p_copy(s, j):
        if s == 0:
            src, dst, target = p_own.at[j, pl.ds(theirs, HALF)], p_recv.at[j], twin
        elif s == 1:
            src, dst, target = p_chip.at[j], p_far.at[j], far
        else:
            src = dst = p_out.at[j, pl.ds(mine, HALF)]
            target = twin
        return pltpu.make_async_remote_copy(
            src_ref=src, dst_ref=dst, send_sem=p_send.at[s, j], recv_sem=p_arrive.at[s, j],
            device_id=target, device_id_type=MESH,
        )

    def p_step(s, j):
        if s > 0:
            p_copy(s - 1, j).wait_recv()
        if s == 1:
            p_chip[j] = p_own[j, pl.ds(mine, HALF)] + p_recv[j]
        if s == 2:
            p_out[j, pl.ds(mine, HALF)] = (p_chip[j] + p_far[j]) * 0.25
        if s < 3:
            p_copy(s, j).start()

    def p_loop(m, _):
        local_p(m)

        @pl.when(m == 1)
        def _():
            pl.semaphore_wait(barrier, len(everyone))
            p_step(0, 0)

        @pl.when(m == 3)
        def _():
            p_step(0, 1)
            p_step(1, 0)

        @pl.when(m == 5)
        def _():
            p_step(0, 2)
            p_step(1, 1)
            p_step(2, 0)

        return 0

    halves = {}

    def three(src, dst, send, arrive, link):
        targets = (near[(link + 1) % 6], near[link], corner[link])
        return [remote(src(f), dst.at[f], send.at[f], arrive.at[f], targets[f]) for f in range(3)]

    def gram_chain(j):
        halves[j] = hi, lo = split(p_out[j].T)
        square = dot_nt(hi, hi) + (dot_nt(hi, lo) + dot_nt(lo, hi))
        lane = lax.broadcasted_iota(jnp.int32, (R, 2 * R), 1)
        gram_own[j] = jnp.where(lane < 64, square[:64], square[64:])
        rows = pl.ds(pl.multiple_of(core * 32, 32), 32)
        gram_half[j, 0] = gram_own[j, rows]
        for s, link in enumerate((2, 5) if j % 2 == 0 else (5, 2)):
            copies = three(
                lambda f: gram_half.at[j, s], gram_recv.at[j, s], gram_send.at[j, s], gram_arrive.at[j, s], link,
            )
            yield
            for copy in copies:
                copy.wait_recv()
            got = gram_recv.at[j, s]
            gram_half[j, s + 1] = (gram_half[j, s] + got[1]) + (got[0] + got[2])
        copy = remote(
            gram_half.at[j, 2], gram_recv.at[j, 2, 0], gram_send.at[j, 2, 0], gram_arrive.at[j, 2, 0], near[1],
        )
        yield
        copy.wait_recv()
        gram_out[j, rows] = gram_half[j, 2] + gram_recv[j, 2, 0]
        part = gram_out.at[j, rows]
        copy = remote(part, part, gram_send.at[j, 2, 1], gram_arrive.at[j, 2, 1], twin)
        yield
        copy.wait_recv()

    def local_g(m):
        j, b = divmod(m, 2)
        hi, lo = halves[j]
        top = hi[64 * b : 64 * b + 64]
        both = jnp.concatenate([top, lo[64 * b : 64 * b + 64]], axis=0)
        for start, size in COLS:
            cols = slice(start, start + size)
            wide = dot(both, mh[m, :, cols])
            g_acc[m, :, cols] = wide[:64] + wide[64:] + dot(top, ml[m, :, cols])

    def g_chain(m):
        link = [(m + s) % 6 for s in range(6)]
        keep = pl.multiple_of(core * 32, 32)
        give = pl.multiple_of((1 - core) * 32, 32)
        kept0 = pl.multiple_of(core * 32 + 16 * sides[link[0]], 16)
        gone0 = pl.multiple_of(core * 32 + 16 - 16 * sides[link[0]], 16)
        kept1 = pl.multiple_of(kept0 + 8 * sides[link[1]], 8)
        gone1 = pl.multiple_of(kept0 + 8 - 8 * sides[link[1]], 8)
        hi, lo = sides[link[2]], sides[link[3]]

        def block(h, l):
            return pl.ds(pl.multiple_of((2 * h + l) * BLOCK, 128), BLOCK)

        own = block(hi, lo)
        others = (block(hi, 1 - lo), block(1 - hi, lo), block(1 - hi, 1 - lo))

        def send(s, src, dst, i):
            return remote(src, dst, a_send.at[s, m], a_arrive.at[s, m], near[link[i]])

        def forward(i, row, size):
            part = g_sum.at[m, pl.ds(row, size), pl.ds(0, D)]
            return remote(part, part, c_send.at[i, m], c_arrive.at[i, m], twin)

        copy = remote(g_acc.at[m, pl.ds(give, 32)], core_recv.at[m], c_send.at[0, m], c_arrive.at[0, m], twin)
        yield
        copy.wait_recv()
        g_acc[m, pl.ds(keep, 32)] += core_recv[m]
        copy = send(0, g_acc.at[m, pl.ds(gone0, 16)], recv0.at[m], 0)
        yield
        copy.wait_recv()
        g_acc[m, pl.ds(kept0, 16)] += recv0[m]
        copy = send(1, g_acc.at[m, pl.ds(gone1, 8)], recv1.at[m], 1)
        yield
        copy.wait_recv()
        q_acc[m, :, :D] = g_acc[m, pl.ds(kept1, 8)] + recv1[m]
        copies = three(lambda f: q_acc.at[m, :, others[f]], recv2.at[m], b_send.at[0, m], b_arrive.at[0, m], link[2])
        yield
        for copy in copies:
            copy.wait_recv()
        x_acc[m] = (q_acc[m, :, own] + recv2[m, 1]) + (recv2[m, 0] + recv2[m, 2])
        copies = three(lambda f: x_acc.at[m], recv3.at[m], b_send.at[1, m], b_arrive.at[1, m], link[4])
        yield
        for copy in copies:
            copy.wait_recv()
        g_sum[m, pl.ds(kept1, 8), own] = (x_acc[m] + recv3[m, 1]) + (recv3[m, 0] + recv3[m, 2])
        part = g_sum.at[m, pl.ds(kept1, 8), own]
        targets = (near[link[3]], near[link[2]], corner[link[2]])
        copies = [remote(part, part, b_send.at[2, m, f], b_arrive.at[2, m, f], targets[f]) for f in range(3)]
        yield
        for copy in copies:
            copy.wait_recv()
        part = g_sum.at[m, pl.ds(kept1, 8), pl.ds(0, D)]
        copy = send(2, part, part, 1)
        passed = [forward(1, kept1, 8)]
        yield
        copy.wait_recv()
        part = g_sum.at[m, pl.ds(kept0, 16), pl.ds(0, D)]
        copy = send(3, part, part, 0)
        passed.append(forward(2, gone1, 8))
        yield
        copy.wait_recv()
        passed.append(forward(3, gone0, 16))
        yield
        for copy in passed:
            copy.wait_recv()

    gc = [gram_chain(j) for j in range(3)]
    ac = [g_chain(m) for m in range(MATS)]
    factor = None

    def behind():
        nonlocal factor
        if factor is None:
            if all([next(chain, 1) for chain in gc]):
                factor = eliminate([gram_out[j] for j in range(3)], y_out)
        if factor is not None:
            next(factor, None)

    lax.fori_loop(0, MATS, p_loop, 0)
    p_step(1, 2)
    p_step(3, 0)
    next(gc[0])
    local_g(0)
    next(ac[0])
    p_step(2, 1)
    local_g(1)
    next(ac[1])
    p_step(2, 2)
    p_step(3, 1)
    next(gc[1])
    next(gc[0])
    local_g(2)
    next(ac[2])
    next(ac[0])
    local_g(3)
    next(ac[3])
    next(ac[1])
    p_step(3, 2)
    next(gc[2])
    next(gc[1])
    next(gc[0])
    local_g(4)
    next(ac[4])
    next(ac[2])
    local_g(5)
    next(ac[5])
    next(ac[3])
    next(gc[2])
    next(gc[1])
    next(gc[0])
    next(ac[4])
    next(ac[5])
    for s in range(8):
        for m in range(MATS):
            next(ac[m], None)
            if factor is not None or m in (2, 5):
                behind()
    for _ in factor:
        pass
    for s in range(3):
        for j in range(3):
            p_copy(s, j).wait_send()
    for copy in sent:
        copy.wait_send()


def finish_kernel(
    g_sum, p_ref, y_ref, m_ref, err_hbm, q_out, mbuf, new_q, wst, store_sem, q_sem,
):
    lane = lax.broadcasted_iota(jnp.int32, (R, 2 * R), 1)
    wide_lane = lax.broadcasted_iota(jnp.int32, (ROWS, 2 * R), 1)
    stores = []
    for m in range(MATS):
        b = m % 2
        side = jnp.where(lane >= 64, y_ref[pl.ds(m, R, stride=8), :], 0.0)
        other = pltpu.roll(side, 64, axis=1)
        inverse = side if b else other
        bh, bl = split(jnp.concatenate([inverse, inverse], axis=0))
        ph, pl_ = split(p_ref[m // 2])
        ortho = dot_nt(ph, bh) + (dot_nt(ph, bl) + dot_nt(pl_, bh))
        oh, ol = split(ortho)
        lhs = jnp.concatenate([jnp.where(wide_lane < 64, oh, ol), oh[:, :64]], axis=1)
        lh, ll = split(side + other)
        lhs_q = jnp.concatenate([jnp.where(lane < 64, lh, ll), lh[:, :64]], axis=1)
        gh, gl = split(g_sum[m, :, :D] * 0.25)
        wst[0, 0:64] = gh
        wst[0, 64:128] = gh
        wst[0, 128:192] = gl
        fresh = dot(lhs_q, wst[0])
        new_q[m] = fresh
        store = pltpu.make_async_copy(new_q.at[m], q_out.at[m], q_sem.at[m])
        store.start()
        stores.append(store)
        nh, nl = split(fresh)
        wst[1, 0:64] = nh
        wst[1, 64:128] = nh
        wst[1, 128:192] = nl
        for start, size in COLS:
            cols = slice(start, start + size)
            mbuf[m, :, cols] = m_ref[m, :, cols] - dot(lhs, wst[1, :, cols])
        store = pltpu.make_async_copy(mbuf.at[m], err_hbm.at[0, m], store_sem.at[m])
        store.start()
        stores.append(store)
    for store in stores:
        store.wait()


def body(gradients, errors, previous_q):
    vmem = pl.BlockSpec(memory_space=pltpu.VMEM)
    far_hbm = pl.BlockSpec(memory_space=pltpu.HBM)
    sem = pltpu.SemaphoreType.DMA
    g_sum, p_mat, y_mat, merged = pl.pallas_call(
        comm_kernel,
        out_shape=(
            jax.ShapeDtypeStruct((MATS, R, 4 * BLOCK), f32),
            jax.ShapeDtypeStruct((MATS // 2, ROWS, 2 * R), f32),
            jax.ShapeDtypeStruct((8 * R, 2 * R), f32),
            jax.ShapeDtypeStruct((MATS, ROWS, D), f32),
        ),
        in_specs=[far_hbm, far_hbm, far_hbm],
        out_specs=(vmem, vmem, vmem, vmem),
        scratch_shapes=[
            pltpu.VMEM((MATS, ROWS, D), bf16),
            pltpu.VMEM((MATS, R, D), f32),
            pltpu.VMEM((MATS, ROWS, D), bf16),
            pltpu.VMEM((MATS, ROWS, D), bf16),
            pltpu.VMEM((2, 256, D), bf16),
            pltpu.VMEM((MATS // 2, ROWS, 128), f32),
            pltpu.VMEM((MATS // 2, HALF, 128), f32),
            pltpu.VMEM((MATS // 2, HALF, 128), f32),
            pltpu.VMEM((MATS // 2, HALF, 128), f32),
            pltpu.VMEM((MATS, R, D), f32),
            pltpu.VMEM((MATS, 32, D), f32),
            pltpu.VMEM((MATS, 16, D), f32),
            pltpu.VMEM((MATS, 8, D), f32),
            pltpu.VMEM((MATS, 8, 4 * BLOCK), f32),
            pltpu.VMEM((MATS, 8, BLOCK), f32),
            pltpu.VMEM((MATS, 3, 8, BLOCK), f32),
            pltpu.VMEM((MATS, 3, 8, BLOCK), f32),
            pltpu.VMEM((MATS // 2, R, 2 * R), f32),
            pltpu.VMEM((MATS // 2, 3, R // 2, 2 * R), f32),
            pltpu.VMEM((MATS // 2, 3, 3, R // 2, 2 * R), f32),
            pltpu.VMEM((MATS // 2, R, 2 * R), f32),
            sem((MATS, 3)),
            sem((3, 3)),
            sem((3, 3)),
            sem((4, MATS)),
            sem((4, MATS)),
            sem((4, MATS)),
            sem((4, MATS)),
            sem((3, MATS, 3)),
            sem((3, MATS, 3)),
            sem((3, 3, 3)),
            sem((3, 3, 3)),
        ],
        compiler_params=pltpu.CompilerParams(
            collective_id=0, has_side_effects=True, vmem_limit_bytes=40 * 2**20
        ),
        name="compress_and_sum",
    )(*[pltpu.with_memory_space_constraint(v, pltpu.HBM) for v in (gradients, errors, previous_q)])
    return pl.pallas_call(
        finish_kernel,
        out_shape=(
            jax.ShapeDtypeStruct((1, MATS, ROWS, D), f32),
            jax.ShapeDtypeStruct((MATS, R, D), f32),
        ),
        in_specs=[vmem, vmem, vmem, vmem],
        out_specs=(far_hbm, far_hbm),
        scratch_shapes=[
            pltpu.VMEM((MATS, ROWS, D), f32),
            pltpu.VMEM((MATS, R, D), f32),
            pltpu.VMEM((2, ROWS, D), bf16),
            sem((MATS,)),
            sem((MATS,)),
        ],
        compiler_params=pltpu.CompilerParams(vmem_limit_bytes=24 * 2**20),
        name="new_q_and_errors",
    )(g_sum, p_mat, y_mat, merged)


def solution(mesh):
    in_specs = (P("dp", None, "mp", None), P("dp", None, "mp", None), P())
    out_specs = (P("dp", None, "mp", None), P())
    return jax.shard_map(body, mesh=mesh, in_specs=in_specs, out_specs=out_specs, check_vma=False)
```

```python
import functools

import jax
import jax.numpy as jnp
from jax import lax
from jax.experimental import pallas as pl
from jax.experimental.pallas import tpu as pltpu
from jax.sharding import PartitionSpec as P

MESH = pl.DeviceIdType.MESH
MATS, ROWS, D, R = 6, 192, 1408, 64
HALF = ROWS // 2
BLOCK = 384
COLS = ((0, 512), (512, 512), (1024, 384))
f32, bf16 = jnp.float32, jnp.bfloat16
FIRST_LINK = (0, 3, 2, 5, 1, 4)
ORDER = (
    ("products", 0), ("p", 0), ("products", 1), ("p", 1), ("p", 0), ("products", 2), ("p", 2), ("p", 1),
    ("p", 2), ("p", 0), ("p", 0), ("gram", 0), ("terms", 0), ("sum", 0), ("terms", 1), ("p", 1), ("sum", 1),
    ("sum", 0), ("p", 1), ("gram", 1), ("sum", 1), ("terms", 2), ("p", 2), ("gram", 0), ("sum", 2),
    ("terms", 3), ("p", 2), ("gram", 2), ("sum", 3), ("terms", 4), ("sum", 4), ("sum", 2), ("terms", 5),
    ("sum", 5), ("sum", 3), ("sum", 4), ("sum", 5), ("sum", 0), ("sum", 1), ("gram", 1), ("gram", 2),
    ("gram", 0), ("sum", 2), ("sum", 3), ("sum", 4), ("sum", 5), ("gram", 1), ("gram", 2), ("sum", 0),
    ("sum", 1), ("gram", 0), ("sum", 2), ("sum", 4), ("gram", 0), ("gram", 1), ("sum", 3), ("sum", 5),
    ("gram", 2), ("gram", 1), ("gram", 2), ("factor", 2), ("sum", 0), ("sum", 1), ("factor", 2), ("sum", 2),
    ("sum", 3), ("sum", 4), ("sum", 5), ("factor", 2), ("factor", 2), ("sum", 0), ("sum", 1), ("factor", 2),
    ("sum", 2), ("sum", 3), ("sum", 4), ("sum", 5), ("factor", 2), ("factor", 2), ("sum", 0), ("sum", 1),
    ("factor", 2), ("sum", 2), ("sum", 3), ("sum", 4), ("factor", 1), ("sum", 5), ("sum", 0), ("sum", 1),
    ("factor", 1), ("sum", 2), ("sum", 3), ("sum", 4), ("factor", 1), ("sum", 5), ("sum", 0), ("sum", 1),
    ("sum", 0), ("sum", 2), ("sum", 1), ("sum", 3), ("sum", 4), ("sum", 5), ("sum", 2), ("sum", 3),
    ("sum", 4), ("sum", 5),
)
NT = (((1,), (1,)), ((), ()))


def dot(a, b):
    return jnp.dot(a, b, preferred_element_type=f32)


def dot_nt(a, b):
    return lax.dot_general(a, b, NT, preferred_element_type=f32)


def split(x):
    hi = x.astype(bf16)
    return hi, (x - hi.astype(f32)).astype(bf16)


def eliminate(grams, y_ref, p_ref, lhs_err, lhs_q):
    row = lax.broadcasted_iota(jnp.int32, (R, 2 * R), 0)
    lane = lax.broadcasted_iota(jnp.int32, (R, 2 * R), 1)
    eye = jnp.where(lane == row + 64, 1.0, 0.0)
    unit = jnp.where(lane == row, 1.0, 0.0)
    for m in range(8):
        if m < MATS:
            gram = grams[m // 2]
            gram = pltpu.roll(gram, 64, axis=1) if m % 2 else gram
        else:
            gram = unit
        y_ref[pl.ds(m, R, stride=8), :] = jnp.where(lane < 64, gram, eye)
    rows = [y_ref[8 * i : 8 * i + 8] for i in range(R)]

    def at(r, k):
        return jnp.broadcast_to(r[:, k : k + 1], (8, 128))

    for k in range(0, R, 4):
        r0, r1, r2, r3 = rows[k : k + 4]
        s00, s01, s02, s03 = (at(r0, k + i) for i in range(4))
        s11, s12, s13 = (at(r1, k + i) for i in range(1, 4))
        s22, s23, s33 = at(r2, k + 2), at(r2, k + 3), at(r3, k + 3)
        i0 = 1.0 / s00
        l10, l20, l30 = s01 * i0, s02 * i0, s03 * i0
        d1 = s11 - l10 * s01
        t12, t13 = s12 - l10 * s02, s13 - l10 * s03
        i1 = 1.0 / d1
        l21, l31 = t12 * i1, t13 * i1
        d2 = s22 - l20 * s02 - l21 * t12
        t23 = s23 - l20 * s03 - l21 * t13
        i2 = 1.0 / d2
        l32 = t23 * i2
        d3 = s33 - l30 * s03 - l31 * t13 - l32 * t23
        i3 = 1.0 / d3
        r1 = r1 - l10 * r0
        r2 = r2 - l20 * r0 - l21 * r1
        r3 = r3 - l30 * r0 - l31 * r1 - l32 * r2
        q0, q1, q2, q3 = r0 * i0, r1 * i1, r2 * i2, r3 * i3
        for i in range(k + 4, R):
            if i < k + 8:
                c0, c1, c2, c3 = (at(rows[i], k + j) for j in range(4))
                c1 = c1 - l10 * c0
                c2 = c2 - l20 * c0 - l21 * c1
                c3 = c3 - l30 * c0 - l31 * c1 - l32 * c2
            else:
                c0, c1, c2, c3 = at(r0, i), at(r1, i), at(r2, i), at(r3, i)
            rows[i] = rows[i] - (c0 * q0 + c1 * q1) - (c2 * q2 + c3 * q3)
        for i, (r, d) in enumerate(((r0, s00), (r1, d1), (r2, d2), (r3, d3))):
            y_ref[8 * (k + i) : 8 * (k + i) + 8] = r * (1.0 / jnp.sqrt(d))
        yield
    wide_lane = lax.broadcasted_iota(jnp.int32, (ROWS, 2 * R), 1)
    for m in range(MATS):
        side = jnp.where(lane >= 64, y_ref[pl.ds(m, R, stride=8), :], 0.0)
        other = pltpu.roll(side, 64, axis=1)
        inverse = side if m % 2 else other
        bh, bl = split(jnp.concatenate([inverse, inverse], axis=0))
        ph, pl_ = split(p_ref[m // 2])
        ortho = dot_nt(ph, bh) + (dot_nt(ph, bl) + dot_nt(pl_, bh))
        oh, ol = split(ortho)
        lhs_err[m] = jnp.concatenate([jnp.where(wide_lane < 64, oh, ol), oh], axis=1)
        lh, ll = split(side + other)
        lhs_q[m] = jnp.concatenate([jnp.where(lane < 64, lh, ll), lh], axis=1)
        if m % 2:
            yield


def comm_kernel(
    g_hbm, e_hbm, q_hbm, g_sum, lhs_err, lhs_q, ebuf,
    p_out, y_out, gbuf, qbuf, mh, ml, qst, p_own, p_recv, p_chip, p_far, g_acc,
    core_recv, recv0, recv1, q_acc, x_acc, recv2, recv3, gram_own, gram_half, gram_recv, gram_out,
    load_sem, p_send, p_arrive, c_send, c_arrive, a_send, a_arrive, b_send, b_arrive,
    gram_send, gram_arrive,
):
    dp, mp = lax.axis_index("dp"), lax.axis_index("mp")
    y_hi, core = lax.div(dp, 2), lax.rem(dp, 2)
    x = lax.rem(mp, 4)
    z = lax.rem(lax.div(mp, 4), 4)
    y = y_hi * 2 + lax.div(mp, 16)

    def device(xx, yy, zz, cc):
        return (lax.div(yy, 2) * 2 + cc, lax.rem(yy, 2) * 16 + zz * 4 + xx)

    def flip(v):
        return v + 1 - 2 * lax.rem(v, 2)

    def side0(v):
        hi = lax.div(v, 2)
        lo = lax.rem(v, 2)
        return hi + lo - 2 * hi * lo

    def side1(v):
        return lax.div(v, 2)

    def over(*links):
        xx, yy, zz = x, y, z
        for link in links:
            if link % 3 == 0:
                xx = flip(x) if link == 0 else 3 - x
            elif link % 3 == 1:
                yy = flip(y) if link == 1 else 3 - y
            else:
                zz = flip(z) if link == 2 else 3 - z
        return device(xx, yy, zz, core)

    near = tuple(over(link) for link in range(6))
    corner = tuple(over(link, (link + 1) % 6) for link in range(6))
    sides = (side0(x), side0(y), side0(z), side1(x), side1(y), side1(z))
    twin = device(x, y, z, 1 - core)
    far = device(x, lax.rem(y + 2, 4), z, core)

    def loads(m):
        return (
            pltpu.make_async_copy(q_hbm.at[m], qbuf.at[m], load_sem.at[m, 0]),
            pltpu.make_async_copy(g_hbm.at[0, m], gbuf.at[m], load_sem.at[m, 1]),
            pltpu.make_async_copy(e_hbm.at[0, m], ebuf.at[m], load_sem.at[m, 2]),
        )

    def begin(m, _):
        for copy in loads(m):
            copy.start()
        return 0

    lax.fori_loop(0, MATS, begin, 0)
    barrier = pltpu.get_barrier_semaphore()
    everyone = near + corner + (twin, far)
    for other in everyone:
        pl.semaphore_signal(barrier, inc=1, device_id=other, device_id_type=MESH)

    sent = []

    def remote(src, dst, send, arrive, target):
        copy = pltpu.make_async_remote_copy(
            src_ref=src, dst_ref=dst, send_sem=send, recv_sem=arrive,
            device_id=target, device_id_type=MESH,
        )
        copy.start()
        sent.append(copy)
        return copy

    mine = pl.multiple_of(core * HALF, 8)
    theirs = pl.multiple_of((1 - core) * HALF, 8)
    qst[...] = jnp.zeros_like(qst)
    q_acc[...] = jnp.zeros_like(q_acc)

    def arrive(m):
        for copy in loads(m):
            copy.wait()

    def merge(m):
        for r in range(0, ROWS, 32):
            rows = slice(r, r + 32)
            merged = gbuf[m, rows].astype(f32) + ebuf[m, rows]
            ebuf[m, rows] = merged
            hi, lo = split(merged)
            mh[m, rows] = hi
            ml[m, rows] = lo
        b = m % 2
        hi, lo = split(qbuf[m])
        qst[b, 64 * b : 64 * b + 64] = hi
        qst[b, 128 + 64 * b : 192 + 64 * b] = lo

    def local_p(j):
        if j == 0:
            arrive(0)
            merge(0)
        total = None
        for m in (2 * j, 2 * j + 1):
            if m + 1 < MATS:
                arrive(m + 1)
            wide = dot_nt(mh[m], qst[m % 2])
            part = wide[:, :128] + wide[:, 128:] + dot_nt(ml[m], qst[m % 2, :128])
            if m + 1 < MATS:
                merge(m + 1)
            total = part if total is None else total + part
        p_own[j] = total

    def p_copy(s, j):
        if s == 0:
            src, dst, target = p_own.at[j, pl.ds(theirs, HALF)], p_recv.at[j], twin
        elif s == 1:
            src, dst, target = p_chip.at[j], p_far.at[j], far
        else:
            src = dst = p_out.at[j, pl.ds(mine, HALF)]
            target = twin
        return pltpu.make_async_remote_copy(
            src_ref=src, dst_ref=dst, send_sem=p_send.at[s, j], recv_sem=p_arrive.at[s, j],
            device_id=target, device_id_type=MESH,
        )

    def p_step(s, j):
        if s > 0:
            p_copy(s - 1, j).wait_recv()
        if s == 1:
            p_chip[j] = p_own[j, pl.ds(mine, HALF)] + p_recv[j]
        if s == 2:
            p_out[j, pl.ds(mine, HALF)] = (p_chip[j] + p_far[j]) * 0.25
        if s < 3:
            p_copy(s, j).start()

    halves = {}

    def three(src, dst, send, arrive, link):
        targets = (near[(link + 1) % 6], near[link], corner[link])
        return [remote(src(f), dst.at[f], send.at[f], arrive.at[f], targets[f]) for f in range(3)]

    def gram_chain(j):
        halves[j] = hi, lo = split(p_out[j].T)
        square = dot_nt(hi, hi) + (dot_nt(hi, lo) + dot_nt(lo, hi))
        lane = lax.broadcasted_iota(jnp.int32, (R, 2 * R), 1)
        gram_own[j] = jnp.where(lane < 64, square[:64], square[64:])
        rows = pl.ds(pl.multiple_of(core * 32, 32), 32)
        gram_half[j, 0] = gram_own[j, rows]
        for s, link in enumerate((2, 5) if j % 2 == 0 else (5, 2)):
            copies = three(
                lambda f: gram_half.at[j, s], gram_recv.at[j, s], gram_send.at[j, s], gram_arrive.at[j, s], link,
            )
            yield
            for copy in copies:
                copy.wait_recv()
            got = gram_recv.at[j, s]
            gram_half[j, s + 1] = (gram_half[j, s] + got[1]) + (got[0] + got[2])
        copy = remote(
            gram_half.at[j, 2], gram_recv.at[j, 2, 0], gram_send.at[j, 2, 0], gram_arrive.at[j, 2, 0], near[1],
        )
        yield
        copy.wait_recv()
        gram_out[j, rows] = gram_half[j, 2] + gram_recv[j, 2, 0]
        part = gram_out.at[j, rows]
        copy = remote(part, part, gram_send.at[j, 2, 1], gram_arrive.at[j, 2, 1], twin)
        yield
        copy.wait_recv()

    def local_g(m):
        j, b = divmod(m, 2)
        hi, lo = halves[j]
        top = hi[64 * b : 64 * b + 64]
        both = jnp.concatenate([top, lo[64 * b : 64 * b + 64]], axis=0)
        for start, size in COLS:
            cols = slice(start, start + size)
            wide = dot(both, mh[m, :, cols])
            g_acc[m, :, cols] = wide[:64] + wide[64:] + dot(top, ml[m, :, cols])

    def g_chain(m):
        link = [(FIRST_LINK[m] + s) % 6 for s in range(6)]
        keep = pl.multiple_of(core * 32, 32)
        give = pl.multiple_of((1 - core) * 32, 32)
        kept0 = pl.multiple_of(core * 32 + 16 * sides[link[0]], 16)
        gone0 = pl.multiple_of(core * 32 + 16 - 16 * sides[link[0]], 16)
        kept1 = pl.multiple_of(kept0 + 8 * sides[link[1]], 8)
        gone1 = pl.multiple_of(kept0 + 8 - 8 * sides[link[1]], 8)
        hi, lo = sides[link[2]], sides[link[3]]

        def block(h, l):
            return pl.ds(pl.multiple_of((2 * h + l) * BLOCK, 128), BLOCK)

        own = block(hi, lo)
        others = (block(hi, 1 - lo), block(1 - hi, lo), block(1 - hi, 1 - lo))

        def send(s, src, dst, i):
            return remote(src, dst, a_send.at[s, m], a_arrive.at[s, m], near[link[i]])

        def forward(i, row, size):
            part = g_sum.at[m, pl.ds(row, size), pl.ds(0, D)]
            return remote(part, part, c_send.at[i, m], c_arrive.at[i, m], twin)

        copy = remote(g_acc.at[m, pl.ds(give, 32)], core_recv.at[m], c_send.at[0, m], c_arrive.at[0, m], twin)
        yield
        copy.wait_recv()
        g_acc[m, pl.ds(keep, 32)] += core_recv[m]
        copy = send(0, g_acc.at[m, pl.ds(gone0, 16)], recv0.at[m], 0)
        yield
        copy.wait_recv()
        g_acc[m, pl.ds(kept0, 16)] += recv0[m]
        copy = send(1, g_acc.at[m, pl.ds(gone1, 8)], recv1.at[m], 1)
        yield
        copy.wait_recv()
        q_acc[m, :, :D] = g_acc[m, pl.ds(kept1, 8)] + recv1[m]
        copies = three(lambda f: q_acc.at[m, :, others[f]], recv2.at[m], b_send.at[0, m], b_arrive.at[0, m], link[2])
        yield
        for copy in copies:
            copy.wait_recv()
        x_acc[m] = (q_acc[m, :, own] + recv2[m, 1]) + (recv2[m, 0] + recv2[m, 2])
        copies = three(lambda f: x_acc.at[m], recv3.at[m], b_send.at[1, m], b_arrive.at[1, m], link[4])
        yield
        for copy in copies:
            copy.wait_recv()
        g_sum[m, pl.ds(kept1, 8), own] = (x_acc[m] + recv3[m, 1]) + (recv3[m, 0] + recv3[m, 2])
        part = g_sum.at[m, pl.ds(kept1, 8), own]
        targets = (near[link[3]], near[link[2]], corner[link[2]])
        copies = [remote(part, part, b_send.at[2, m, f], b_arrive.at[2, m, f], targets[f]) for f in range(3)]
        yield
        for copy in copies:
            copy.wait_recv()
        part = g_sum.at[m, pl.ds(kept1, 8), pl.ds(0, D)]
        copy = send(2, part, part, 1)
        passed = [forward(1, kept1, 8)]
        yield
        copy.wait_recv()
        part = g_sum.at[m, pl.ds(kept0, 16), pl.ds(0, D)]
        copy = send(3, part, part, 0)
        passed.append(forward(2, gone1, 8))
        yield
        copy.wait_recv()
        passed.append(forward(3, gone0, 16))
        yield
        for copy in passed:
            copy.wait_recv()

    gc = [gram_chain(j) for j in range(3)]
    ac = [g_chain(m) for m in range(MATS)]
    factor = None

    p_stage = [0, 0, 0]
    for what, i in ORDER:
        if what == "products":
            local_p(i)
            if i == 0:
                pl.semaphore_wait(barrier, len(everyone))
        elif what == "p":
            p_step(p_stage[i], i)
            p_stage[i] += 1
        elif what == "gram":
            next(gc[i], None)
        elif what == "terms":
            local_g(i)
        elif what == "sum":
            next(ac[i], None)
        else:
            if factor is None:
                factor = eliminate([gram_out[j] for j in range(3)], y_out, p_out, lhs_err, lhs_q)
            for _ in range(i):
                next(factor, None)
    for _ in factor:
        pass
    for s in range(3):
        for j in range(3):
            p_copy(s, j).wait_send()
    for copy in sent:
        copy.wait_send()


def finish_kernel(g_sum, lhs_err, lhs_q, m_ref, err_hbm, q_out, ebuf, new_q, wst, store_sem, q_sem):
    stores = []
    for m in range(MATS):
        gh, gl = split(g_sum[m, :, :D] * 0.25)
        wst[0, 0:64] = gh
        wst[0, 64:128] = gh
        wst[0, 128:192] = gl
        fresh = dot(lhs_q[m, :, :192], wst[0])
        new_q[m] = fresh
        store = pltpu.make_async_copy(new_q.at[m], q_out.at[m], q_sem.at[m])
        store.start()
        stores.append(store)
        nh, nl = split(fresh)
        wst[1, 0:64] = nh
        wst[1, 64:128] = nh
        wst[1, 128:192] = nl
        for i, (start, size) in enumerate(COLS):
            cols = slice(start, start + size)
            ebuf[m, :, cols] = m_ref[m, :, cols] - dot(lhs_err[m, :, :192], wst[1, :, cols])
            place = pl.ds(start, size)
            store = pltpu.make_async_copy(
                ebuf.at[m, :, place], err_hbm.at[0, m, :, place], store_sem.at[m, i]
            )
            store.start()
            stores.append(store)
    for store in stores:
        store.wait()


def body(gradients, errors, previous_q):
    vmem = pl.BlockSpec(memory_space=pltpu.VMEM)
    far_hbm = pl.BlockSpec(memory_space=pltpu.HBM)
    sem = pltpu.SemaphoreType.DMA
    g_sum, lhs_err, lhs_q, merged = pl.pallas_call(
        comm_kernel,
        out_shape=(
            jax.ShapeDtypeStruct((MATS, R, 4 * BLOCK), f32),
            jax.ShapeDtypeStruct((MATS, ROWS, 256), bf16),
            jax.ShapeDtypeStruct((MATS, R, 256), bf16),
            jax.ShapeDtypeStruct((MATS, ROWS, D), f32),
        ),
        in_specs=[far_hbm, far_hbm, far_hbm],
        out_specs=(vmem, vmem, vmem, vmem),
        scratch_shapes=[
            pltpu.VMEM((MATS // 2, ROWS, 2 * R), f32),
            pltpu.VMEM((8 * R, 2 * R), f32),
            pltpu.VMEM((MATS, ROWS, D), bf16),
            pltpu.VMEM((MATS, R, D), f32),
            pltpu.VMEM((MATS, ROWS, D), bf16),
            pltpu.VMEM((MATS, ROWS, D), bf16),
            pltpu.VMEM((2, 256, D), bf16),
            pltpu.VMEM((MATS // 2, ROWS, 128), f32),
            pltpu.VMEM((MATS // 2, HALF, 128), f32),
            pltpu.VMEM((MATS // 2, HALF, 128), f32),
            pltpu.VMEM((MATS // 2, HALF, 128), f32),
            pltpu.VMEM((MATS, R, D), f32),
            pltpu.VMEM((MATS, 32, D), f32),
            pltpu.VMEM((MATS, 16, D), f32),
            pltpu.VMEM((MATS, 8, D), f32),
            pltpu.VMEM((MATS, 8, 4 * BLOCK), f32),
            pltpu.VMEM((MATS, 8, BLOCK), f32),
            pltpu.VMEM((MATS, 3, 8, BLOCK), f32),
            pltpu.VMEM((MATS, 3, 8, BLOCK), f32),
            pltpu.VMEM((MATS // 2, R, 2 * R), f32),
            pltpu.VMEM((MATS // 2, 3, R // 2, 2 * R), f32),
            pltpu.VMEM((MATS // 2, 3, 3, R // 2, 2 * R), f32),
            pltpu.VMEM((MATS // 2, R, 2 * R), f32),
            sem((MATS, 3)),
            sem((3, 3)),
            sem((3, 3)),
            sem((4, MATS)),
            sem((4, MATS)),
            sem((4, MATS)),
            sem((4, MATS)),
            sem((3, MATS, 3)),
            sem((3, MATS, 3)),
            sem((3, 3, 3)),
            sem((3, 3, 3)),
        ],
        compiler_params=pltpu.CompilerParams(
            collective_id=0, has_side_effects=True, vmem_limit_bytes=40 * 2**20
        ),
        name="compress_and_sum",
    )(*[pltpu.with_memory_space_constraint(v, pltpu.HBM) for v in (gradients, errors, previous_q)])
    return pl.pallas_call(
        finish_kernel,
        out_shape=(
            jax.ShapeDtypeStruct((1, MATS, ROWS, D), f32),
            jax.ShapeDtypeStruct((MATS, R, D), f32),
        ),
        in_specs=[vmem, vmem, vmem, vmem],
        out_specs=(far_hbm, far_hbm),
        scratch_shapes=[
            pltpu.VMEM((MATS, ROWS, D), f32),
            pltpu.VMEM((MATS, R, D), f32),
            pltpu.VMEM((2, ROWS, D), bf16),
            sem((MATS, 3)),
            sem((MATS,)),
        ],
        compiler_params=pltpu.CompilerParams(vmem_limit_bytes=24 * 2**20),
        name="new_q_and_errors",
    )(g_sum, lhs_err, lhs_q, merged)


def solution(mesh):
    in_specs = (P("dp", None, "mp", None), P("dp", None, "mp", None), P())
    out_specs = (P("dp", None, "mp", None), P())
    return jax.shard_map(body, mesh=mesh, in_specs=in_specs, out_specs=out_specs, check_vma=False)
```

```python
import functools

import jax
import jax.numpy as jnp
from jax import lax
from jax.experimental import pallas as pl
from jax.experimental.pallas import tpu as pltpu
from jax.sharding import PartitionSpec as P

MESH = pl.DeviceIdType.MESH
MATS, ROWS, D, R = 6, 192, 1408, 64
HALF = ROWS // 2
BLOCK = 384
COLS = ((0, 512), (512, 512), (1024, 384))
f32, bf16 = jnp.float32, jnp.bfloat16
LINKS = (
    (0, 1, 3, 2, 4, 5),
    (1, 2, 4, 0, 5, 3),
    (2, 0, 1, 5, 3, 4),
    (0, 1, 4, 3, 2, 5),
    (1, 2, 0, 4, 5, 3),
    (2, 0, 1, 5, 4, 3),
)
PAIRS = tuple(sorted({tuple(sorted(links[i : i + 2])) for links in LINKS for i in (2, 4)}))
ORDER = (
    ("products", 0), ("p", 0), ("products", 1), ("p", 1), ("p", 0), ("products", 2), ("p", 2), ("p", 1),
    ("p", 2), ("p", 0), ("p", 0), ("terms", 0), ("sum", 0), ("terms", 1), ("p", 1), ("sum", 1), ("gram", 0),
    ("sum", 0), ("p", 1), ("terms", 2), ("sum", 2), ("sum", 1), ("terms", 3), ("p", 2), ("sum", 3),
    ("gram", 1), ("sum", 2), ("gram", 0), ("p", 2), ("terms", 4), ("sum", 4), ("sum", 3), ("sum", 0),
    ("terms", 5), ("sum", 5), ("gram", 2), ("sum", 4), ("sum", 1), ("gram", 1), ("sum", 5), ("sum", 2),
    ("gram", 0), ("sum", 0), ("gram", 2), ("sum", 3), ("sum", 1), ("gram", 1), ("sum", 2), ("sum", 4),
    ("gram", 0), ("gram", 2), ("sum", 5), ("sum", 3), ("sum", 0), ("gram", 1), ("sum", 1), ("sum", 2),
    ("sum", 4), ("sum", 5), ("gram", 2), ("gram", 0), ("gram", 1), ("sum", 3), ("sum", 0), ("sum", 4),
    ("sum", 1), ("gram", 1), ("gram", 0), ("sum", 2), ("sum", 5), ("gram", 1), ("gram", 2), ("gram", 0),
    ("sum", 3), ("sum", 0), ("sum", 1), ("sum", 4), ("sum", 2), ("sum", 5), ("gram", 2), ("sum", 0),
    ("sum", 3), ("gram", 2), ("factor", 2), ("sum", 4), ("sum", 1), ("sum", 2), ("factor", 2), ("sum", 5),
    ("factor", 2), ("sum", 3), ("factor", 2), ("sum", 4), ("sum", 0), ("factor", 2), ("sum", 5), ("sum", 1),
    ("sum", 0), ("factor", 2), ("sum", 2), ("sum", 1), ("factor", 2), ("sum", 2), ("factor", 2),
    ("factor", 1), ("factor", 1), ("factor", 1), ("sum", 3), ("sum", 4), ("sum", 5), ("sum", 3), ("sum", 4),
    ("sum", 5),
)
NT = (((1,), (1,)), ((), ()))


def dot(a, b):
    return jnp.dot(a, b, preferred_element_type=f32)


def dot_nt(a, b):
    return lax.dot_general(a, b, NT, preferred_element_type=f32)


def split(x):
    hi = x.astype(bf16)
    return hi, (x - hi.astype(f32)).astype(bf16)


def eliminate(grams, y_ref, p_ref, lhs_err, lhs_q):
    row = lax.broadcasted_iota(jnp.int32, (R, 2 * R), 0)
    lane = lax.broadcasted_iota(jnp.int32, (R, 2 * R), 1)
    eye = jnp.where(lane == row + 64, 1.0, 0.0)
    unit = jnp.where(lane == row, 1.0, 0.0)
    for m in range(8):
        if m < MATS:
            gram = grams[m // 2]
            gram = pltpu.roll(gram, 64, axis=1) if m % 2 else gram
        else:
            gram = unit
        y_ref[pl.ds(m, R, stride=8), :] = jnp.where(lane < 64, gram, eye)
    rows = [y_ref[8 * i : 8 * i + 8] for i in range(R)]

    def at(r, k):
        return jnp.broadcast_to(r[:, k : k + 1], (8, 128))

    for k in range(0, R, 4):
        r0, r1, r2, r3 = rows[k : k + 4]
        s00, s01, s02, s03 = (at(r0, k + i) for i in range(4))
        s11, s12, s13 = (at(r1, k + i) for i in range(1, 4))
        s22, s23, s33 = at(r2, k + 2), at(r2, k + 3), at(r3, k + 3)
        i0 = 1.0 / s00
        l10, l20, l30 = s01 * i0, s02 * i0, s03 * i0
        d1 = s11 - l10 * s01
        t12, t13 = s12 - l10 * s02, s13 - l10 * s03
        i1 = 1.0 / d1
        l21, l31 = t12 * i1, t13 * i1
        d2 = s22 - l20 * s02 - l21 * t12
        t23 = s23 - l20 * s03 - l21 * t13
        i2 = 1.0 / d2
        l32 = t23 * i2
        d3 = s33 - l30 * s03 - l31 * t13 - l32 * t23
        i3 = 1.0 / d3
        r1 = r1 - l10 * r0
        r2 = r2 - l20 * r0 - l21 * r1
        r3 = r3 - l30 * r0 - l31 * r1 - l32 * r2
        q0, q1, q2, q3 = r0 * i0, r1 * i1, r2 * i2, r3 * i3
        for i in range(k + 4, R):
            if i < k + 8:
                c0, c1, c2, c3 = (at(rows[i], k + j) for j in range(4))
                c1 = c1 - l10 * c0
                c2 = c2 - l20 * c0 - l21 * c1
                c3 = c3 - l30 * c0 - l31 * c1 - l32 * c2
            else:
                c0, c1, c2, c3 = at(r0, i), at(r1, i), at(r2, i), at(r3, i)
            rows[i] = rows[i] - (c0 * q0 + c1 * q1) - (c2 * q2 + c3 * q3)
        for i, (r, d) in enumerate(((r0, s00), (r1, d1), (r2, d2), (r3, d3))):
            y_ref[8 * (k + i) : 8 * (k + i) + 8] = r * (1.0 / jnp.sqrt(d))
        yield
    wide_lane = lax.broadcasted_iota(jnp.int32, (ROWS, 2 * R), 1)
    for m in range(MATS):
        side = jnp.where(lane >= 64, y_ref[pl.ds(m, R, stride=8), :], 0.0)
        other = pltpu.roll(side, 64, axis=1)
        inverse = side if m % 2 else other
        bh, bl = split(jnp.concatenate([inverse, inverse], axis=0))
        ph, pl_ = split(p_ref[m // 2])
        ortho = dot_nt(ph, bh) + (dot_nt(ph, bl) + dot_nt(pl_, bh))
        oh, ol = split(ortho)
        lhs_err[m] = jnp.concatenate([jnp.where(wide_lane < 64, oh, ol), oh], axis=1)
        lh, ll = split(side + other)
        lhs_q[m] = jnp.concatenate([jnp.where(lane < 64, lh, ll), lh], axis=1)
        if m % 2:
            yield


def comm_kernel(
    g_hbm, e_hbm, q_hbm, g_sum, lhs_err, lhs_q, ebuf,
    p_out, y_out, gbuf, qbuf, mh, ml, qst, p_own, p_recv, p_chip, p_far, g_acc,
    core_recv, recv0, recv1, q_acc, x_acc, recv2, recv3, gram_own, gram_half, gram_recv, gram_out,
    load_sem, p_send, p_arrive, c_send, c_arrive, a_send, a_arrive, b_send, b_arrive,
    gram_send, gram_arrive,
):
    dp, mp = lax.axis_index("dp"), lax.axis_index("mp")
    y_hi, core = lax.div(dp, 2), lax.rem(dp, 2)
    x = lax.rem(mp, 4)
    z = lax.rem(lax.div(mp, 4), 4)
    y = y_hi * 2 + lax.div(mp, 16)

    def device(xx, yy, zz, cc):
        return (lax.div(yy, 2) * 2 + cc, lax.rem(yy, 2) * 16 + zz * 4 + xx)

    def flip(v):
        return v + 1 - 2 * lax.rem(v, 2)

    sides = (lax.rem(x, 2), lax.rem(y, 2), lax.rem(z, 2), lax.div(x, 2), lax.div(y, 2), lax.div(z, 2))

    def across(v):
        return lax.rem(v + 2, 4)

    def over(*links):
        xx, yy, zz = x, y, z
        for link in links:
            if link % 3 == 0:
                xx = flip(xx) if link == 0 else across(xx)
            elif link % 3 == 1:
                yy = flip(yy) if link == 1 else across(yy)
            else:
                zz = flip(zz) if link == 2 else across(zz)
        return device(xx, yy, zz, core)

    near = tuple(over(link) for link in range(6))
    corner = {pair: over(*pair) for pair in PAIRS}
    twin = device(x, y, z, 1 - core)
    far = near[4]

    def loads(m):
        return (
            pltpu.make_async_copy(q_hbm.at[m], qbuf.at[m], load_sem.at[m, 0]),
            pltpu.make_async_copy(g_hbm.at[0, m], gbuf.at[m], load_sem.at[m, 1]),
            pltpu.make_async_copy(e_hbm.at[0, m], ebuf.at[m], load_sem.at[m, 2]),
        )

    def begin(m, _):
        for copy in loads(m):
            copy.start()
        return 0

    lax.fori_loop(0, MATS, begin, 0)
    barrier = pltpu.get_barrier_semaphore()
    everyone = near + tuple(corner.values()) + (twin,)
    for other in everyone:
        pl.semaphore_signal(barrier, inc=1, device_id=other, device_id_type=MESH)

    sent = []

    def remote(src, dst, send, arrive, target):
        copy = pltpu.make_async_remote_copy(
            src_ref=src, dst_ref=dst, send_sem=send, recv_sem=arrive,
            device_id=target, device_id_type=MESH,
        )
        copy.start()
        sent.append(copy)
        return copy

    mine = pl.multiple_of(core * HALF, 8)
    theirs = pl.multiple_of((1 - core) * HALF, 8)
    qst[...] = jnp.zeros_like(qst)
    q_acc[...] = jnp.zeros_like(q_acc)

    def arrive(m):
        for copy in loads(m):
            copy.wait()

    def merge(m):
        for r in range(0, ROWS, 32):
            rows = slice(r, r + 32)
            merged = gbuf[m, rows].astype(f32) + ebuf[m, rows]
            ebuf[m, rows] = merged
            hi, lo = split(merged)
            mh[m, rows] = hi
            ml[m, rows] = lo
        b = m % 2
        hi, lo = split(qbuf[m])
        qst[b, 64 * b : 64 * b + 64] = hi
        qst[b, 128 + 64 * b : 192 + 64 * b] = lo

    def local_p(j):
        if j == 0:
            arrive(0)
            merge(0)
        total = None
        for m in (2 * j, 2 * j + 1):
            if m + 1 < MATS:
                arrive(m + 1)
            wide = dot_nt(mh[m], qst[m % 2])
            part = wide[:, :128] + wide[:, 128:] + dot_nt(ml[m], qst[m % 2, :128])
            if m + 1 < MATS:
                merge(m + 1)
            total = part if total is None else total + part
        p_own[j] = total

    def p_copy(s, j):
        if s == 0:
            src, dst, target = p_own.at[j, pl.ds(theirs, HALF)], p_recv.at[j], twin
        elif s == 1:
            src, dst, target = p_chip.at[j], p_far.at[j], far
        else:
            src = dst = p_out.at[j, pl.ds(mine, HALF)]
            target = twin
        return pltpu.make_async_remote_copy(
            src_ref=src, dst_ref=dst, send_sem=p_send.at[s, j], recv_sem=p_arrive.at[s, j],
            device_id=target, device_id_type=MESH,
        )

    def p_step(s, j):
        if s > 0:
            p_copy(s - 1, j).wait_recv()
        if s == 1:
            p_chip[j] = p_own[j, pl.ds(mine, HALF)] + p_recv[j]
        if s == 2:
            p_out[j, pl.ds(mine, HALF)] = (p_chip[j] + p_far[j]) * 0.25
        if s < 3:
            p_copy(s, j).start()

    halves = {}

    def transposed(j):
        if j not in halves:
            halves[j] = split(p_out[j].T)
        return halves[j]

    def three(src, dst, send, arrive, a, b):
        targets = (near[b], near[a], corner[min(a, b), max(a, b)])
        return [remote(src(f), dst(f), send.at[f], arrive.at[f], targets[f]) for f in range(3)]

    def gram_chain(j):
        hi, lo = transposed(j)
        square = dot_nt(hi, hi) + (dot_nt(hi, lo) + dot_nt(lo, hi))
        lane = lax.broadcasted_iota(jnp.int32, (R, 2 * R), 1)
        gram_own[j] = jnp.where(lane < 64, square[:64], square[64:])
        rows = pl.ds(pl.multiple_of(core * 32, 32), 32)
        gram_half[j, 0] = gram_own[j, rows]
        order = (0, 2, 3, 5, 1)
        for s in range(5):
            copy = remote(
                gram_half.at[j, s], gram_recv.at[j, s], gram_send.at[j, s], gram_arrive.at[j, s],
                near[order[(s + 2 * j) % 5]],
            )
            yield
            copy.wait_recv()
            total = gram_half[j, s] + gram_recv[j, s]
            if s < 4:
                gram_half[j, s + 1] = total
        gram_out[j, rows] = total
        part = gram_out.at[j, rows]
        copy = remote(part, part, gram_send.at[j, 5], gram_arrive.at[j, 5], twin)
        yield
        copy.wait_recv()

    def local_g(m):
        j, b = divmod(m, 2)
        hi, lo = transposed(j)
        top = hi[64 * b : 64 * b + 64]
        both = jnp.concatenate([top, lo[64 * b : 64 * b + 64]], axis=0)
        for start, size in COLS:
            cols = slice(start, start + size)
            wide = dot(both, mh[m, :, cols])
            g_acc[m, :, cols] = wide[:64] + wide[64:] + dot(top, ml[m, :, cols])

    def g_chain(m):
        link = LINKS[m]
        keep = pl.multiple_of(core * 32, 32)
        give = pl.multiple_of((1 - core) * 32, 32)
        kept0 = pl.multiple_of(core * 32 + 16 * sides[link[0]], 16)
        gone0 = pl.multiple_of(core * 32 + 16 - 16 * sides[link[0]], 16)
        kept1 = pl.multiple_of(kept0 + 8 * sides[link[1]], 8)
        gone1 = pl.multiple_of(kept0 + 8 - 8 * sides[link[1]], 8)
        hi, lo = sides[link[2]], sides[link[3]]

        def block(h, l):
            return pl.ds(pl.multiple_of((2 * h + l) * BLOCK, 128), BLOCK)

        own = block(hi, lo)
        others = (block(hi, 1 - lo), block(1 - hi, lo), block(1 - hi, 1 - lo))

        def send(s, src, dst, i):
            return remote(src, dst, a_send.at[s, m], a_arrive.at[s, m], near[link[i]])

        def forward(i, row, size):
            part = g_sum.at[m, pl.ds(row, size), pl.ds(0, D)]
            return remote(part, part, c_send.at[i, m], c_arrive.at[i, m], twin)

        copy = remote(g_acc.at[m, pl.ds(give, 32)], core_recv.at[m], c_send.at[0, m], c_arrive.at[0, m], twin)
        yield
        copy.wait_recv()
        g_acc[m, pl.ds(keep, 32)] += core_recv[m]
        copy = send(0, g_acc.at[m, pl.ds(gone0, 16)], recv0.at[m], 0)
        yield
        copy.wait_recv()
        g_acc[m, pl.ds(kept0, 16)] += recv0[m]
        copy = send(1, g_acc.at[m, pl.ds(gone1, 8)], recv1.at[m], 1)
        yield
        copy.wait_recv()
        q_acc[m, :, :D] = g_acc[m, pl.ds(kept1, 8)] + recv1[m]
        copies = three(
            lambda f: q_acc.at[m, :, others[f]], lambda f: recv2.at[m, f], b_send.at[0, m], b_arrive.at[0, m],
            link[2], link[3],
        )
        yield
        for copy in copies:
            copy.wait_recv()
        x_acc[m] = (q_acc[m, :, own] + recv2[m, 1]) + (recv2[m, 0] + recv2[m, 2])
        copies = three(
            lambda f: x_acc.at[m], lambda f: recv3.at[m, f], b_send.at[1, m], b_arrive.at[1, m], link[4], link[5],
        )
        yield
        for copy in copies:
            copy.wait_recv()
        g_sum[m, pl.ds(kept1, 8), own] = (x_acc[m] + recv3[m, 1]) + (recv3[m, 0] + recv3[m, 2])
        part = g_sum.at[m, pl.ds(kept1, 8), own]
        copies = three(lambda f: part, lambda f: part, b_send.at[2, m], b_arrive.at[2, m], link[2], link[3])
        yield
        for copy in copies:
            copy.wait_recv()
        part = g_sum.at[m, pl.ds(kept1, 8), pl.ds(0, D)]
        copy = send(2, part, part, 1)
        passed = [forward(1, kept1, 8)]
        yield
        copy.wait_recv()
        part = g_sum.at[m, pl.ds(kept0, 16), pl.ds(0, D)]
        copy = send(3, part, part, 0)
        passed.append(forward(2, gone1, 8))
        yield
        copy.wait_recv()
        passed.append(forward(3, gone0, 16))
        yield
        for copy in passed:
            copy.wait_recv()

    gc = [gram_chain(j) for j in range(3)]
    ac = [g_chain(m) for m in range(MATS)]
    factor = None

    p_stage = [0, 0, 0]
    for what, i in ORDER:
        if what == "products":
            local_p(i)
            if i == 0:
                pl.semaphore_wait(barrier, len(everyone))
        elif what == "p":
            p_step(p_stage[i], i)
            p_stage[i] += 1
        elif what == "gram":
            next(gc[i], None)
        elif what == "terms":
            local_g(i)
        elif what == "sum":
            next(ac[i], None)
        else:
            if factor is None:
                factor = eliminate([gram_out[j] for j in range(3)], y_out, p_out, lhs_err, lhs_q)
            for _ in range(i):
                next(factor, None)
    for _ in factor:
        pass
    for s in range(3):
        for j in range(3):
            p_copy(s, j).wait_send()
    for copy in sent:
        copy.wait_send()


def finish_kernel(g_sum, lhs_err, lhs_q, m_ref, err_hbm, q_out, ebuf, new_q, wst, store_sem, q_sem):
    stores = []
    for m in range(MATS):
        gh, gl = split(g_sum[m, :, :D] * 0.25)
        wst[0, 0:64] = gh
        wst[0, 64:128] = gh
        wst[0, 128:192] = gl
        fresh = dot(lhs_q[m, :, :192], wst[0])
        new_q[m] = fresh
        store = pltpu.make_async_copy(new_q.at[m], q_out.at[m], q_sem.at[m])
        store.start()
        stores.append(store)
        nh, nl = split(fresh)
        wst[1, 0:64] = nh
        wst[1, 64:128] = nh
        wst[1, 128:192] = nl
        for i, (start, size) in enumerate(COLS):
            cols = slice(start, start + size)
            ebuf[m, :, cols] = m_ref[m, :, cols] - dot(lhs_err[m, :, :192], wst[1, :, cols])
            place = pl.ds(start, size)
            store = pltpu.make_async_copy(
                ebuf.at[m, :, place], err_hbm.at[0, m, :, place], store_sem.at[m, i]
            )
            store.start()
            stores.append(store)
    for store in stores:
        store.wait()


def body(gradients, errors, previous_q):
    vmem = pl.BlockSpec(memory_space=pltpu.VMEM)
    far_hbm = pl.BlockSpec(memory_space=pltpu.HBM)
    sem = pltpu.SemaphoreType.DMA
    g_sum, lhs_err, lhs_q, merged = pl.pallas_call(
        comm_kernel,
        out_shape=(
            jax.ShapeDtypeStruct((MATS, R, 4 * BLOCK), f32),
            jax.ShapeDtypeStruct((MATS, ROWS, 256), bf16),
            jax.ShapeDtypeStruct((MATS, R, 256), bf16),
            jax.ShapeDtypeStruct((MATS, ROWS, D), f32),
        ),
        in_specs=[far_hbm, far_hbm, far_hbm],
        out_specs=(vmem, vmem, vmem, vmem),
        scratch_shapes=[
            pltpu.VMEM((MATS // 2, ROWS, 2 * R), f32),
            pltpu.VMEM((8 * R, 2 * R), f32),
            pltpu.VMEM((MATS, ROWS, D), bf16),
            pltpu.VMEM((MATS, R, D), f32),
            pltpu.VMEM((MATS, ROWS, D), bf16),
            pltpu.VMEM((MATS, ROWS, D), bf16),
            pltpu.VMEM((2, 256, D), bf16),
            pltpu.VMEM((MATS // 2, ROWS, 128), f32),
            pltpu.VMEM((MATS // 2, HALF, 128), f32),
            pltpu.VMEM((MATS // 2, HALF, 128), f32),
            pltpu.VMEM((MATS // 2, HALF, 128), f32),
            pltpu.VMEM((MATS, R, D), f32),
            pltpu.VMEM((MATS, 32, D), f32),
            pltpu.VMEM((MATS, 16, D), f32),
            pltpu.VMEM((MATS, 8, D), f32),
            pltpu.VMEM((MATS, 8, 4 * BLOCK), f32),
            pltpu.VMEM((MATS, 8, BLOCK), f32),
            pltpu.VMEM((MATS, 3, 8, BLOCK), f32),
            pltpu.VMEM((MATS, 3, 8, BLOCK), f32),
            pltpu.VMEM((MATS // 2, R, 2 * R), f32),
            pltpu.VMEM((MATS // 2, 5, R // 2, 2 * R), f32),
            pltpu.VMEM((MATS // 2, 5, R // 2, 2 * R), f32),
            pltpu.VMEM((MATS // 2, R, 2 * R), f32),
            sem((MATS, 3)),
            sem((3, 3)),
            sem((3, 3)),
            sem((4, MATS)),
            sem((4, MATS)),
            sem((4, MATS)),
            sem((4, MATS)),
            sem((3, MATS, 3)),
            sem((3, MATS, 3)),
            sem((3, 6)),
            sem((3, 6)),
        ],
        compiler_params=pltpu.CompilerParams(
            collective_id=0, has_side_effects=True, vmem_limit_bytes=40 * 2**20
        ),
        name="compress_and_sum",
    )(*[pltpu.with_memory_space_constraint(v, pltpu.HBM) for v in (gradients, errors, previous_q)])
    return pl.pallas_call(
        finish_kernel,
        out_shape=(
            jax.ShapeDtypeStruct((1, MATS, ROWS, D), f32),
            jax.ShapeDtypeStruct((MATS, R, D), f32),
        ),
        in_specs=[vmem, vmem, vmem, vmem],
        out_specs=(far_hbm, far_hbm),
        scratch_shapes=[
            pltpu.VMEM((MATS, ROWS, D), f32),
            pltpu.VMEM((MATS, R, D), f32),
            pltpu.VMEM((2, ROWS, D), bf16),
            sem((MATS, 3)),
            sem((MATS,)),
        ],
        compiler_params=pltpu.CompilerParams(vmem_limit_bytes=24 * 2**20),
        name="new_q_and_errors",
    )(g_sum, lhs_err, lhs_q, merged)


def solution(mesh):
    in_specs = (P("dp", None, "mp", None), P("dp", None, "mp", None), P())
    out_specs = (P("dp", None, "mp", None), P())
    return jax.shard_map(body, mesh=mesh, in_specs=in_specs, out_specs=out_specs, check_vma=False)
```

```python
import functools

import jax
import jax.numpy as jnp
from jax import lax
from jax.experimental import pallas as pl
from jax.experimental.pallas import tpu as pltpu
from jax.sharding import PartitionSpec as P

MESH = pl.DeviceIdType.MESH
MATS, ROWS, D, R = 6, 192, 1408, 64
HALF = ROWS // 2
BLOCK = 384
COLS = ((0, 512), (512, 512), (1024, 384))
f32, bf16 = jnp.float32, jnp.bfloat16
LINKS = (
    (1, 2, 4, 3, 5, 0),
    (3, 4, 1, 2, 5, 0),
    (0, 5, 1, 2, 4, 3),
    (0, 5, 3, 4, 2, 1),
    (4, 3, 2, 1, 0, 5),
    (2, 1, 5, 0, 3, 4),
)
GRAM_PAIRS = ((2, 3), (5, 0))
PAIRS = tuple(sorted({tuple(sorted(links[i : i + 2])) for links in LINKS + GRAM_PAIRS for i in range(0, len(links), 2)}))
ORDER = (
    ("products", 0), ("p", 0), ("products", 1), ("p", 1), ("p", 0), ("products", 2), ("p", 2), ("p", 1),
    ("p", 2), ("p", 0), ("p", 0), ("terms", 0), ("p", 1), ("sum", 0), ("terms", 1), ("sum", 1), ("gram", 0),
    ("p", 1), ("terms", 2), ("p", 2), ("sum", 2), ("sum", 0), ("sum", 1), ("terms", 3), ("sum", 3),
    ("gram", 1), ("p", 2), ("terms", 4), ("sum", 4), ("sum", 2), ("terms", 5), ("sum", 5), ("sum", 3),
    ("gram", 2), ("gram", 0), ("sum", 4), ("sum", 5), ("sum", 0), ("gram", 1), ("sum", 1), ("gram", 2),
    ("sum", 2), ("sum", 5), ("sum", 4), ("sum", 3), ("sum", 0), ("sum", 1), ("gram", 0), ("gram", 1),
    ("sum", 2), ("gram", 2), ("sum", 4), ("sum", 5), ("gram", 0), ("sum", 3), ("gram", 1), ("sum", 0),
    ("gram", 2), ("sum", 1), ("gram", 0), ("sum", 2), ("gram", 1), ("gram", 2), ("factor", 1), ("factor", 1),
    ("sum", 4), ("sum", 3), ("sum", 5), ("factor", 1), ("sum", 0), ("sum", 1), ("sum", 2), ("factor", 1),
    ("factor", 1), ("factor", 1), ("sum", 4), ("factor", 1), ("sum", 3), ("sum", 5), ("factor", 1),
    ("factor", 1), ("sum", 0), ("factor", 1), ("factor", 1), ("sum", 1), ("sum", 2), ("sum", 0),
    ("factor", 1), ("factor", 1), ("sum", 1), ("factor", 1), ("sum", 4), ("sum", 5), ("sum", 2),
    ("factor", 1), ("sum", 3), ("factor", 1), ("factor", 1), ("factor", 1), ("factor", 1), ("sum", 4),
    ("sum", 5), ("sum", 3),
)
NT = (((1,), (1,)), ((), ()))


def dot(a, b):
    return jnp.dot(a, b, preferred_element_type=f32)


def dot_nt(a, b):
    return lax.dot_general(a, b, NT, preferred_element_type=f32)


def split(x):
    hi = x.astype(bf16)
    return hi, (x - hi.astype(f32)).astype(bf16)


def eliminate(grams, y_ref, p_ref, lhs_err, lhs_q):
    row = lax.broadcasted_iota(jnp.int32, (R, 2 * R), 0)
    lane = lax.broadcasted_iota(jnp.int32, (R, 2 * R), 1)
    eye = jnp.where(lane == row + 64, 1.0, 0.0)
    unit = jnp.where(lane == row, 1.0, 0.0)
    for m in range(8):
        if m < MATS:
            gram = grams[m // 2]
            gram = pltpu.roll(gram, 64, axis=1) if m % 2 else gram
        else:
            gram = unit
        y_ref[pl.ds(m, R, stride=8), :] = jnp.where(lane < 64, gram, eye)
    rows = [y_ref[8 * i : 8 * i + 8] for i in range(R)]

    def at(r, k):
        return jnp.broadcast_to(r[:, k : k + 1], (8, 128))

    for k in range(0, R, 4):
        r0, r1, r2, r3 = rows[k : k + 4]
        s00, s01, s02, s03 = (at(r0, k + i) for i in range(4))
        s11, s12, s13 = (at(r1, k + i) for i in range(1, 4))
        s22, s23, s33 = at(r2, k + 2), at(r2, k + 3), at(r3, k + 3)
        i0 = 1.0 / s00
        l10, l20, l30 = s01 * i0, s02 * i0, s03 * i0
        d1 = s11 - l10 * s01
        t12, t13 = s12 - l10 * s02, s13 - l10 * s03
        i1 = 1.0 / d1
        l21, l31 = t12 * i1, t13 * i1
        d2 = s22 - l20 * s02 - l21 * t12
        t23 = s23 - l20 * s03 - l21 * t13
        i2 = 1.0 / d2
        l32 = t23 * i2
        d3 = s33 - l30 * s03 - l31 * t13 - l32 * t23
        i3 = 1.0 / d3
        r1 = r1 - l10 * r0
        r2 = r2 - l20 * r0 - l21 * r1
        r3 = r3 - l30 * r0 - l31 * r1 - l32 * r2
        q0, q1, q2, q3 = r0 * i0, r1 * i1, r2 * i2, r3 * i3
        for i in range(k + 4, R):
            if i < k + 8:
                c0, c1, c2, c3 = (at(rows[i], k + j) for j in range(4))
                c1 = c1 - l10 * c0
                c2 = c2 - l20 * c0 - l21 * c1
                c3 = c3 - l30 * c0 - l31 * c1 - l32 * c2
            else:
                c0, c1, c2, c3 = at(r0, i), at(r1, i), at(r2, i), at(r3, i)
            rows[i] = rows[i] - (c0 * q0 + c1 * q1) - (c2 * q2 + c3 * q3)
        for i, (r, d) in enumerate(((r0, s00), (r1, d1), (r2, d2), (r3, d3))):
            y_ref[8 * (k + i) : 8 * (k + i) + 8] = r * (1.0 / jnp.sqrt(d))
        yield
    wide_lane = lax.broadcasted_iota(jnp.int32, (ROWS, 2 * R), 1)
    for m in range(MATS):
        side = jnp.where(lane >= 64, y_ref[pl.ds(m, R, stride=8), :], 0.0)
        other = pltpu.roll(side, 64, axis=1)
        inverse = side if m % 2 else other
        bh, bl = split(jnp.concatenate([inverse, inverse], axis=0))
        ph, pl_ = split(p_ref[m // 2])
        ortho = dot_nt(ph, bh) + (dot_nt(ph, bl) + dot_nt(pl_, bh))
        oh, ol = split(ortho)
        lhs_err[m] = jnp.concatenate([jnp.where(wide_lane < 64, oh, ol), oh], axis=1)
        lh, ll = split(side + other)
        lhs_q[m] = jnp.concatenate([jnp.where(lane < 64, lh, ll), lh], axis=1)
        if m % 2:
            yield


def comm_kernel(
    g_hbm, e_hbm, q_hbm, g_sum, lhs_err, lhs_q, ebuf,
    p_out, y_out, gbuf, qbuf, mh, ml, qst, p_own, p_recv, p_chip, p_far, g_acc,
    core_recv, recv1, q_acc, x_acc, recv2, recv3, gram_own, gram_half, gram_recv, gram_out,
    load_sem, p_send, p_arrive, c_send, c_arrive, a_send, a_arrive,
    gram_send, gram_arrive,
):
    dp, mp = lax.axis_index("dp"), lax.axis_index("mp")
    y_hi, core = lax.div(dp, 2), lax.rem(dp, 2)
    x = lax.rem(mp, 4)
    z = lax.rem(lax.div(mp, 4), 4)
    y = y_hi * 2 + lax.div(mp, 16)

    def device(xx, yy, zz, cc):
        return (lax.div(yy, 2) * 2 + cc, lax.rem(yy, 2) * 16 + zz * 4 + xx)

    def flip(v):
        return v + 1 - 2 * lax.rem(v, 2)

    def side0(v):
        hi = lax.div(v, 2)
        lo = lax.rem(v, 2)
        return hi + lo - 2 * hi * lo

    def side1(v):
        return lax.div(v, 2)

    def over(*links):
        xx, yy, zz = x, y, z
        for link in links:
            if link % 3 == 0:
                xx = flip(x) if link == 0 else 3 - x
            elif link % 3 == 1:
                yy = flip(y) if link == 1 else 3 - y
            else:
                zz = flip(z) if link == 2 else 3 - z
        return device(xx, yy, zz, core)

    near = tuple(over(link) for link in range(6))
    corner = {pair: over(*pair) for pair in PAIRS}
    sides = (side0(x), side0(y), side0(z), side1(x), side1(y), side1(z))
    twin = device(x, y, z, 1 - core)
    far = device(x, lax.rem(y + 2, 4), z, core)

    def loads(m):
        return (
            pltpu.make_async_copy(q_hbm.at[m], qbuf.at[m], load_sem.at[m, 0]),
            pltpu.make_async_copy(g_hbm.at[0, m], gbuf.at[m], load_sem.at[m, 1]),
            pltpu.make_async_copy(e_hbm.at[0, m], ebuf.at[m], load_sem.at[m, 2]),
        )

    def begin(m, _):
        for copy in loads(m):
            copy.start()
        return 0

    lax.fori_loop(0, MATS, begin, 0)
    barrier = pltpu.get_barrier_semaphore()
    everyone = near + tuple(corner.values()) + (twin, far)
    for other in everyone:
        pl.semaphore_signal(barrier, inc=1, device_id=other, device_id_type=MESH)

    sent = []

    def remote(src, dst, send, arrive, target):
        copy = pltpu.make_async_remote_copy(
            src_ref=src, dst_ref=dst, send_sem=send, recv_sem=arrive,
            device_id=target, device_id_type=MESH,
        )
        copy.start()
        sent.append(copy)
        return copy

    mine = pl.multiple_of(core * HALF, 8)
    theirs = pl.multiple_of((1 - core) * HALF, 8)
    qst[...] = jnp.zeros_like(qst)
    q_acc[...] = jnp.zeros_like(q_acc)

    def arrive(m):
        for copy in loads(m):
            copy.wait()

    def merge(m):
        for r in range(0, ROWS, 32):
            rows = slice(r, r + 32)
            merged = gbuf[m, rows].astype(f32) + ebuf[m, rows]
            ebuf[m, rows] = merged
            hi, lo = split(merged)
            mh[m, rows] = hi
            ml[m, rows] = lo
        b = m % 2
        hi, lo = split(qbuf[m])
        qst[b, 64 * b : 64 * b + 64] = hi
        qst[b, 128 + 64 * b : 192 + 64 * b] = lo

    def local_p(j):
        if j == 0:
            arrive(0)
            merge(0)
        total = None
        for m in (2 * j, 2 * j + 1):
            if m + 1 < MATS:
                arrive(m + 1)
            wide = dot_nt(mh[m], qst[m % 2])
            part = wide[:, :128] + wide[:, 128:] + dot_nt(ml[m], qst[m % 2, :128])
            if m + 1 < MATS:
                merge(m + 1)
            total = part if total is None else total + part
        p_own[j] = total

    def p_copy(s, j):
        if s == 0:
            src, dst, target = p_own.at[j, pl.ds(theirs, HALF)], p_recv.at[j], twin
        elif s == 1:
            src, dst, target = p_chip.at[j], p_far.at[j], far
        else:
            src = dst = p_out.at[j, pl.ds(mine, HALF)]
            target = twin
        return pltpu.make_async_remote_copy(
            src_ref=src, dst_ref=dst, send_sem=p_send.at[s, j], recv_sem=p_arrive.at[s, j],
            device_id=target, device_id_type=MESH,
        )

    def p_step(s, j):
        if s > 0:
            p_copy(s - 1, j).wait_recv()
        if s == 1:
            p_chip[j] = p_own[j, pl.ds(mine, HALF)] + p_recv[j]
        if s == 2:
            p_out[j, pl.ds(mine, HALF)] = (p_chip[j] + p_far[j]) * 0.25
        if s < 3:
            p_copy(s, j).start()

    halves = {}

    def transposed(j):
        if j not in halves:
            halves[j] = split(p_out[j].T)
        return halves[j]

    def three(src, dst, send, arrive, a, b):
        targets = (near[b], near[a], corner[min(a, b), max(a, b)])
        return [remote(src(f), dst(f), send.at[f], arrive.at[f], targets[f]) for f in range(3)]

    def gram_chain(j):
        hi, lo = transposed(j)
        square = dot_nt(hi, hi) + (dot_nt(hi, lo) + dot_nt(lo, hi))
        lane = lax.broadcasted_iota(jnp.int32, (R, 2 * R), 1)
        gram_own[j] = jnp.where(lane < 64, square[:64], square[64:])
        rows = pl.ds(pl.multiple_of(core * 32, 32), 32)
        gram_half[j, 0] = gram_own[j, rows]
        for s, (one, two) in enumerate(GRAM_PAIRS if j % 2 == 0 else GRAM_PAIRS[::-1]):
            copies = three(
                lambda f: gram_half.at[j, s], lambda f: gram_recv.at[j, s, f], gram_send.at[j, s], gram_arrive.at[j, s],
                one, two,
            )
            yield
            for copy in copies:
                copy.wait_recv()
            got = gram_recv.at[j, s]
            gram_half[j, s + 1] = (gram_half[j, s] + got[1]) + (got[0] + got[2])
        copy = remote(
            gram_half.at[j, 2], gram_recv.at[j, 2, 0], gram_send.at[j, 2, 0], gram_arrive.at[j, 2, 0], near[1],
        )
        yield
        copy.wait_recv()
        gram_out[j, rows] = gram_half[j, 2] + gram_recv[j, 2, 0]
        part = gram_out.at[j, rows]
        copy = remote(part, part, gram_send.at[j, 2, 1], gram_arrive.at[j, 2, 1], twin)
        yield
        copy.wait_recv()

    def local_g(m):
        j, b = divmod(m, 2)
        hi, lo = transposed(j)
        top = hi[64 * b : 64 * b + 64]
        both = jnp.concatenate([top, lo[64 * b : 64 * b + 64]], axis=0)
        for start, size in COLS:
            cols = slice(start, start + size)
            wide = dot(both, mh[m, :, cols])
            g_acc[m, :, cols] = wide[:64] + wide[64:] + dot(top, ml[m, :, cols])

    def g_chain(m):
        link = LINKS[m]
        keep = pl.multiple_of(core * 32, 32)
        give = pl.multiple_of((1 - core) * 32, 32)

        def both_ways(place, i):
            hi, lo = sides[link[i]], sides[link[i + 1]]
            return place(hi, lo), (place(hi, 1 - lo), place(1 - hi, lo), place(1 - hi, 1 - lo))

        def tile(h, l):
            return pl.ds(pl.multiple_of(core * 32 + (2 * h + l) * 8, 8), 8)

        def block(h, l):
            return pl.ds(pl.multiple_of((2 * h + l) * BLOCK, 128), BLOCK)

        rows, other_rows = both_ways(tile, 0)
        own, others = both_ways(block, 2)
        far_rows = pl.ds(pl.multiple_of(core * 32 + 16 - 16 * sides[link[0]], 16), 16)

        def send(s, src, dst, i):
            return three(src, dst, a_send.at[s, m], a_arrive.at[s, m], link[i], link[i + 1])

        def forward(i, where):
            part = g_sum.at[m, where, pl.ds(0, D)]
            return remote(part, part, c_send.at[i, m], c_arrive.at[i, m], twin)

        def wait(copies):
            for copy in copies:
                copy.wait_recv()

        copy = remote(g_acc.at[m, pl.ds(give, 32)], core_recv.at[m], c_send.at[0, m], c_arrive.at[0, m], twin)
        yield
        copy.wait_recv()
        g_acc[m, pl.ds(keep, 32)] += core_recv[m]
        copies = send(0, lambda f: g_acc.at[m, other_rows[f]], lambda f: recv1.at[m, f], 0)
        yield
        wait(copies)
        q_acc[m, :, :D] = (g_acc[m, rows] + recv1[m, 1]) + (recv1[m, 0] + recv1[m, 2])
        copies = send(1, lambda f: q_acc.at[m, :, others[f]], lambda f: recv2.at[m, f], 2)
        yield
        wait(copies)
        x_acc[m] = (q_acc[m, :, own] + recv2[m, 1]) + (recv2[m, 0] + recv2[m, 2])
        copies = send(2, lambda f: x_acc.at[m], lambda f: recv3.at[m, f], 4)
        yield
        wait(copies)
        g_sum[m, rows, own] = (x_acc[m] + recv3[m, 1]) + (recv3[m, 0] + recv3[m, 2])
        part = g_sum.at[m, rows, own]
        copies = send(3, lambda f: part, lambda f: part, 2)
        yield
        wait(copies)
        whole = g_sum.at[m, rows, pl.ds(0, D)]
        copies = send(4, lambda f: whole, lambda f: whole, 0)
        passed = [forward(1, rows)]
        yield
        wait(copies)
        passed += [forward(2, other_rows[0]), forward(3, far_rows)]
        yield
        wait(passed)

    gc = [gram_chain(j) for j in range(3)]
    ac = [g_chain(m) for m in range(MATS)]
    factor = None

    p_stage = [0, 0, 0]
    for what, i in ORDER:
        if what == "products":
            local_p(i)
            if i == 0:
                pl.semaphore_wait(barrier, len(everyone))
        elif what == "p":
            p_step(p_stage[i], i)
            p_stage[i] += 1
        elif what == "gram":
            next(gc[i], None)
        elif what == "terms":
            local_g(i)
        elif what == "sum":
            next(ac[i], None)
        else:
            if factor is None:
                factor = eliminate([gram_out[j] for j in range(3)], y_out, p_out, lhs_err, lhs_q)
            for _ in range(i):
                next(factor, None)
    for _ in factor:
        pass
    for s in range(3):
        for j in range(3):
            p_copy(s, j).wait_send()
    for copy in sent:
        copy.wait_send()


def finish_kernel(g_sum, lhs_err, lhs_q, m_ref, err_hbm, q_out, ebuf, new_q, wst, store_sem, q_sem):
    stores = []
    for m in range(MATS):
        gh, gl = split(g_sum[m, :, :D] * 0.25)
        wst[0, 0:64] = gh
        wst[0, 64:128] = gh
        wst[0, 128:192] = gl
        fresh = dot(lhs_q[m, :, :192], wst[0])
        new_q[m] = fresh
        store = pltpu.make_async_copy(new_q.at[m], q_out.at[m], q_sem.at[m])
        store.start()
        stores.append(store)
        nh, nl = split(fresh)
        wst[1, 0:64] = nh
        wst[1, 64:128] = nh
        wst[1, 128:192] = nl
        for i, (start, size) in enumerate(COLS):
            cols = slice(start, start + size)
            ebuf[m, :, cols] = m_ref[m, :, cols] - dot(lhs_err[m, :, :192], wst[1, :, cols])
            place = pl.ds(start, size)
            store = pltpu.make_async_copy(
                ebuf.at[m, :, place], err_hbm.at[0, m, :, place], store_sem.at[m, i]
            )
            store.start()
            stores.append(store)
    for store in stores:
        store.wait()


def body(gradients, errors, previous_q):
    vmem = pl.BlockSpec(memory_space=pltpu.VMEM)
    far_hbm = pl.BlockSpec(memory_space=pltpu.HBM)
    sem = pltpu.SemaphoreType.DMA
    g_sum, lhs_err, lhs_q, merged = pl.pallas_call(
        comm_kernel,
        out_shape=(
            jax.ShapeDtypeStruct((MATS, R, 4 * BLOCK), f32),
            jax.ShapeDtypeStruct((MATS, ROWS, 256), bf16),
            jax.ShapeDtypeStruct((MATS, R, 256), bf16),
            jax.ShapeDtypeStruct((MATS, ROWS, D), f32),
        ),
        in_specs=[far_hbm, far_hbm, far_hbm],
        out_specs=(vmem, vmem, vmem, vmem),
        scratch_shapes=[
            pltpu.VMEM((MATS // 2, ROWS, 2 * R), f32),
            pltpu.VMEM((8 * R, 2 * R), f32),
            pltpu.VMEM((MATS, ROWS, D), bf16),
            pltpu.VMEM((MATS, R, D), f32),
            pltpu.VMEM((MATS, ROWS, D), bf16),
            pltpu.VMEM((MATS, ROWS, D), bf16),
            pltpu.VMEM((2, 256, D), bf16),
            pltpu.VMEM((MATS // 2, ROWS, 128), f32),
            pltpu.VMEM((MATS // 2, HALF, 128), f32),
            pltpu.VMEM((MATS // 2, HALF, 128), f32),
            pltpu.VMEM((MATS // 2, HALF, 128), f32),
            pltpu.VMEM((MATS, R, D), f32),
            pltpu.VMEM((MATS, 32, D), f32),
            pltpu.VMEM((MATS, 3, 8, D), f32),
            pltpu.VMEM((MATS, 8, 4 * BLOCK), f32),
            pltpu.VMEM((MATS, 8, BLOCK), f32),
            pltpu.VMEM((MATS, 3, 8, BLOCK), f32),
            pltpu.VMEM((MATS, 3, 8, BLOCK), f32),
            pltpu.VMEM((MATS // 2, R, 2 * R), f32),
            pltpu.VMEM((MATS // 2, 3, R // 2, 2 * R), f32),
            pltpu.VMEM((MATS // 2, 3, 3, R // 2, 2 * R), f32),
            pltpu.VMEM((MATS // 2, R, 2 * R), f32),
            sem((MATS, 3)),
            sem((3, 3)),
            sem((3, 3)),
            sem((4, MATS)),
            sem((4, MATS)),
            sem((5, MATS, 3)),
            sem((5, MATS, 3)),
            sem((3, 3, 3)),
            sem((3, 3, 3)),
        ],
        compiler_params=pltpu.CompilerParams(
            collective_id=0, has_side_effects=True, vmem_limit_bytes=40 * 2**20
        ),
        name="compress_and_sum",
    )(*[pltpu.with_memory_space_constraint(v, pltpu.HBM) for v in (gradients, errors, previous_q)])
    return pl.pallas_call(
        finish_kernel,
        out_shape=(
            jax.ShapeDtypeStruct((1, MATS, ROWS, D), f32),
            jax.ShapeDtypeStruct((MATS, R, D), f32),
        ),
        in_specs=[vmem, vmem, vmem, vmem],
        out_specs=(far_hbm, far_hbm),
        scratch_shapes=[
            pltpu.VMEM((MATS, ROWS, D), f32),
            pltpu.VMEM((MATS, R, D), f32),
            pltpu.VMEM((2, ROWS, D), bf16),
            sem((MATS, 3)),
            sem((MATS,)),
        ],
        compiler_params=pltpu.CompilerParams(vmem_limit_bytes=24 * 2**20),
        name="new_q_and_errors",
    )(g_sum, lhs_err, lhs_q, merged)


def solution(mesh):
    in_specs = (P("dp", None, "mp", None), P("dp", None, "mp", None), P())
    out_specs = (P("dp", None, "mp", None), P())
    return jax.shard_map(body, mesh=mesh, in_specs=in_specs, out_specs=out_specs, check_vma=False)
```

```python
import functools

import jax
import jax.numpy as jnp
from jax import lax
from jax.experimental import pallas as pl
from jax.experimental.pallas import tpu as pltpu
from jax.sharding import PartitionSpec as P

MESH = pl.DeviceIdType.MESH
MATS, ROWS, D, R = 6, 192, 1408, 64
HALF = ROWS // 2
BLOCK = 384
AHEAD = 3
COLS = ((0, 512), (512, 512), (1024, 384))
f32, bf16 = jnp.float32, jnp.bfloat16
LINKS = (
    (1, 2, 4, 3, 5, 0),
    (3, 4, 1, 2, 5, 0),
    (0, 5, 1, 2, 4, 3),
    (0, 5, 3, 4, 2, 1),
    (4, 3, 2, 1, 0, 5),
    (2, 1, 5, 0, 3, 4),
)
GRAM_PAIRS = ((2, 3), (5, 0))
PAIRS = tuple(sorted({tuple(sorted(links[i : i + 2])) for links in LINKS + GRAM_PAIRS for i in range(0, len(links), 2)}))
ORDER = (
    ("products", 0), ("p", 0), ("products", 1), ("p", 1), ("p", 0), ("products", 2), ("p", 2), ("p", 1),
    ("p", 2), ("p", 0), ("p", 0), ("terms", 0), ("p", 1), ("sum", 0), ("terms", 1), ("sum", 1), ("gram", 0),
    ("p", 1), ("terms", 2), ("p", 2), ("sum", 2), ("sum", 0), ("sum", 1), ("terms", 3), ("sum", 3),
    ("gram", 1), ("p", 2), ("terms", 4), ("sum", 4), ("sum", 2), ("terms", 5), ("sum", 5), ("sum", 3),
    ("gram", 2), ("gram", 0), ("sum", 4), ("sum", 5), ("sum", 0), ("gram", 1), ("sum", 1), ("gram", 2),
    ("sum", 2), ("sum", 5), ("sum", 4), ("sum", 3), ("sum", 0), ("sum", 1), ("gram", 0), ("gram", 1),
    ("sum", 2), ("gram", 2), ("sum", 4), ("sum", 5), ("gram", 0), ("sum", 3), ("gram", 1), ("sum", 0),
    ("gram", 2), ("sum", 1), ("gram", 0), ("sum", 2), ("gram", 1), ("gram", 2), ("factor", 1), ("factor", 1),
    ("sum", 4), ("sum", 3), ("sum", 5), ("factor", 1), ("sum", 0), ("sum", 1), ("sum", 2), ("factor", 1),
    ("factor", 1), ("factor", 1), ("sum", 4), ("factor", 1), ("sum", 3), ("sum", 5), ("factor", 1),
    ("factor", 1), ("sum", 0), ("factor", 1), ("factor", 1), ("sum", 1), ("sum", 2), ("sum", 0),
    ("factor", 1), ("factor", 1), ("sum", 1), ("factor", 1), ("sum", 4), ("sum", 5), ("sum", 2),
    ("factor", 1), ("sum", 3), ("factor", 1), ("factor", 1), ("factor", 1), ("factor", 1), ("sum", 4),
    ("sum", 5), ("sum", 3),
)
NT = (((1,), (1,)), ((), ()))


def dot(a, b):
    return jnp.dot(a, b, preferred_element_type=f32)


def dot_nt(a, b):
    return lax.dot_general(a, b, NT, preferred_element_type=f32)


def split(x):
    hi = x.astype(bf16)
    return hi, (x - hi.astype(f32)).astype(bf16)


def eliminate(grams, y_ref, p_ref, lhs_err, lhs_q):
    row = lax.broadcasted_iota(jnp.int32, (R, 2 * R), 0)
    lane = lax.broadcasted_iota(jnp.int32, (R, 2 * R), 1)
    eye = jnp.where(lane == row + 64, 1.0, 0.0)
    unit = jnp.where(lane == row, 1.0, 0.0)
    for m in range(8):
        if m < MATS:
            gram = grams[m // 2]
            gram = pltpu.roll(gram, 64, axis=1) if m % 2 else gram
        else:
            gram = unit
        y_ref[pl.ds(m, R, stride=8), :] = jnp.where(lane < 64, gram, eye)
    rows = [y_ref[8 * i : 8 * i + 8] for i in range(R)]

    def at(r, k):
        return jnp.broadcast_to(r[:, k : k + 1], (8, 128))

    for k in range(0, R, 4):
        r0, r1, r2, r3 = rows[k : k + 4]
        s00, s01, s02, s03 = (at(r0, k + i) for i in range(4))
        s11, s12, s13 = (at(r1, k + i) for i in range(1, 4))
        s22, s23, s33 = at(r2, k + 2), at(r2, k + 3), at(r3, k + 3)
        i0 = 1.0 / s00
        l10, l20, l30 = s01 * i0, s02 * i0, s03 * i0
        d1 = s11 - l10 * s01
        t12, t13 = s12 - l10 * s02, s13 - l10 * s03
        i1 = 1.0 / d1
        l21, l31 = t12 * i1, t13 * i1
        d2 = s22 - l20 * s02 - l21 * t12
        t23 = s23 - l20 * s03 - l21 * t13
        i2 = 1.0 / d2
        l32 = t23 * i2
        d3 = s33 - l30 * s03 - l31 * t13 - l32 * t23
        i3 = 1.0 / d3
        r1 = r1 - l10 * r0
        r2 = r2 - l20 * r0 - l21 * r1
        r3 = r3 - l30 * r0 - l31 * r1 - l32 * r2
        q0, q1, q2, q3 = r0 * i0, r1 * i1, r2 * i2, r3 * i3
        for i in range(k + 4, R):
            if i < k + 8:
                c0, c1, c2, c3 = (at(rows[i], k + j) for j in range(4))
                c1 = c1 - l10 * c0
                c2 = c2 - l20 * c0 - l21 * c1
                c3 = c3 - l30 * c0 - l31 * c1 - l32 * c2
            else:
                c0, c1, c2, c3 = at(r0, i), at(r1, i), at(r2, i), at(r3, i)
            rows[i] = rows[i] - (c0 * q0 + c1 * q1) - (c2 * q2 + c3 * q3)
        for i, (r, d) in enumerate(((r0, s00), (r1, d1), (r2, d2), (r3, d3))):
            y_ref[8 * (k + i) : 8 * (k + i) + 8] = r * (1.0 / jnp.sqrt(d))
        yield
    wide_lane = lax.broadcasted_iota(jnp.int32, (ROWS, 2 * R), 1)
    for m in range(MATS):
        side = jnp.where(lane >= 64, y_ref[pl.ds(m, R, stride=8), :], 0.0)
        other = pltpu.roll(side, 64, axis=1)
        inverse = side if m % 2 else other
        bh, bl = split(jnp.concatenate([inverse, inverse], axis=0))
        ph, pl_ = split(p_ref[m // 2])
        ortho = dot_nt(ph, bh) + (dot_nt(ph, bl) + dot_nt(pl_, bh))
        oh, ol = split(ortho)
        lhs_err[m] = jnp.concatenate([jnp.where(wide_lane < 64, oh, ol), oh], axis=1)
        lh, ll = split(side + other)
        lhs_q[m] = jnp.concatenate([jnp.where(lane < 64, lh, ll), lh], axis=1)
        if m % 2:
            yield


def comm_kernel(
    g_hbm, e_hbm, q_hbm, g_sum, lhs_err, lhs_q, ebuf,
    p_out, y_out, gbuf, qbuf, mh, ml, qst, p_own, p_recv, p_chip, p_far, g_acc,
    core_recv, recv1, q_acc, x_acc, recv2, recv3, gram_own, gram_half, gram_recv, gram_out,
    load_sem, p_send, p_arrive, c_send, c_arrive, a_send, a_arrive,
    gram_send, gram_arrive,
):
    dp, mp = lax.axis_index("dp"), lax.axis_index("mp")
    y_hi, core = lax.div(dp, 2), lax.rem(dp, 2)
    x = lax.rem(mp, 4)
    z = lax.rem(lax.div(mp, 4), 4)
    y = y_hi * 2 + lax.div(mp, 16)

    def device(xx, yy, zz, cc):
        return (lax.div(yy, 2) * 2 + cc, lax.rem(yy, 2) * 16 + zz * 4 + xx)

    def flip(v):
        return v + 1 - 2 * lax.rem(v, 2)

    def side0(v):
        hi = lax.div(v, 2)
        lo = lax.rem(v, 2)
        return hi + lo - 2 * hi * lo

    def side1(v):
        return lax.div(v, 2)

    def over(*links):
        xx, yy, zz = x, y, z
        for link in links:
            if link % 3 == 0:
                xx = flip(x) if link == 0 else 3 - x
            elif link % 3 == 1:
                yy = flip(y) if link == 1 else 3 - y
            else:
                zz = flip(z) if link == 2 else 3 - z
        return device(xx, yy, zz, core)

    near = tuple(over(link) for link in range(6))
    corner = {pair: over(*pair) for pair in PAIRS}
    sides = (side0(x), side0(y), side0(z), side1(x), side1(y), side1(z))
    twin = device(x, y, z, 1 - core)
    far = device(x, lax.rem(y + 2, 4), z, core)

    def loads(m):
        return (
            pltpu.make_async_copy(q_hbm.at[m], qbuf.at[m], load_sem.at[m, 0]),
            pltpu.make_async_copy(g_hbm.at[0, m], gbuf.at[m], load_sem.at[m, 1]),
            pltpu.make_async_copy(e_hbm.at[0, m], ebuf.at[m], load_sem.at[m, 2]),
        )

    def begin(m, _):
        for copy in loads(m):
            copy.start()
        return 0

    lax.fori_loop(0, AHEAD, begin, 0)
    barrier = pltpu.get_barrier_semaphore()
    everyone = near + tuple(corner.values()) + (twin, far)
    for other in everyone:
        pl.semaphore_signal(barrier, inc=1, device_id=other, device_id_type=MESH)

    sent = []

    def remote(src, dst, send, arrive, target):
        copy = pltpu.make_async_remote_copy(
            src_ref=src, dst_ref=dst, send_sem=send, recv_sem=arrive,
            device_id=target, device_id_type=MESH,
        )
        copy.start()
        sent.append(copy)
        return copy

    mine = pl.multiple_of(core * HALF, 8)
    theirs = pl.multiple_of((1 - core) * HALF, 8)
    qst[...] = jnp.zeros_like(qst)
    q_acc[...] = jnp.zeros_like(q_acc)

    def arrive(m):
        for copy in loads(m):
            copy.wait()

    def merge(m):
        for r in range(0, ROWS, 32):
            rows = slice(r, r + 32)
            merged = gbuf[m, rows].astype(f32) + ebuf[m, rows]
            ebuf[m, rows] = merged
            hi, lo = split(merged)
            mh[m, rows] = hi
            ml[m, rows] = lo
        b = m % 2
        hi, lo = split(qbuf[m])
        qst[b, 64 * b : 64 * b + 64] = hi
        qst[b, 128 + 64 * b : 192 + 64 * b] = lo

    def local_p(j):
        if j == 0:
            arrive(0)
            begin(AHEAD, 0)
            merge(0)
        total = None
        for m in (2 * j, 2 * j + 1):
            if m + 1 < MATS:
                arrive(m + 1)
                if m + 1 + AHEAD < MATS:
                    begin(m + 1 + AHEAD, 0)
            wide = dot_nt(mh[m], qst[m % 2])
            part = wide[:, :128] + wide[:, 128:] + dot_nt(ml[m], qst[m % 2, :128])
            if m + 1 < MATS:
                merge(m + 1)
            total = part if total is None else total + part
        p_own[j] = total

    def p_copy(s, j):
        if s == 0:
            src, dst, target = p_own.at[j, pl.ds(theirs, HALF)], p_recv.at[j], twin
        elif s == 1:
            src, dst, target = p_chip.at[j], p_far.at[j], far
        else:
            src = dst = p_out.at[j, pl.ds(mine, HALF)]
            target = twin
        return pltpu.make_async_remote_copy(
            src_ref=src, dst_ref=dst, send_sem=p_send.at[s, j], recv_sem=p_arrive.at[s, j],
            device_id=target, device_id_type=MESH,
        )

    def p_step(s, j):
        if s > 0:
            p_copy(s - 1, j).wait_recv()
        if s == 1:
            p_chip[j] = p_own[j, pl.ds(mine, HALF)] + p_recv[j]
        if s == 2:
            p_out[j, pl.ds(mine, HALF)] = (p_chip[j] + p_far[j]) * 0.25
        if s < 3:
            p_copy(s, j).start()

    halves = {}

    def transposed(j):
        if j not in halves:
            halves[j] = split(p_out[j].T)
        return halves[j]

    def three(src, dst, send, arrive, a, b):
        targets = (near[b], near[a], corner[min(a, b), max(a, b)])
        return [remote(src(f), dst(f), send.at[f], arrive.at[f], targets[f]) for f in range(3)]

    def gram_chain(j):
        hi, lo = transposed(j)
        square = dot_nt(hi, hi) + (dot_nt(hi, lo) + dot_nt(lo, hi))
        lane = lax.broadcasted_iota(jnp.int32, (R, 2 * R), 1)
        gram_own[j] = jnp.where(lane < 64, square[:64], square[64:])
        rows = pl.ds(pl.multiple_of(core * 32, 32), 32)
        gram_half[j, 0] = gram_own[j, rows]
        for s, (one, two) in enumerate(GRAM_PAIRS if j % 2 == 0 else GRAM_PAIRS[::-1]):
            copies = three(
                lambda f: gram_half.at[j, s], lambda f: gram_recv.at[j, s, f], gram_send.at[j, s], gram_arrive.at[j, s],
                one, two,
            )
            yield
            for copy in copies:
                copy.wait_recv()
            got = gram_recv.at[j, s]
            gram_half[j, s + 1] = (gram_half[j, s] + got[1]) + (got[0] + got[2])
        copy = remote(
            gram_half.at[j, 2], gram_recv.at[j, 2, 0], gram_send.at[j, 2, 0], gram_arrive.at[j, 2, 0], near[1],
        )
        yield
        copy.wait_recv()
        gram_out[j, rows] = gram_half[j, 2] + gram_recv[j, 2, 0]
        part = gram_out.at[j, rows]
        copy = remote(part, part, gram_send.at[j, 2, 1], gram_arrive.at[j, 2, 1], twin)
        yield
        copy.wait_recv()

    def local_g(m):
        j, b = divmod(m, 2)
        hi, lo = transposed(j)
        top = hi[64 * b : 64 * b + 64]
        both = jnp.concatenate([top, lo[64 * b : 64 * b + 64]], axis=0)
        for start, size in COLS:
            cols = slice(start, start + size)
            wide = dot(both, mh[m, :, cols])
            g_acc[m, :, cols] = wide[:64] + wide[64:] + dot(top, ml[m, :, cols])

    def g_chain(m):
        link = LINKS[m]
        keep = pl.multiple_of(core * 32, 32)
        give = pl.multiple_of((1 - core) * 32, 32)

        def both_ways(place, i):
            hi, lo = sides[link[i]], sides[link[i + 1]]
            return place(hi, lo), (place(hi, 1 - lo), place(1 - hi, lo), place(1 - hi, 1 - lo))

        def tile(h, l):
            return pl.ds(pl.multiple_of(core * 32 + (2 * h + l) * 8, 8), 8)

        def block(h, l):
            return pl.ds(pl.multiple_of((2 * h + l) * BLOCK, 128), BLOCK)

        rows, other_rows = both_ways(tile, 0)
        own, others = both_ways(block, 2)
        far_rows = pl.ds(pl.multiple_of(core * 32 + 16 - 16 * sides[link[0]], 16), 16)

        def send(s, src, dst, i):
            return three(src, dst, a_send.at[s, m], a_arrive.at[s, m], link[i], link[i + 1])

        def forward(i, where):
            part = g_sum.at[m, where, pl.ds(0, D)]
            return remote(part, part, c_send.at[i, m], c_arrive.at[i, m], twin)

        def wait(copies):
            for copy in copies:
                copy.wait_recv()

        copy = remote(g_acc.at[m, pl.ds(give, 32)], core_recv.at[m], c_send.at[0, m], c_arrive.at[0, m], twin)
        yield
        copy.wait_recv()
        g_acc[m, pl.ds(keep, 32)] += core_recv[m]
        copies = send(0, lambda f: g_acc.at[m, other_rows[f]], lambda f: recv1.at[m, f], 0)
        yield
        wait(copies)
        q_acc[m, :, :D] = (g_acc[m, rows] + recv1[m, 1]) + (recv1[m, 0] + recv1[m, 2])
        copies = send(1, lambda f: q_acc.at[m, :, others[f]], lambda f: recv2.at[m, f], 2)
        yield
        wait(copies)
        x_acc[m] = (q_acc[m, :, own] + recv2[m, 1]) + (recv2[m, 0] + recv2[m, 2])
        copies = send(2, lambda f: x_acc.at[m], lambda f: recv3.at[m, f], 4)
        yield
        wait(copies)
        g_sum[m, rows, own] = (x_acc[m] + recv3[m, 1]) + (recv3[m, 0] + recv3[m, 2])
        part = g_sum.at[m, rows, own]
        copies = send(3, lambda f: part, lambda f: part, 2)
        yield
        wait(copies)
        whole = g_sum.at[m, rows, pl.ds(0, D)]
        copies = send(4, lambda f: whole, lambda f: whole, 0)
        passed = [forward(1, rows)]
        yield
        wait(copies)
        passed += [forward(2, other_rows[0]), forward(3, far_rows)]
        yield
        wait(passed)

    gc = [gram_chain(j) for j in range(3)]
    ac = [g_chain(m) for m in range(MATS)]
    factor = None

    p_stage = [0, 0, 0]
    for what, i in ORDER:
        if what == "products":
            local_p(i)
            if i == 0:
                pl.semaphore_wait(barrier, len(everyone))
        elif what == "p":
            p_step(p_stage[i], i)
            p_stage[i] += 1
        elif what == "gram":
            next(gc[i], None)
        elif what == "terms":
            local_g(i)
        elif what == "sum":
            next(ac[i], None)
        else:
            if factor is None:
                factor = eliminate([gram_out[j] for j in range(3)], y_out, p_out, lhs_err, lhs_q)
            for _ in range(i):
                next(factor, None)
    for _ in factor:
        pass
    for s in range(3):
        for j in range(3):
            p_copy(s, j).wait_send()
    for copy in sent:
        copy.wait_send()


def finish_kernel(g_sum, lhs_err, lhs_q, m_ref, err_hbm, q_out, ebuf, new_q, wst, store_sem, q_sem):
    stores = []
    for m in range(MATS):
        gh, gl = split(g_sum[m, :, :D] * 0.25)
        wst[0, 0:64] = gh
        wst[0, 64:128] = gh
        wst[0, 128:192] = gl
        fresh = dot(lhs_q[m, :, :192], wst[0])
        new_q[m] = fresh
        store = pltpu.make_async_copy(new_q.at[m], q_out.at[m], q_sem.at[m])
        store.start()
        stores.append(store)
        nh, nl = split(fresh)
        wst[1, 0:64] = nh
        wst[1, 64:128] = nh
        wst[1, 128:192] = nl
        for i, (start, size) in enumerate(COLS):
            cols = slice(start, start + size)
            ebuf[m, :, cols] = m_ref[m, :, cols] - dot(lhs_err[m, :, :192], wst[1, :, cols])
            place = pl.ds(start, size)
            store = pltpu.make_async_copy(
                ebuf.at[m, :, place], err_hbm.at[0, m, :, place], store_sem.at[m, i]
            )
            store.start()
            stores.append(store)
    for store in stores:
        store.wait()


def body(gradients, errors, previous_q):
    vmem = pl.BlockSpec(memory_space=pltpu.VMEM)
    far_hbm = pl.BlockSpec(memory_space=pltpu.HBM)
    sem = pltpu.SemaphoreType.DMA
    g_sum, lhs_err, lhs_q, merged = pl.pallas_call(
        comm_kernel,
        out_shape=(
            jax.ShapeDtypeStruct((MATS, R, 4 * BLOCK), f32),
            jax.ShapeDtypeStruct((MATS, ROWS, 256), bf16),
            jax.ShapeDtypeStruct((MATS, R, 256), bf16),
            jax.ShapeDtypeStruct((MATS, ROWS, D), f32),
        ),
        in_specs=[far_hbm, far_hbm, far_hbm],
        out_specs=(vmem, vmem, vmem, vmem),
        scratch_shapes=[
            pltpu.VMEM((MATS // 2, ROWS, 2 * R), f32),
            pltpu.VMEM((8 * R, 2 * R), f32),
            pltpu.VMEM((MATS, ROWS, D), bf16),
            pltpu.VMEM((MATS, R, D), f32),
            pltpu.VMEM((MATS, ROWS, D), bf16),
            pltpu.VMEM((MATS, ROWS, D), bf16),
            pltpu.VMEM((2, 256, D), bf16),
            pltpu.VMEM((MATS // 2, ROWS, 128), f32),
            pltpu.VMEM((MATS // 2, HALF, 128), f32),
            pltpu.VMEM((MATS // 2, HALF, 128), f32),
            pltpu.VMEM((MATS // 2, HALF, 128), f32),
            pltpu.VMEM((MATS, R, D), f32),
            pltpu.VMEM((MATS, 32, D), f32),
            pltpu.VMEM((MATS, 3, 8, D), f32),
            pltpu.VMEM((MATS, 8, 4 * BLOCK), f32),
            pltpu.VMEM((MATS, 8, BLOCK), f32),
            pltpu.VMEM((MATS, 3, 8, BLOCK), f32),
            pltpu.VMEM((MATS, 3, 8, BLOCK), f32),
            pltpu.VMEM((MATS // 2, R, 2 * R), f32),
            pltpu.VMEM((MATS // 2, 3, R // 2, 2 * R), f32),
            pltpu.VMEM((MATS // 2, 3, 3, R // 2, 2 * R), f32),
            pltpu.VMEM((MATS // 2, R, 2 * R), f32),
            sem((MATS, 3)),
            sem((3, 3)),
            sem((3, 3)),
            sem((4, MATS)),
            sem((4, MATS)),
            sem((5, MATS, 3)),
            sem((5, MATS, 3)),
            sem((3, 3, 3)),
            sem((3, 3, 3)),
        ],
        compiler_params=pltpu.CompilerParams(
            collective_id=0, has_side_effects=True, vmem_limit_bytes=40 * 2**20
        ),
        name="compress_and_sum",
    )(*[pltpu.with_memory_space_constraint(v, pltpu.HBM) for v in (gradients, errors, previous_q)])
    return pl.pallas_call(
        finish_kernel,
        out_shape=(
            jax.ShapeDtypeStruct((1, MATS, ROWS, D), f32),
            jax.ShapeDtypeStruct((MATS, R, D), f32),
        ),
        in_specs=[vmem, vmem, vmem, vmem],
        out_specs=(far_hbm, far_hbm),
        scratch_shapes=[
            pltpu.VMEM((MATS, ROWS, D), f32),
            pltpu.VMEM((MATS, R, D), f32),
            pltpu.VMEM((2, ROWS, D), bf16),
            sem((MATS, 3)),
            sem((MATS,)),
        ],
        compiler_params=pltpu.CompilerParams(vmem_limit_bytes=24 * 2**20),
        name="new_q_and_errors",
    )(g_sum, lhs_err, lhs_q, merged)


def solution(mesh):
    in_specs = (P("dp", None, "mp", None), P("dp", None, "mp", None), P())
    out_specs = (P("dp", None, "mp", None), P())
    return jax.shard_map(body, mesh=mesh, in_specs=in_specs, out_specs=out_specs, check_vma=False)
```

```python
import functools

import jax
import jax.numpy as jnp
from jax import lax
from jax.experimental import pallas as pl
from jax.experimental.pallas import tpu as pltpu
from jax.sharding import PartitionSpec as P

MESH = pl.DeviceIdType.MESH
MATS, ROWS, D, R = 6, 192, 1408, 64
HALF = ROWS // 2
BLOCK = 384
COLS = ((0, 512), (512, 512), (1024, 384))
f32, bf16 = jnp.float32, jnp.bfloat16
LINKS = (
    (1, 2, 4, 3, 5, 0),
    (5, 0, 1, 2, 3, 4),
    (4, 3, 0, 5, 1, 2),
    (5, 0, 3, 4, 2, 1),
    (1, 2, 5, 0, 3, 4),
    (4, 3, 1, 2, 0, 5),
)
GRAM_PAIRS = ((2, 3), (5, 0))
PAIRS = tuple(sorted({tuple(sorted(links[i : i + 2])) for links in LINKS + GRAM_PAIRS for i in range(0, len(links), 2)}))
ORDER = (
    ("products", 0), ("p", 0), ("products", 1), ("p", 1), ("p", 0), ("products", 2), ("p", 2), ("p", 1),
    ("p", 2), ("p", 0), ("p", 0), ("terms", 0), ("sum", 0), ("terms", 1), ("p", 1), ("sum", 1), ("gram", 0),
    ("sum", 0), ("p", 1), ("terms", 2), ("sum", 2), ("sum", 1), ("p", 2), ("terms", 3), ("sum", 3),
    ("gram", 1), ("p", 2), ("sum", 2), ("terms", 4), ("sum", 4), ("sum", 3), ("terms", 5), ("sum", 5),
    ("gram", 2), ("sum", 4), ("gram", 0), ("sum", 5), ("sum", 0), ("sum", 1), ("gram", 1), ("sum", 2),
    ("gram", 2), ("sum", 4), ("sum", 3), ("sum", 1), ("gram", 0), ("sum", 5), ("sum", 2), ("sum", 0),
    ("gram", 1), ("gram", 2), ("gram", 0), ("sum", 4), ("sum", 3), ("gram", 0), ("sum", 5), ("sum", 1),
    ("sum", 2), ("gram", 1), ("gram", 2), ("sum", 0), ("gram", 1), ("gram", 2), ("factor", 1), ("factor", 1),
    ("sum", 3), ("sum", 4), ("factor", 1), ("sum", 5), ("sum", 1), ("sum", 2), ("factor", 1), ("sum", 0),
    ("factor", 1), ("factor", 1), ("factor", 1), ("sum", 3), ("sum", 4), ("sum", 5), ("factor", 1),
    ("factor", 1), ("factor", 1), ("factor", 1), ("factor", 1), ("sum", 1), ("sum", 2), ("sum", 0),
    ("factor", 1), ("factor", 1), ("sum", 1), ("sum", 2), ("factor", 1), ("sum", 0), ("factor", 1),
    ("sum", 3), ("factor", 1), ("sum", 4), ("sum", 5), ("factor", 1), ("factor", 1), ("sum", 3), ("sum", 4),
    ("sum", 5),
)
NT = (((1,), (1,)), ((), ()))


def dot(a, b):
    return jnp.dot(a, b, preferred_element_type=f32)


def dot_nt(a, b):
    return lax.dot_general(a, b, NT, preferred_element_type=f32)


def split(x):
    hi = x.astype(bf16)
    return hi, (x - hi.astype(f32)).astype(bf16)


def eliminate(grams, y_ref, p_ref, lhs_err, lhs_q):
    row = lax.broadcasted_iota(jnp.int32, (R, 2 * R), 0)
    lane = lax.broadcasted_iota(jnp.int32, (R, 2 * R), 1)
    eye = jnp.where(lane == row + 64, 1.0, 0.0)
    unit = jnp.where(lane == row, 1.0, 0.0)
    for m in range(8):
        if m < MATS:
            gram = grams[m // 2]
            gram = pltpu.roll(gram, 64, axis=1) if m % 2 else gram
        else:
            gram = unit
        y_ref[pl.ds(m, R, stride=8), :] = jnp.where(lane < 64, gram, eye)
    rows = [y_ref[8 * i : 8 * i + 8] for i in range(R)]

    def at(r, k):
        return jnp.broadcast_to(r[:, k : k + 1], (8, 128))

    for k in range(0, R, 4):
        r0, r1, r2, r3 = rows[k : k + 4]
        s00, s01, s02, s03 = (at(r0, k + i) for i in range(4))
        s11, s12, s13 = (at(r1, k + i) for i in range(1, 4))
        s22, s23, s33 = at(r2, k + 2), at(r2, k + 3), at(r3, k + 3)
        i0 = 1.0 / s00
        l10, l20, l30 = s01 * i0, s02 * i0, s03 * i0
        d1 = s11 - l10 * s01
        t12, t13 = s12 - l10 * s02, s13 - l10 * s03
        i1 = 1.0 / d1
        l21, l31 = t12 * i1, t13 * i1
        d2 = s22 - l20 * s02 - l21 * t12
        t23 = s23 - l20 * s03 - l21 * t13
        i2 = 1.0 / d2
        l32 = t23 * i2
        d3 = s33 - l30 * s03 - l31 * t13 - l32 * t23
        i3 = 1.0 / d3
        r1 = r1 - l10 * r0
        r2 = r2 - l20 * r0 - l21 * r1
        r3 = r3 - l30 * r0 - l31 * r1 - l32 * r2
        q0, q1, q2, q3 = r0 * i0, r1 * i1, r2 * i2, r3 * i3
        for i in range(k + 4, R):
            if i < k + 8:
                c0, c1, c2, c3 = (at(rows[i], k + j) for j in range(4))
                c1 = c1 - l10 * c0
                c2 = c2 - l20 * c0 - l21 * c1
                c3 = c3 - l30 * c0 - l31 * c1 - l32 * c2
            else:
                c0, c1, c2, c3 = at(r0, i), at(r1, i), at(r2, i), at(r3, i)
            rows[i] = rows[i] - (c0 * q0 + c1 * q1) - (c2 * q2 + c3 * q3)
        for i, (r, d) in enumerate(((r0, s00), (r1, d1), (r2, d2), (r3, d3))):
            y_ref[8 * (k + i) : 8 * (k + i) + 8] = r * (1.0 / jnp.sqrt(d))
        yield
    wide_lane = lax.broadcasted_iota(jnp.int32, (ROWS, 2 * R), 1)
    for m in range(MATS):
        side = jnp.where(lane >= 64, y_ref[pl.ds(m, R, stride=8), :], 0.0)
        other = pltpu.roll(side, 64, axis=1)
        inverse = side if m % 2 else other
        bh, bl = split(jnp.concatenate([inverse, inverse], axis=0))
        ph, pl_ = split(p_ref[m // 2])
        ortho = dot_nt(ph, bh) + (dot_nt(ph, bl) + dot_nt(pl_, bh))
        oh, ol = split(ortho)
        lhs_err[m] = jnp.concatenate([jnp.where(wide_lane < 64, oh, ol), oh], axis=1)
        lh, ll = split(side + other)
        lhs_q[m] = jnp.concatenate([jnp.where(lane < 64, lh, ll), lh], axis=1)
        if m % 2:
            yield


def comm_kernel(
    g_hbm, e_hbm, q_hbm, g_sum, lhs_err, lhs_q, ebuf,
    p_out, y_out, gbuf, qbuf, mh, ml, qst, p_own, p_recv, p_chip, p_far, g_acc,
    core_recv, recv1, q_acc, x_acc, recv2, recv3, gram_own, gram_half, gram_recv, gram_out,
    load_sem, p_send, p_arrive, c_send, c_arrive, a_send, a_arrive,
    gram_send, gram_arrive,
):
    dp, mp = lax.axis_index("dp"), lax.axis_index("mp")
    y_hi, core = lax.div(dp, 2), lax.rem(dp, 2)
    x = lax.rem(mp, 4)
    z = lax.rem(lax.div(mp, 4), 4)
    y = y_hi * 2 + lax.div(mp, 16)

    def device(xx, yy, zz, cc):
        return (lax.div(yy, 2) * 2 + cc, lax.rem(yy, 2) * 16 + zz * 4 + xx)

    def flip(v):
        return v + 1 - 2 * lax.rem(v, 2)

    def side0(v):
        hi = lax.div(v, 2)
        lo = lax.rem(v, 2)
        return hi + lo - 2 * hi * lo

    def side1(v):
        return lax.div(v, 2)

    def over(*links):
        xx, yy, zz = x, y, z
        for link in links:
            if link % 3 == 0:
                xx = flip(x) if link == 0 else 3 - x
            elif link % 3 == 1:
                yy = flip(y) if link == 1 else 3 - y
            else:
                zz = flip(z) if link == 2 else 3 - z
        return device(xx, yy, zz, core)

    near = tuple(over(link) for link in range(6))
    corner = {pair: over(*pair) for pair in PAIRS}
    sides = (side0(x), side0(y), side0(z), side1(x), side1(y), side1(z))
    twin = device(x, y, z, 1 - core)
    far = device(x, lax.rem(y + 2, 4), z, core)

    def loads(m):
        return (
            pltpu.make_async_copy(q_hbm.at[m], qbuf.at[m], load_sem.at[m, 0]),
            pltpu.make_async_copy(g_hbm.at[0, m], gbuf.at[m], load_sem.at[m, 1]),
            pltpu.make_async_copy(e_hbm.at[0, m], ebuf.at[m], load_sem.at[m, 2]),
        )

    def begin(m, _):
        for copy in loads(m):
            copy.start()
        return 0

    lax.fori_loop(0, MATS, begin, 0)
    barrier = pltpu.get_barrier_semaphore()
    everyone = near + tuple(corner.values()) + (twin, far)
    for other in everyone:
        pl.semaphore_signal(barrier, inc=1, device_id=other, device_id_type=MESH)

    sent = []

    def remote(src, dst, send, arrive, target):
        copy = pltpu.make_async_remote_copy(
            src_ref=src, dst_ref=dst, send_sem=send, recv_sem=arrive,
            device_id=target, device_id_type=MESH,
        )
        copy.start()
        sent.append(copy)
        return copy

    mine = pl.multiple_of(core * HALF, 8)
    theirs = pl.multiple_of((1 - core) * HALF, 8)
    qst[...] = jnp.zeros_like(qst)
    q_acc[...] = jnp.zeros_like(q_acc)

    def arrive(m):
        for copy in loads(m):
            copy.wait()

    def merge(m):
        for r in range(0, ROWS, 32):
            rows = slice(r, r + 32)
            merged = gbuf[m, rows].astype(f32) + ebuf[m, rows]
            ebuf[m, rows] = merged
            hi, lo = split(merged)
            mh[m, rows] = hi
            ml[m, rows] = lo
        b = m % 2
        hi, lo = split(qbuf[m])
        qst[b, 64 * b : 64 * b + 64] = hi
        qst[b, 128 + 64 * b : 192 + 64 * b] = lo

    def local_p(j):
        if j == 0:
            arrive(0)
            merge(0)
        total = None
        for m in (2 * j, 2 * j + 1):
            if m + 1 < MATS:
                arrive(m + 1)
            wide = dot_nt(mh[m], qst[m % 2])
            part = wide[:, :128] + wide[:, 128:] + dot_nt(ml[m], qst[m % 2, :128])
            if m + 1 < MATS:
                merge(m + 1)
            total = part if total is None else total + part
        p_own[j] = total

    def p_copy(s, j):
        if s == 0:
            src, dst, target = p_own.at[j, pl.ds(theirs, HALF)], p_recv.at[j], twin
        elif s == 1:
            src, dst, target = p_chip.at[j], p_far.at[j], far
        else:
            src = dst = p_out.at[j, pl.ds(mine, HALF)]
            target = twin
        return pltpu.make_async_remote_copy(
            src_ref=src, dst_ref=dst, send_sem=p_send.at[s, j], recv_sem=p_arrive.at[s, j],
            device_id=target, device_id_type=MESH,
        )

    def p_step(s, j):
        if s > 0:
            p_copy(s - 1, j).wait_recv()
        if s == 1:
            p_chip[j] = p_own[j, pl.ds(mine, HALF)] + p_recv[j]
        if s == 2:
            p_out[j, pl.ds(mine, HALF)] = (p_chip[j] + p_far[j]) * 0.25
        if s < 3:
            p_copy(s, j).start()

    halves = {}

    def transposed(j):
        if j not in halves:
            halves[j] = split(p_out[j].T)
        return halves[j]

    def three(src, dst, send, arrive, a, b):
        targets = (near[b], near[a], corner[min(a, b), max(a, b)])
        return [remote(src(f), dst(f), send.at[f], arrive.at[f], targets[f]) for f in range(3)]

    def gram_chain(j):
        hi, lo = transposed(j)
        square = dot_nt(hi, hi) + (dot_nt(hi, lo) + dot_nt(lo, hi))
        lane = lax.broadcasted_iota(jnp.int32, (R, 2 * R), 1)
        gram_own[j] = jnp.where(lane < 64, square[:64], square[64:])
        rows = pl.ds(pl.multiple_of(core * 32, 32), 32)
        gram_half[j, 0] = gram_own[j, rows]
        for s, (one, two) in enumerate(GRAM_PAIRS if j % 2 == 0 else GRAM_PAIRS[::-1]):
            copies = three(
                lambda f: gram_half.at[j, s], lambda f: gram_recv.at[j, s, f], gram_send.at[j, s], gram_arrive.at[j, s],
                one, two,
            )
            yield
            for copy in copies:
                copy.wait_recv()
            got = gram_recv.at[j, s]
            gram_half[j, s + 1] = (gram_half[j, s] + got[1]) + (got[0] + got[2])
        copy = remote(
            gram_half.at[j, 2], gram_recv.at[j, 2, 0], gram_send.at[j, 2, 0], gram_arrive.at[j, 2, 0], near[1],
        )
        yield
        copy.wait_recv()
        gram_out[j, rows] = gram_half[j, 2] + gram_recv[j, 2, 0]
        part = gram_out.at[j, rows]
        copy = remote(part, part, gram_send.at[j, 2, 1], gram_arrive.at[j, 2, 1], twin)
        yield
        copy.wait_recv()

    def local_g(m):
        j, b = divmod(m, 2)
        hi, lo = transposed(j)
        top = hi[64 * b : 64 * b + 64]
        both = jnp.concatenate([top, lo[64 * b : 64 * b + 64]], axis=0)
        for start, size in COLS:
            cols = slice(start, start + size)
            wide = dot(both, mh[m, :, cols])
            g_acc[m, :, cols] = wide[:64] + wide[64:] + dot(top, ml[m, :, cols])

    def g_chain(m):
        link = LINKS[m]
        keep = pl.multiple_of(core * 32, 32)
        give = pl.multiple_of((1 - core) * 32, 32)

        def both_ways(place, i):
            hi, lo = sides[link[i]], sides[link[i + 1]]
            return place(hi, lo), (place(hi, 1 - lo), place(1 - hi, lo), place(1 - hi, 1 - lo))

        def tile(h, l):
            return pl.ds(pl.multiple_of(core * 32 + (2 * h + l) * 8, 8), 8)

        def block(h, l):
            return pl.ds(pl.multiple_of((2 * h + l) * BLOCK, 128), BLOCK)

        rows, other_rows = both_ways(tile, 0)
        own, others = both_ways(block, 2)
        far_rows = pl.ds(pl.multiple_of(core * 32 + 16 - 16 * sides[link[0]], 16), 16)

        def send(s, src, dst, i):
            return three(src, dst, a_send.at[s, m], a_arrive.at[s, m], link[i], link[i + 1])

        def forward(i, where):
            part = g_sum.at[m, where, pl.ds(0, D)]
            return remote(part, part, c_send.at[i, m], c_arrive.at[i, m], twin)

        def wait(copies):
            for copy in copies:
                copy.wait_recv()

        copy = remote(g_acc.at[m, pl.ds(give, 32)], core_recv.at[m], c_send.at[0, m], c_arrive.at[0, m], twin)
        yield
        copy.wait_recv()
        g_acc[m, pl.ds(keep, 32)] += core_recv[m]
        copies = send(0, lambda f: g_acc.at[m, other_rows[f]], lambda f: recv1.at[m, f], 0)
        yield
        wait(copies)
        q_acc[m, :, :D] = (g_acc[m, rows] + recv1[m, 1]) + (recv1[m, 0] + recv1[m, 2])
        copies = send(1, lambda f: q_acc.at[m, :, others[f]], lambda f: recv2.at[m, f], 2)
        yield
        wait(copies)
        x_acc[m] = (q_acc[m, :, own] + recv2[m, 1]) + (recv2[m, 0] + recv2[m, 2])
        copies = send(2, lambda f: x_acc.at[m], lambda f: recv3.at[m, f], 4)
        yield
        wait(copies)
        g_sum[m, rows, own] = (x_acc[m] + recv3[m, 1]) + (recv3[m, 0] + recv3[m, 2])
        part = g_sum.at[m, rows, own]
        copies = send(3, lambda f: part, lambda f: part, 2)
        yield
        wait(copies)
        whole = g_sum.at[m, rows, pl.ds(0, D)]
        copies = send(4, lambda f: whole, lambda f: whole, 0)
        passed = [forward(1, rows)]
        yield
        wait(copies)
        passed += [forward(2, other_rows[0]), forward(3, far_rows)]
        yield
        wait(passed)

    gc = [gram_chain(j) for j in range(3)]
    ac = [g_chain(m) for m in range(MATS)]
    factor = None

    p_stage = [0, 0, 0]
    for what, i in ORDER:
        if what == "products":
            local_p(i)
            if i == 0:
                pl.semaphore_wait(barrier, len(everyone))
        elif what == "p":
            p_step(p_stage[i], i)
            p_stage[i] += 1
        elif what == "gram":
            next(gc[i], None)
        elif what == "terms":
            local_g(i)
        elif what == "sum":
            next(ac[i], None)
        else:
            if factor is None:
                factor = eliminate([gram_out[j] for j in range(3)], y_out, p_out, lhs_err, lhs_q)
            for _ in range(i):
                next(factor, None)
    for _ in factor:
        pass
    for s in range(3):
        for j in range(3):
            p_copy(s, j).wait_send()
    for copy in sent:
        copy.wait_send()


def finish_kernel(g_sum, lhs_err, lhs_q, m_ref, err_hbm, q_out, ebuf, new_q, store_sem, q_sem):
    stores = []
    for m in range(MATS):
        for i, (start, size) in enumerate(COLS):
            cols, place = slice(start, start + size), pl.ds(start, size)
            gh, gl = split(g_sum[m, :, cols] * 0.25)
            fresh = dot(lhs_q[m, :, :192], jnp.concatenate([gh, gh, gl], axis=0))
            new_q[m, :, cols] = fresh
            nh, nl = split(fresh)
            approx = dot(lhs_err[m, :, :192], jnp.concatenate([nh, nh, nl], axis=0))
            ebuf[m, :, cols] = m_ref[m, :, cols] - approx
            store = pltpu.make_async_copy(ebuf.at[m, :, place], err_hbm.at[0, m, :, place], store_sem.at[m, i])
            store.start()
            stores.append(store)
        store = pltpu.make_async_copy(new_q.at[m], q_out.at[m], q_sem.at[m])
        store.start()
        stores.append(store)
    for store in stores:
        store.wait()


def body(gradients, errors, previous_q):
    vmem = pl.BlockSpec(memory_space=pltpu.VMEM)
    far_hbm = pl.BlockSpec(memory_space=pltpu.HBM)
    sem = pltpu.SemaphoreType.DMA
    g_sum, lhs_err, lhs_q, merged = pl.pallas_call(
        comm_kernel,
        out_shape=(
            jax.ShapeDtypeStruct((MATS, R, 4 * BLOCK), f32),
            jax.ShapeDtypeStruct((MATS, ROWS, 256), bf16),
            jax.ShapeDtypeStruct((MATS, R, 256), bf16),
            jax.ShapeDtypeStruct((MATS, ROWS, D), f32),
        ),
        in_specs=[far_hbm, far_hbm, far_hbm],
        out_specs=(vmem, vmem, vmem, vmem),
        scratch_shapes=[
            pltpu.VMEM((MATS // 2, ROWS, 2 * R), f32),
            pltpu.VMEM((8 * R, 2 * R), f32),
            pltpu.VMEM((MATS, ROWS, D), bf16),
            pltpu.VMEM((MATS, R, D), f32),
            pltpu.VMEM((MATS, ROWS, D), bf16),
            pltpu.VMEM((MATS, ROWS, D), bf16),
            pltpu.VMEM((2, 256, D), bf16),
            pltpu.VMEM((MATS // 2, ROWS, 128), f32),
            pltpu.VMEM((MATS // 2, HALF, 128), f32),
            pltpu.VMEM((MATS // 2, HALF, 128), f32),
            pltpu.VMEM((MATS // 2, HALF, 128), f32),
            pltpu.VMEM((MATS, R, D), f32),
            pltpu.VMEM((MATS, 32, D), f32),
            pltpu.VMEM((MATS, 3, 8, D), f32),
            pltpu.VMEM((MATS, 8, 4 * BLOCK), f32),
            pltpu.VMEM((MATS, 8, BLOCK), f32),
            pltpu.VMEM((MATS, 3, 8, BLOCK), f32),
            pltpu.VMEM((MATS, 3, 8, BLOCK), f32),
            pltpu.VMEM((MATS // 2, R, 2 * R), f32),
            pltpu.VMEM((MATS // 2, 3, R // 2, 2 * R), f32),
            pltpu.VMEM((MATS // 2, 3, 3, R // 2, 2 * R), f32),
            pltpu.VMEM((MATS // 2, R, 2 * R), f32),
            sem((MATS, 3)),
            sem((3, 3)),
            sem((3, 3)),
            sem((4, MATS)),
            sem((4, MATS)),
            sem((5, MATS, 3)),
            sem((5, MATS, 3)),
            sem((3, 3, 3)),
            sem((3, 3, 3)),
        ],
        compiler_params=pltpu.CompilerParams(
            collective_id=0, has_side_effects=True, vmem_limit_bytes=40 * 2**20
        ),
        name="compress_and_sum",
    )(*[pltpu.with_memory_space_constraint(v, pltpu.HBM) for v in (gradients, errors, previous_q)])
    return pl.pallas_call(
        finish_kernel,
        out_shape=(
            jax.ShapeDtypeStruct((1, MATS, ROWS, D), f32),
            jax.ShapeDtypeStruct((MATS, R, D), f32),
        ),
        in_specs=[vmem, vmem, vmem, vmem],
        out_specs=(far_hbm, far_hbm),
        scratch_shapes=[
            pltpu.VMEM((MATS, ROWS, D), f32),
            pltpu.VMEM((MATS, R, D), f32),
            sem((MATS, 3)),
            sem((MATS,)),
        ],
        compiler_params=pltpu.CompilerParams(vmem_limit_bytes=24 * 2**20),
        name="new_q_and_errors",
    )(g_sum, lhs_err, lhs_q, merged)


def solution(mesh):
    in_specs = (P("dp", None, "mp", None), P("dp", None, "mp", None), P())
    out_specs = (P("dp", None, "mp", None), P())
    return jax.shard_map(body, mesh=mesh, in_specs=in_specs, out_specs=out_specs, check_vma=False)
```

```python
import functools

import jax
import jax.numpy as jnp
from jax import lax
from jax.experimental import pallas as pl
from jax.experimental.pallas import tpu as pltpu
from jax.sharding import PartitionSpec as P

MESH = pl.DeviceIdType.MESH
MATS, ROWS, D, R = 6, 192, 1408, 64
HALF = ROWS // 2
BLOCK = 384
COLS = ((0, 512), (512, 512), (1024, 384))
f32, bf16 = jnp.float32, jnp.bfloat16
LINKS = (
    (1, 2, 4, 3, 5, 0),
    (3, 4, 1, 2, 5, 0),
    (0, 5, 1, 2, 4, 3),
    (0, 5, 3, 4, 2, 1),
    (4, 3, 2, 1, 0, 5),
    (2, 1, 5, 0, 3, 4),
)
GRAM_PAIRS = ((2, 3), (5, 0))
PAIRS = tuple(sorted({tuple(sorted(links[i : i + 2])) for links in LINKS + GRAM_PAIRS for i in range(0, len(links), 2)}))
ORDER = (
    ("products", 0), ("p", 0), ("products", 1), ("p", 1), ("p", 0), ("products", 2), ("p", 2), ("p", 1),
    ("p", 2), ("p", 0), ("p", 0), ("terms", 0), ("p", 1), ("sum", 0), ("terms", 1), ("sum", 1), ("gram", 0),
    ("p", 1), ("terms", 2), ("p", 2), ("sum", 2), ("sum", 0), ("sum", 1), ("terms", 3), ("sum", 3),
    ("gram", 1), ("p", 2), ("terms", 4), ("sum", 4), ("sum", 2), ("terms", 5), ("sum", 5), ("sum", 3),
    ("gram", 2), ("gram", 0), ("sum", 4), ("sum", 5), ("sum", 0), ("gram", 1), ("sum", 1), ("gram", 2),
    ("sum", 2), ("sum", 5), ("sum", 4), ("sum", 3), ("sum", 0), ("sum", 1), ("gram", 0), ("gram", 1),
    ("sum", 2), ("gram", 2), ("sum", 4), ("sum", 5), ("gram", 0), ("sum", 3), ("gram", 1), ("sum", 0),
    ("gram", 2), ("sum", 1), ("gram", 0), ("sum", 2), ("gram", 1), ("gram", 2), ("factor", 1), ("factor", 1),
    ("sum", 4), ("sum", 3), ("sum", 5), ("factor", 1), ("sum", 0), ("sum", 1), ("sum", 2), ("factor", 1),
    ("factor", 1), ("factor", 1), ("sum", 4), ("factor", 1), ("sum", 3), ("sum", 5), ("factor", 1),
    ("factor", 1), ("sum", 0), ("factor", 1), ("factor", 1), ("sum", 1), ("sum", 2), ("sum", 0),
    ("factor", 1), ("factor", 1), ("sum", 1), ("factor", 1), ("sum", 4), ("sum", 5), ("sum", 2),
    ("factor", 1), ("sum", 3), ("factor", 1), ("factor", 1), ("factor", 1), ("factor", 1), ("sum", 4),
    ("sum", 5), ("sum", 3),
)
NT = (((1,), (1,)), ((), ()))


def dot(a, b):
    return jnp.dot(a, b, preferred_element_type=f32)


def dot_nt(a, b):
    return lax.dot_general(a, b, NT, preferred_element_type=f32)


def split(x):
    hi = x.astype(bf16)
    return hi, (x - hi.astype(f32)).astype(bf16)


def eliminate(grams, y_ref, p_ref, lhs_err, lhs_q):
    row = lax.broadcasted_iota(jnp.int32, (R, 2 * R), 0)
    lane = lax.broadcasted_iota(jnp.int32, (R, 2 * R), 1)
    eye = jnp.where(lane == row + 64, 1.0, 0.0)
    unit = jnp.where(lane == row, 1.0, 0.0)
    for m in range(8):
        if m < MATS:
            gram = grams[m // 2]
            gram = pltpu.roll(gram, 64, axis=1) if m % 2 else gram
        else:
            gram = unit
        y_ref[pl.ds(m, R, stride=8), :] = jnp.where(lane < 64, gram, eye)
    rows = [y_ref[8 * i : 8 * i + 8] for i in range(R)]

    def at(r, k):
        return jnp.broadcast_to(r[:, k : k + 1], (8, 128))

    for k in range(0, R, 4):
        r0, r1, r2, r3 = rows[k : k + 4]
        s00, s01, s02, s03 = (at(r0, k + i) for i in range(4))
        s11, s12, s13 = (at(r1, k + i) for i in range(1, 4))
        s22, s23, s33 = at(r2, k + 2), at(r2, k + 3), at(r3, k + 3)
        i0 = 1.0 / s00
        l10, l20, l30 = s01 * i0, s02 * i0, s03 * i0
        d1 = s11 - l10 * s01
        t12, t13 = s12 - l10 * s02, s13 - l10 * s03
        i1 = 1.0 / d1
        l21, l31 = t12 * i1, t13 * i1
        d2 = s22 - l20 * s02 - l21 * t12
        t23 = s23 - l20 * s03 - l21 * t13
        i2 = 1.0 / d2
        l32 = t23 * i2
        d3 = s33 - l30 * s03 - l31 * t13 - l32 * t23
        i3 = 1.0 / d3
        r1 = r1 - l10 * r0
        r2 = r2 - l20 * r0 - l21 * r1
        r3 = r3 - l30 * r0 - l31 * r1 - l32 * r2
        q0, q1, q2, q3 = r0 * i0, r1 * i1, r2 * i2, r3 * i3
        for i in range(k + 4, R):
            if i < k + 8:
                c0, c1, c2, c3 = (at(rows[i], k + j) for j in range(4))
                c1 = c1 - l10 * c0
                c2 = c2 - l20 * c0 - l21 * c1
                c3 = c3 - l30 * c0 - l31 * c1 - l32 * c2
            else:
                c0, c1, c2, c3 = at(r0, i), at(r1, i), at(r2, i), at(r3, i)
            rows[i] = rows[i] - (c0 * q0 + c1 * q1) - (c2 * q2 + c3 * q3)
        for i, (r, d) in enumerate(((r0, s00), (r1, d1), (r2, d2), (r3, d3))):
            y_ref[8 * (k + i) : 8 * (k + i) + 8] = r * (1.0 / jnp.sqrt(d))
        yield
    wide_lane = lax.broadcasted_iota(jnp.int32, (ROWS, 2 * R), 1)
    for m in range(MATS):
        side = jnp.where(lane >= 64, y_ref[pl.ds(m, R, stride=8), :], 0.0)
        other = pltpu.roll(side, 64, axis=1)
        inverse = side if m % 2 else other
        bh, bl = split(jnp.concatenate([inverse, inverse], axis=0))
        ph, pl_ = split(p_ref[m // 2])
        ortho = dot_nt(ph, bh) + (dot_nt(ph, bl) + dot_nt(pl_, bh))
        oh, ol = split(ortho)
        lhs_err[m] = jnp.concatenate([jnp.where(wide_lane < 64, oh, ol), oh], axis=1)
        lh, ll = split(side + other)
        lhs_q[m] = jnp.concatenate([jnp.where(lane < 64, lh, ll), lh], axis=1)
        if m % 2:
            yield


def comm_kernel(
    g_hbm, e_hbm, q_hbm, g_sum, lhs_err, lhs_q, ebuf,
    p_out, y_out, gbuf, qbuf, mh, ml, qst, p_own, p_recv, p_chip, p_far, g_acc,
    core_recv, recv1, q_acc, x_acc, recv2, recv3, gram_own, gram_half, gram_recv, gram_out,
    load_sem, p_send, p_arrive, c_send, c_arrive, a_send, a_arrive,
    gram_send, gram_arrive,
):
    dp, mp = lax.axis_index("dp"), lax.axis_index("mp")
    y_hi, core = lax.div(dp, 2), lax.rem(dp, 2)
    x = lax.rem(mp, 4)
    z = lax.rem(lax.div(mp, 4), 4)
    y = y_hi * 2 + lax.div(mp, 16)

    def device(xx, yy, zz, cc):
        return (lax.div(yy, 2) * 2 + cc, lax.rem(yy, 2) * 16 + zz * 4 + xx)

    def flip(v):
        return v + 1 - 2 * lax.rem(v, 2)

    def side0(v):
        hi = lax.div(v, 2)
        lo = lax.rem(v, 2)
        return hi + lo - 2 * hi * lo

    def side1(v):
        return lax.div(v, 2)

    def over(*links):
        xx, yy, zz = x, y, z
        for link in links:
            if link % 3 == 0:
                xx = flip(x) if link == 0 else 3 - x
            elif link % 3 == 1:
                yy = flip(y) if link == 1 else 3 - y
            else:
                zz = flip(z) if link == 2 else 3 - z
        return device(xx, yy, zz, core)

    near = tuple(over(link) for link in range(6))
    corner = {pair: over(*pair) for pair in PAIRS}
    sides = (side0(x), side0(y), side0(z), side1(x), side1(y), side1(z))
    twin = device(x, y, z, 1 - core)
    far = device(x, lax.rem(y + 2, 4), z, core)

    def loads(m):
        return (
            pltpu.make_async_copy(q_hbm.at[m], qbuf.at[m], load_sem.at[m, 0]),
            pltpu.make_async_copy(g_hbm.at[0, m], gbuf.at[m], load_sem.at[m, 1]),
            pltpu.make_async_copy(e_hbm.at[0, m], ebuf.at[m], load_sem.at[m, 2]),
        )

    def begin(m, _):
        for copy in loads(m):
            copy.start()
        return 0

    lax.fori_loop(0, MATS, begin, 0)
    barrier = pltpu.get_barrier_semaphore()
    everyone = near + tuple(corner.values()) + (twin, far)
    for other in everyone:
        pl.semaphore_signal(barrier, inc=1, device_id=other, device_id_type=MESH)

    sent = []

    def remote(src, dst, send, arrive, target):
        copy = pltpu.make_async_remote_copy(
            src_ref=src, dst_ref=dst, send_sem=send, recv_sem=arrive,
            device_id=target, device_id_type=MESH,
        )
        copy.start()
        sent.append(copy)
        return copy

    mine = pl.multiple_of(core * HALF, 8)
    theirs = pl.multiple_of((1 - core) * HALF, 8)
    qst[...] = jnp.zeros_like(qst)
    q_acc[...] = jnp.zeros_like(q_acc)

    def arrive(m):
        for copy in loads(m):
            copy.wait()

    def merge(m):
        for r in range(0, ROWS, 32):
            rows = slice(r, r + 32)
            merged = gbuf[m, rows].astype(f32) + ebuf[m, rows]
            ebuf[m, rows] = merged
            hi, lo = split(merged)
            mh[m, rows] = hi
            ml[m, rows] = lo
        b = m % 2
        hi, lo = split(qbuf[m])
        qst[b, 64 * b : 64 * b + 64] = hi
        qst[b, 128 + 64 * b : 192 + 64 * b] = lo

    def local_p(j):
        if j == 0:
            arrive(0)
            merge(0)
        total = None
        for m in (2 * j, 2 * j + 1):
            if m + 1 < MATS:
                arrive(m + 1)
            wide = dot_nt(mh[m], qst[m % 2])
            part = wide[:, :128] + wide[:, 128:] + dot_nt(ml[m], qst[m % 2, :128])
            if m + 1 < MATS:
                merge(m + 1)
            total = part if total is None else total + part
        p_own[j] = total

    def p_copy(s, j):
        if s == 0:
            src, dst, target = p_own.at[j, pl.ds(theirs, HALF)], p_recv.at[j], twin
        elif s == 1:
            src, dst, target = p_chip.at[j], p_far.at[j], far
        else:
            src = dst = p_out.at[j, pl.ds(mine, HALF)]
            target = twin
        return pltpu.make_async_remote_copy(
            src_ref=src, dst_ref=dst, send_sem=p_send.at[s, j], recv_sem=p_arrive.at[s, j],
            device_id=target, device_id_type=MESH,
        )

    def p_step(s, j):
        if s > 0:
            p_copy(s - 1, j).wait_recv()
        if s == 1:
            p_chip[j] = p_own[j, pl.ds(mine, HALF)] + p_recv[j]
        if s == 2:
            p_out[j, pl.ds(mine, HALF)] = (p_chip[j] + p_far[j]) * 0.25
        if s < 3:
            p_copy(s, j).start()

    halves = {}

    def transposed(j):
        if j not in halves:
            halves[j] = split(p_out[j].T)
        return halves[j]

    def three(src, dst, send, arrive, a, b):
        targets = (near[b], near[a], corner[min(a, b), max(a, b)])
        return [remote(src(f), dst(f), send.at[f], arrive.at[f], targets[f]) for f in range(3)]

    def gram_chain(j):
        hi, lo = transposed(j)
        square = dot_nt(hi, hi) + (dot_nt(hi, lo) + dot_nt(lo, hi))
        lane = lax.broadcasted_iota(jnp.int32, (R, 2 * R), 1)
        gram_own[j] = jnp.where(lane < 64, square[:64], square[64:])
        rows = pl.ds(pl.multiple_of(core * 32, 32), 32)
        gram_half[j, 0] = gram_own[j, rows]
        for s, (one, two) in enumerate(GRAM_PAIRS if j % 2 == 0 else GRAM_PAIRS[::-1]):
            copies = three(
                lambda f: gram_half.at[j, s], lambda f: gram_recv.at[j, s, f], gram_send.at[j, s], gram_arrive.at[j, s],
                one, two,
            )
            yield
            for copy in copies:
                copy.wait_recv()
            got = gram_recv.at[j, s]
            gram_half[j, s + 1] = (gram_half[j, s] + got[1]) + (got[0] + got[2])
        copy = remote(
            gram_half.at[j, 2], gram_recv.at[j, 2, 0], gram_send.at[j, 2, 0], gram_arrive.at[j, 2, 0], near[1],
        )
        yield
        copy.wait_recv()
        gram_out[j, rows] = gram_half[j, 2] + gram_recv[j, 2, 0]
        part = gram_out.at[j, rows]
        copy = remote(part, part, gram_send.at[j, 2, 1], gram_arrive.at[j, 2, 1], twin)
        yield
        copy.wait_recv()

    def local_g(m):
        j, b = divmod(m, 2)
        hi, lo = transposed(j)
        top = hi[64 * b : 64 * b + 64]
        both = jnp.concatenate([top, lo[64 * b : 64 * b + 64]], axis=0)
        for start, size in COLS:
            cols = slice(start, start + size)
            wide = dot(both, mh[m, :, cols])
            g_acc[m, :, cols] = wide[:64] + wide[64:] + dot(top, ml[m, :, cols])

    def g_chain(m):
        link = LINKS[m]
        keep = pl.multiple_of(core * 32, 32)
        give = pl.multiple_of((1 - core) * 32, 32)

        def both_ways(place, i):
            hi, lo = sides[link[i]], sides[link[i + 1]]
            return place(hi, lo), (place(hi, 1 - lo), place(1 - hi, lo), place(1 - hi, 1 - lo))

        def tile(h, l):
            return pl.ds(pl.multiple_of(core * 32 + (2 * h + l) * 8, 8), 8)

        def block(h, l):
            return pl.ds(pl.multiple_of((2 * h + l) * BLOCK, 128), BLOCK)

        rows, other_rows = both_ways(tile, 0)
        own, others = both_ways(block, 2)

        def send(s, src, dst, i):
            return three(src, dst, a_send.at[s, m], a_arrive.at[s, m], link[i], link[i + 1])

        def wait(copies):
            for copy in copies:
                copy.wait_recv()

        copy = remote(g_acc.at[m, pl.ds(give, 32)], core_recv.at[m], c_send.at[0, m], c_arrive.at[0, m], twin)
        yield
        copy.wait_recv()
        g_acc[m, pl.ds(keep, 32)] += core_recv[m]
        copies = send(0, lambda f: g_acc.at[m, other_rows[f]], lambda f: recv1.at[m, f], 0)
        yield
        wait(copies)
        q_acc[m, :, :D] = (g_acc[m, rows] + recv1[m, 1]) + (recv1[m, 0] + recv1[m, 2])
        copies = send(1, lambda f: q_acc.at[m, :, others[f]], lambda f: recv2.at[m, f], 2)
        yield
        wait(copies)
        x_acc[m] = (q_acc[m, :, own] + recv2[m, 1]) + (recv2[m, 0] + recv2[m, 2])
        copies = send(2, lambda f: x_acc.at[m], lambda f: recv3.at[m, f], 4)
        yield
        wait(copies)
        g_sum[m, rows, own] = (x_acc[m] + recv3[m, 1]) + (recv3[m, 0] + recv3[m, 2])
        part = g_sum.at[m, rows, own]
        copies = send(3, lambda f: part, lambda f: part, 2)
        yield
        wait(copies)
        whole = g_sum.at[m, rows, pl.ds(0, D)]
        copies = send(4, lambda f: whole, lambda f: whole, 0)
        yield
        wait(copies)
        half = g_sum.at[m, pl.ds(keep, 32), pl.ds(0, D)]
        copy = remote(half, half, c_send.at[1, m], c_arrive.at[1, m], twin)
        yield
        copy.wait_recv()

    gc = [gram_chain(j) for j in range(3)]
    ac = [g_chain(m) for m in range(MATS)]
    factor = None

    p_stage = [0, 0, 0]
    for what, i in ORDER:
        if what == "products":
            local_p(i)
            if i == 0:
                pl.semaphore_wait(barrier, len(everyone))
        elif what == "p":
            p_step(p_stage[i], i)
            p_stage[i] += 1
        elif what == "gram":
            next(gc[i], None)
        elif what == "terms":
            local_g(i)
        elif what == "sum":
            next(ac[i], None)
        else:
            if factor is None:
                factor = eliminate([gram_out[j] for j in range(3)], y_out, p_out, lhs_err, lhs_q)
            for _ in range(i):
                next(factor, None)
    for _ in factor:
        pass
    for s in range(3):
        for j in range(3):
            p_copy(s, j).wait_send()
    for copy in sent:
        copy.wait_send()


def finish_kernel(g_sum, lhs_err, lhs_q, m_ref, err_hbm, q_out, ebuf, new_q, wst, store_sem, q_sem):
    stores = []

    def fresh(m):
        gh, gl = split(g_sum[m, :, :D] * 0.25)
        wst[m % 2, 0, 0:64] = gh
        wst[m % 2, 0, 64:128] = gh
        wst[m % 2, 0, 128:192] = gl
        value = dot(lhs_q[m, :, :192], wst[m % 2, 0])
        new_q[m] = value
        store = pltpu.make_async_copy(new_q.at[m], q_out.at[m], q_sem.at[m])
        store.start()
        stores.append(store)
        nh, nl = split(value)
        wst[m % 2, 1, 0:64] = nh
        wst[m % 2, 1, 64:128] = nh
        wst[m % 2, 1, 128:192] = nl

    fresh(0)
    for m in range(MATS):
        if m + 1 < MATS:
            fresh(m + 1)
        for i, (start, size) in enumerate(COLS):
            cols = slice(start, start + size)
            ebuf[m, :, cols] = m_ref[m, :, cols] - dot(lhs_err[m, :, :192], wst[m % 2, 1, :, cols])
            place = pl.ds(start, size)
            store = pltpu.make_async_copy(
                ebuf.at[m, :, place], err_hbm.at[0, m, :, place], store_sem.at[m, i]
            )
            store.start()
            stores.append(store)
    for store in stores:
        store.wait()


def body(gradients, errors, previous_q):
    vmem = pl.BlockSpec(memory_space=pltpu.VMEM)
    far_hbm = pl.BlockSpec(memory_space=pltpu.HBM)
    sem = pltpu.SemaphoreType.DMA
    g_sum, lhs_err, lhs_q, merged = pl.pallas_call(
        comm_kernel,
        out_shape=(
            jax.ShapeDtypeStruct((MATS, R, 4 * BLOCK), f32),
            jax.ShapeDtypeStruct((MATS, ROWS, 256), bf16),
            jax.ShapeDtypeStruct((MATS, R, 256), bf16),
            jax.ShapeDtypeStruct((MATS, ROWS, D), f32),
        ),
        in_specs=[far_hbm, far_hbm, far_hbm],
        out_specs=(vmem, vmem, vmem, vmem),
        scratch_shapes=[
            pltpu.VMEM((MATS // 2, ROWS, 2 * R), f32),
            pltpu.VMEM((8 * R, 2 * R), f32),
            pltpu.VMEM((MATS, ROWS, D), bf16),
            pltpu.VMEM((MATS, R, D), f32),
            pltpu.VMEM((MATS, ROWS, D), bf16),
            pltpu.VMEM((MATS, ROWS, D), bf16),
            pltpu.VMEM((2, 256, D), bf16),
            pltpu.VMEM((MATS // 2, ROWS, 128), f32),
            pltpu.VMEM((MATS // 2, HALF, 128), f32),
            pltpu.VMEM((MATS // 2, HALF, 128), f32),
            pltpu.VMEM((MATS // 2, HALF, 128), f32),
            pltpu.VMEM((MATS, R, D), f32),
            pltpu.VMEM((MATS, 32, D), f32),
            pltpu.VMEM((MATS, 3, 8, D), f32),
            pltpu.VMEM((MATS, 8, 4 * BLOCK), f32),
            pltpu.VMEM((MATS, 8, BLOCK), f32),
            pltpu.VMEM((MATS, 3, 8, BLOCK), f32),
            pltpu.VMEM((MATS, 3, 8, BLOCK), f32),
            pltpu.VMEM((MATS // 2, R, 2 * R), f32),
            pltpu.VMEM((MATS // 2, 3, R // 2, 2 * R), f32),
            pltpu.VMEM((MATS // 2, 3, 3, R // 2, 2 * R), f32),
            pltpu.VMEM((MATS // 2, R, 2 * R), f32),
            sem((MATS, 3)),
            sem((3, 3)),
            sem((3, 3)),
            sem((2, MATS)),
            sem((2, MATS)),
            sem((5, MATS, 3)),
            sem((5, MATS, 3)),
            sem((3, 3, 3)),
            sem((3, 3, 3)),
        ],
        compiler_params=pltpu.CompilerParams(
            collective_id=0, has_side_effects=True, vmem_limit_bytes=40 * 2**20
        ),
        name="compress_and_sum",
    )(*[pltpu.with_memory_space_constraint(v, pltpu.HBM) for v in (gradients, errors, previous_q)])
    return pl.pallas_call(
        finish_kernel,
        out_shape=(
            jax.ShapeDtypeStruct((1, MATS, ROWS, D), f32),
            jax.ShapeDtypeStruct((MATS, R, D), f32),
        ),
        in_specs=[vmem, vmem, vmem, vmem],
        out_specs=(far_hbm, far_hbm),
        scratch_shapes=[
            pltpu.VMEM((MATS, ROWS, D), f32),
            pltpu.VMEM((MATS, R, D), f32),
            pltpu.VMEM((2, 2, ROWS, D), bf16),
            sem((MATS, 3)),
            sem((MATS,)),
        ],
        compiler_params=pltpu.CompilerParams(vmem_limit_bytes=24 * 2**20),
        name="new_q_and_errors",
    )(g_sum, lhs_err, lhs_q, merged)


def solution(mesh):
    in_specs = (P("dp", None, "mp", None), P("dp", None, "mp", None), P())
    out_specs = (P("dp", None, "mp", None), P())
    return jax.shard_map(body, mesh=mesh, in_specs=in_specs, out_specs=out_specs, check_vma=False)
```

```python
import functools

import jax
import jax.numpy as jnp
from jax import lax
from jax.experimental import pallas as pl
from jax.experimental.pallas import tpu as pltpu
from jax.sharding import PartitionSpec as P

MESH = pl.DeviceIdType.MESH
MATS, ROWS, D, R = 6, 192, 1408, 64
HALF = ROWS // 2
BLOCK = 384
LAG = 16
COLS = ((0, 512), (512, 512), (1024, 384))
f32, bf16 = jnp.float32, jnp.bfloat16
LINKS = (
    (1, 2, 4, 3, 5, 0),
    (3, 4, 1, 2, 5, 0),
    (0, 5, 1, 2, 4, 3),
    (0, 5, 3, 4, 2, 1),
    (4, 3, 2, 1, 0, 5),
    (2, 1, 5, 0, 3, 4),
)
GRAM_PAIRS = ((2, 3), (5, 0))
PAIRS = tuple(sorted({tuple(sorted(links[i : i + 2])) for links in LINKS + GRAM_PAIRS for i in range(0, len(links), 2)}))
ORDER = (
    ("products", 0), ("p", 0), ("products", 1), ("p", 1), ("p", 0), ("products", 2), ("p", 2), ("p", 1),
    ("p", 2), ("p", 0), ("p", 0), ("terms", 0), ("p", 1), ("sum", 0), ("terms", 1), ("sum", 1), ("gram", 0),
    ("p", 1), ("terms", 2), ("p", 2), ("sum", 2), ("sum", 0), ("sum", 1), ("terms", 3), ("sum", 3),
    ("gram", 1), ("p", 2), ("terms", 4), ("sum", 4), ("sum", 2), ("terms", 5), ("sum", 5), ("sum", 3),
    ("gram", 2), ("gram", 0), ("sum", 4), ("sum", 5), ("sum", 0), ("gram", 1), ("sum", 1), ("gram", 2),
    ("sum", 2), ("sum", 5), ("sum", 4), ("sum", 3), ("sum", 0), ("sum", 1), ("gram", 0), ("gram", 1),
    ("sum", 2), ("gram", 2), ("sum", 4), ("sum", 5), ("gram", 0), ("sum", 3), ("gram", 1), ("sum", 0),
    ("gram", 2), ("sum", 1), ("gram", 0), ("sum", 2), ("gram", 1), ("gram", 2), ("factor", 1), ("factor", 1),
    ("sum", 4), ("sum", 3), ("sum", 5), ("factor", 1), ("sum", 0), ("sum", 1), ("sum", 2), ("factor", 1),
    ("factor", 1), ("factor", 1), ("sum", 4), ("factor", 1), ("sum", 3), ("sum", 5), ("factor", 1),
    ("factor", 1), ("sum", 0), ("factor", 1), ("factor", 1), ("sum", 1), ("sum", 2), ("sum", 0),
    ("factor", 1), ("factor", 1), ("sum", 1), ("factor", 1), ("sum", 4), ("sum", 5), ("sum", 2),
    ("factor", 1), ("sum", 3), ("factor", 1), ("factor", 1), ("factor", 1), ("factor", 1), ("sum", 4),
    ("sum", 5), ("sum", 3),
)
NT = (((1,), (1,)), ((), ()))


def dot(a, b):
    return jnp.dot(a, b, preferred_element_type=f32)


def dot_nt(a, b):
    return lax.dot_general(a, b, NT, preferred_element_type=f32)


def split(x):
    hi = x.astype(bf16)
    return hi, (x - hi.astype(f32)).astype(bf16)


def eliminate(grams, y_ref, p_ref, lhs_err, lhs_q):
    row = lax.broadcasted_iota(jnp.int32, (R, 2 * R), 0)
    lane = lax.broadcasted_iota(jnp.int32, (R, 2 * R), 1)
    eye = jnp.where(lane == row + 64, 1.0, 0.0)
    unit = jnp.where(lane == row, 1.0, 0.0)
    for m in range(8):
        if m < MATS:
            gram = grams[m // 2]
            gram = pltpu.roll(gram, 64, axis=1) if m % 2 else gram
        else:
            gram = unit
        y_ref[pl.ds(m, R, stride=8), :] = jnp.where(lane < 64, gram, eye)
    rows = [y_ref[8 * i : 8 * i + 8] for i in range(R)]

    def at(r, k):
        return jnp.broadcast_to(r[:, k : k + 1], (8, 128))

    for k in range(0, R, 4):
        r0, r1, r2, r3 = rows[k : k + 4]
        s00, s01, s02, s03 = (at(r0, k + i) for i in range(4))
        s11, s12, s13 = (at(r1, k + i) for i in range(1, 4))
        s22, s23, s33 = at(r2, k + 2), at(r2, k + 3), at(r3, k + 3)
        i0 = 1.0 / s00
        l10, l20, l30 = s01 * i0, s02 * i0, s03 * i0
        d1 = s11 - l10 * s01
        t12, t13 = s12 - l10 * s02, s13 - l10 * s03
        i1 = 1.0 / d1
        l21, l31 = t12 * i1, t13 * i1
        d2 = s22 - l20 * s02 - l21 * t12
        t23 = s23 - l20 * s03 - l21 * t13
        i2 = 1.0 / d2
        l32 = t23 * i2
        d3 = s33 - l30 * s03 - l31 * t13 - l32 * t23
        i3 = 1.0 / d3
        r1 = r1 - l10 * r0
        r2 = r2 - l20 * r0 - l21 * r1
        r3 = r3 - l30 * r0 - l31 * r1 - l32 * r2
        q0, q1, q2, q3 = r0 * i0, r1 * i1, r2 * i2, r3 * i3
        for i in range(k + 4, R):
            if i < k + 8:
                c0, c1, c2, c3 = (at(rows[i], k + j) for j in range(4))
                c1 = c1 - l10 * c0
                c2 = c2 - l20 * c0 - l21 * c1
                c3 = c3 - l30 * c0 - l31 * c1 - l32 * c2
            else:
                c0, c1, c2, c3 = at(r0, i), at(r1, i), at(r2, i), at(r3, i)
            rows[i] = rows[i] - (c0 * q0 + c1 * q1) - (c2 * q2 + c3 * q3)
        for i, (r, d) in enumerate(((r0, s00), (r1, d1), (r2, d2), (r3, d3))):
            y_ref[8 * (k + i) : 8 * (k + i) + 8] = r * (1.0 / jnp.sqrt(d))
        yield
    wide_lane = lax.broadcasted_iota(jnp.int32, (ROWS, 2 * R), 1)
    for m in range(MATS):
        side = jnp.where(lane >= 64, y_ref[pl.ds(m, R, stride=8), :], 0.0)
        other = pltpu.roll(side, 64, axis=1)
        inverse = side if m % 2 else other
        bh, bl = split(jnp.concatenate([inverse, inverse], axis=0))
        ph, pl_ = split(p_ref[m // 2])
        ortho = dot_nt(ph, bh) + (dot_nt(ph, bl) + dot_nt(pl_, bh))
        oh, ol = split(ortho)
        lhs_err[m] = jnp.concatenate([jnp.where(wide_lane < 64, oh, ol), oh], axis=1)
        lh, ll = split(side + other)
        lhs_q[m] = jnp.concatenate([jnp.where(lane < 64, lh, ll), lh], axis=1)
        if m % 2:
            yield


def comm_kernel(
    g_hbm, e_hbm, q_hbm, g_sum, lhs_err, lhs_q, ebuf,
    p_out, y_out, gbuf, qbuf, mh, ml, qst, p_own, p_recv, p_chip, p_far, g_acc,
    core_recv, recv1, q_acc, x_acc, recv2, recv3, gram_own, gram_half, gram_recv, gram_out,
    load_sem, p_send, p_arrive, c_send, c_arrive, a_send, a_arrive,
    gram_send, gram_arrive,
):
    dp, mp = lax.axis_index("dp"), lax.axis_index("mp")
    y_hi, core = lax.div(dp, 2), lax.rem(dp, 2)
    x = lax.rem(mp, 4)
    z = lax.rem(lax.div(mp, 4), 4)
    y = y_hi * 2 + lax.div(mp, 16)

    def device(xx, yy, zz, cc):
        return (lax.div(yy, 2) * 2 + cc, lax.rem(yy, 2) * 16 + zz * 4 + xx)

    def flip(v):
        return v + 1 - 2 * lax.rem(v, 2)

    def side0(v):
        hi = lax.div(v, 2)
        lo = lax.rem(v, 2)
        return hi + lo - 2 * hi * lo

    def side1(v):
        return lax.div(v, 2)

    def over(*links):
        xx, yy, zz = x, y, z
        for link in links:
            if link % 3 == 0:
                xx = flip(x) if link == 0 else 3 - x
            elif link % 3 == 1:
                yy = flip(y) if link == 1 else 3 - y
            else:
                zz = flip(z) if link == 2 else 3 - z
        return device(xx, yy, zz, core)

    near = tuple(over(link) for link in range(6))
    corner = {pair: over(*pair) for pair in PAIRS}
    sides = (side0(x), side0(y), side0(z), side1(x), side1(y), side1(z))
    twin = device(x, y, z, 1 - core)
    far = device(x, lax.rem(y + 2, 4), z, core)

    def loads(m):
        return (
            pltpu.make_async_copy(q_hbm.at[m], qbuf.at[m], load_sem.at[m, 0]),
            pltpu.make_async_copy(g_hbm.at[0, m], gbuf.at[m], load_sem.at[m, 1]),
            pltpu.make_async_copy(e_hbm.at[0, m], ebuf.at[m], load_sem.at[m, 2]),
        )

    def begin(m, _):
        for copy in loads(m):
            copy.start()
        return 0

    lax.fori_loop(0, MATS, begin, 0)
    barrier = pltpu.get_barrier_semaphore()
    everyone = near + tuple(corner.values()) + (twin, far)
    for other in everyone:
        pl.semaphore_signal(barrier, inc=1, device_id=other, device_id_type=MESH)

    sent = []
    step = 0

    def remote(src, dst, send, arrive, target):
        copy = pltpu.make_async_remote_copy(
            src_ref=src, dst_ref=dst, send_sem=send, recv_sem=arrive,
            device_id=target, device_id_type=MESH,
        )
        copy.start()
        sent.append((step, copy))
        return copy

    mine = pl.multiple_of(core * HALF, 8)
    theirs = pl.multiple_of((1 - core) * HALF, 8)
    qst[...] = jnp.zeros_like(qst)
    q_acc[...] = jnp.zeros_like(q_acc)

    def arrive(m):
        for copy in loads(m):
            copy.wait()

    def merge(m):
        for r in range(0, ROWS, 32):
            rows = slice(r, r + 32)
            merged = gbuf[m, rows].astype(f32) + ebuf[m, rows]
            ebuf[m, rows] = merged
            hi, lo = split(merged)
            mh[m, rows] = hi
            ml[m, rows] = lo
        b = m % 2
        hi, lo = split(qbuf[m])
        qst[b, 64 * b : 64 * b + 64] = hi
        qst[b, 128 + 64 * b : 192 + 64 * b] = lo

    def local_p(j):
        if j == 0:
            arrive(0)
            merge(0)
        total = None
        for m in (2 * j, 2 * j + 1):
            if m + 1 < MATS:
                arrive(m + 1)
            wide = dot_nt(mh[m], qst[m % 2])
            part = wide[:, :128] + wide[:, 128:] + dot_nt(ml[m], qst[m % 2, :128])
            if m + 1 < MATS:
                merge(m + 1)
            total = part if total is None else total + part
        p_own[j] = total

    def p_copy(s, j):
        if s == 0:
            src, dst, target = p_own.at[j, pl.ds(theirs, HALF)], p_recv.at[j], twin
        elif s == 1:
            src, dst, target = p_chip.at[j], p_far.at[j], far
        else:
            src = dst = p_out.at[j, pl.ds(mine, HALF)]
            target = twin
        return pltpu.make_async_remote_copy(
            src_ref=src, dst_ref=dst, send_sem=p_send.at[s, j], recv_sem=p_arrive.at[s, j],
            device_id=target, device_id_type=MESH,
        )

    def p_step(s, j):
        if s > 0:
            p_copy(s - 1, j).wait_recv()
        if s == 1:
            p_chip[j] = p_own[j, pl.ds(mine, HALF)] + p_recv[j]
        if s == 2:
            p_out[j, pl.ds(mine, HALF)] = (p_chip[j] + p_far[j]) * 0.25
        if s < 3:
            p_copy(s, j).start()

    halves = {}

    def transposed(j):
        if j not in halves:
            halves[j] = split(p_out[j].T)
        return halves[j]

    def three(src, dst, send, arrive, a, b):
        targets = (near[b], near[a], corner[min(a, b), max(a, b)])
        return [remote(src(f), dst(f), send.at[f], arrive.at[f], targets[f]) for f in range(3)]

    def gram_chain(j):
        hi, lo = transposed(j)
        square = dot_nt(hi, hi) + (dot_nt(hi, lo) + dot_nt(lo, hi))
        lane = lax.broadcasted_iota(jnp.int32, (R, 2 * R), 1)
        gram_own[j] = jnp.where(lane < 64, square[:64], square[64:])
        rows = pl.ds(pl.multiple_of(core * 32, 32), 32)
        gram_half[j, 0] = gram_own[j, rows]
        for s, (one, two) in enumerate(GRAM_PAIRS if j % 2 == 0 else GRAM_PAIRS[::-1]):
            copies = three(
                lambda f: gram_half.at[j, s], lambda f: gram_recv.at[j, s, f], gram_send.at[j, s], gram_arrive.at[j, s],
                one, two,
            )
            yield
            for copy in copies:
                copy.wait_recv()
            got = gram_recv.at[j, s]
            gram_half[j, s + 1] = (gram_half[j, s] + got[1]) + (got[0] + got[2])
        copy = remote(
            gram_half.at[j, 2], gram_recv.at[j, 2, 0], gram_send.at[j, 2, 0], gram_arrive.at[j, 2, 0], near[1],
        )
        yield
        copy.wait_recv()
        gram_out[j, rows] = gram_half[j, 2] + gram_recv[j, 2, 0]
        part = gram_out.at[j, rows]
        copy = remote(part, part, gram_send.at[j, 2, 1], gram_arrive.at[j, 2, 1], twin)
        yield
        copy.wait_recv()

    def local_g(m):
        j, b = divmod(m, 2)
        hi, lo = transposed(j)
        top = hi[64 * b : 64 * b + 64]
        both = jnp.concatenate([top, lo[64 * b : 64 * b + 64]], axis=0)
        for start, size in COLS:
            cols = slice(start, start + size)
            wide = dot(both, mh[m, :, cols])
            g_acc[m, :, cols] = wide[:64] + wide[64:] + dot(top, ml[m, :, cols])

    def g_chain(m):
        link = LINKS[m]
        keep = pl.multiple_of(core * 32, 32)
        give = pl.multiple_of((1 - core) * 32, 32)

        def both_ways(place, i):
            hi, lo = sides[link[i]], sides[link[i + 1]]
            return place(hi, lo), (place(hi, 1 - lo), place(1 - hi, lo), place(1 - hi, 1 - lo))

        def tile(h, l):
            return pl.ds(pl.multiple_of(core * 32 + (2 * h + l) * 8, 8), 8)

        def block(h, l):
            return pl.ds(pl.multiple_of((2 * h + l) * BLOCK, 128), BLOCK)

        rows, other_rows = both_ways(tile, 0)
        own, others = both_ways(block, 2)

        def send(s, src, dst, i):
            return three(src, dst, a_send.at[s, m], a_arrive.at[s, m], link[i], link[i + 1])

        def wait(copies):
            for copy in copies:
                copy.wait_recv()

        copy = remote(g_acc.at[m, pl.ds(give, 32)], core_recv.at[m], c_send.at[0, m], c_arrive.at[0, m], twin)
        yield
        copy.wait_recv()
        g_acc[m, pl.ds(keep, 32)] += core_recv[m]
        copies = send(0, lambda f: g_acc.at[m, other_rows[f]], lambda f: recv1.at[m, f], 0)
        yield
        wait(copies)
        q_acc[m, :, :D] = (g_acc[m, rows] + recv1[m, 1]) + (recv1[m, 0] + recv1[m, 2])
        copies = send(1, lambda f: q_acc.at[m, :, others[f]], lambda f: recv2.at[m, f], 2)
        yield
        wait(copies)
        x_acc[m] = (q_acc[m, :, own] + recv2[m, 1]) + (recv2[m, 0] + recv2[m, 2])
        copies = send(2, lambda f: x_acc.at[m], lambda f: recv3.at[m, f], 4)
        yield
        wait(copies)
        g_sum[m, rows, own] = (x_acc[m] + recv3[m, 1]) + (recv3[m, 0] + recv3[m, 2])
        part = g_sum.at[m, rows, own]
        copies = send(3, lambda f: part, lambda f: part, 2)
        yield
        wait(copies)
        whole = g_sum.at[m, rows, pl.ds(0, D)]
        copies = send(4, lambda f: whole, lambda f: whole, 0)
        yield
        wait(copies)
        half = g_sum.at[m, pl.ds(keep, 32), pl.ds(0, D)]
        copy = remote(half, half, c_send.at[1, m], c_arrive.at[1, m], twin)
        yield
        copy.wait_recv()

    gc = [gram_chain(j) for j in range(3)]
    ac = [g_chain(m) for m in range(MATS)]
    factor = None

    p_stage = [0, 0, 0]
    for step, (what, i) in enumerate(ORDER):
        while sent and sent[0][0] <= step - LAG:
            sent.pop(0)[1].wait_send()
        if what == "products":
            local_p(i)
            if i == 0:
                pl.semaphore_wait(barrier, len(everyone))
        elif what == "p":
            p_step(p_stage[i], i)
            p_stage[i] += 1
            if p_stage[i] == 4:
                for k in range(3):
                    p_copy(k, i).wait_send()
        elif what == "gram":
            next(gc[i], None)
        elif what == "terms":
            local_g(i)
        elif what == "sum":
            next(ac[i], None)
        else:
            if factor is None:
                factor = eliminate([gram_out[j] for j in range(3)], y_out, p_out, lhs_err, lhs_q)
            for _ in range(i):
                next(factor, None)
    for _ in factor:
        pass
    for _, copy in sent:
        copy.wait_send()


def finish_kernel(g_sum, lhs_err, lhs_q, m_ref, err_hbm, q_out, ebuf, new_q, wst, store_sem, q_sem):
    stores = []
    for m in range(MATS):
        gh, gl = split(g_sum[m, :, :D] * 0.25)
        wst[0, 0:64] = gh
        wst[0, 64:128] = gh
        wst[0, 128:192] = gl
        fresh = dot(lhs_q[m, :, :192], wst[0])
        new_q[m] = fresh
        store = pltpu.make_async_copy(new_q.at[m], q_out.at[m], q_sem.at[m])
        store.start()
        stores.append(store)
        nh, nl = split(fresh)
        wst[1, 0:64] = nh
        wst[1, 64:128] = nh
        wst[1, 128:192] = nl
        for i, (start, size) in enumerate(COLS):
            cols = slice(start, start + size)
            ebuf[m, :, cols] = m_ref[m, :, cols] - dot(lhs_err[m, :, :192], wst[1, :, cols])
            place = pl.ds(start, size)
            store = pltpu.make_async_copy(
                ebuf.at[m, :, place], err_hbm.at[0, m, :, place], store_sem.at[m, i]
            )
            store.start()
            stores.append(store)
    for store in stores:
        store.wait()


def body(gradients, errors, previous_q):
    vmem = pl.BlockSpec(memory_space=pltpu.VMEM)
    far_hbm = pl.BlockSpec(memory_space=pltpu.HBM)
    sem = pltpu.SemaphoreType.DMA
    g_sum, lhs_err, lhs_q, merged = pl.pallas_call(
        comm_kernel,
        out_shape=(
            jax.ShapeDtypeStruct((MATS, R, 4 * BLOCK), f32),
            jax.ShapeDtypeStruct((MATS, ROWS, 256), bf16),
            jax.ShapeDtypeStruct((MATS, R, 256), bf16),
            jax.ShapeDtypeStruct((MATS, ROWS, D), f32),
        ),
        in_specs=[far_hbm, far_hbm, far_hbm],
        out_specs=(vmem, vmem, vmem, vmem),
        scratch_shapes=[
            pltpu.VMEM((MATS // 2, ROWS, 2 * R), f32),
            pltpu.VMEM((8 * R, 2 * R), f32),
            pltpu.VMEM((MATS, ROWS, D), bf16),
            pltpu.VMEM((MATS, R, D), f32),
            pltpu.VMEM((MATS, ROWS, D), bf16),
            pltpu.VMEM((MATS, ROWS, D), bf16),
            pltpu.VMEM((2, 256, D), bf16),
            pltpu.VMEM((MATS // 2, ROWS, 128), f32),
            pltpu.VMEM((MATS // 2, HALF, 128), f32),
            pltpu.VMEM((MATS // 2, HALF, 128), f32),
            pltpu.VMEM((MATS // 2, HALF, 128), f32),
            pltpu.VMEM((MATS, R, D), f32),
            pltpu.VMEM((MATS, 32, D), f32),
            pltpu.VMEM((MATS, 3, 8, D), f32),
            pltpu.VMEM((MATS, 8, 4 * BLOCK), f32),
            pltpu.VMEM((MATS, 8, BLOCK), f32),
            pltpu.VMEM((MATS, 3, 8, BLOCK), f32),
            pltpu.VMEM((MATS, 3, 8, BLOCK), f32),
            pltpu.VMEM((MATS // 2, R, 2 * R), f32),
            pltpu.VMEM((MATS // 2, 3, R // 2, 2 * R), f32),
            pltpu.VMEM((MATS // 2, 3, 3, R // 2, 2 * R), f32),
            pltpu.VMEM((MATS // 2, R, 2 * R), f32),
            sem((MATS, 3)),
            sem((3, 3)),
            sem((3, 3)),
            sem((2, MATS)),
            sem((2, MATS)),
            sem((5, MATS, 3)),
            sem((5, MATS, 3)),
            sem((3, 3, 3)),
            sem((3, 3, 3)),
        ],
        compiler_params=pltpu.CompilerParams(
            collective_id=0, has_side_effects=True, vmem_limit_bytes=40 * 2**20
        ),
        name="compress_and_sum",
    )(*[pltpu.with_memory_space_constraint(v, pltpu.HBM) for v in (gradients, errors, previous_q)])
    return pl.pallas_call(
        finish_kernel,
        out_shape=(
            jax.ShapeDtypeStruct((1, MATS, ROWS, D), f32),
            jax.ShapeDtypeStruct((MATS, R, D), f32),
        ),
        in_specs=[vmem, vmem, vmem, vmem],
        out_specs=(far_hbm, far_hbm),
        scratch_shapes=[
            pltpu.VMEM((MATS, ROWS, D), f32),
            pltpu.VMEM((MATS, R, D), f32),
            pltpu.VMEM((2, ROWS, D), bf16),
            sem((MATS, 3)),
            sem((MATS,)),
        ],
        compiler_params=pltpu.CompilerParams(vmem_limit_bytes=24 * 2**20),
        name="new_q_and_errors",
    )(g_sum, lhs_err, lhs_q, merged)


def solution(mesh):
    in_specs = (P("dp", None, "mp", None), P("dp", None, "mp", None), P())
    out_specs = (P("dp", None, "mp", None), P())
    return jax.shard_map(body, mesh=mesh, in_specs=in_specs, out_specs=out_specs, check_vma=False)
```

```python
import functools

import jax
import jax.numpy as jnp
from jax import lax
from jax.experimental import pallas as pl
from jax.experimental.pallas import tpu as pltpu
from jax.sharding import PartitionSpec as P

MESH = pl.DeviceIdType.MESH
MATS, ROWS, D, R = 6, 192, 1408, 64
HALF = ROWS // 2
BLOCK = 384
LAG = 16
COLS = ((0, 512), (512, 512), (1024, 384))
f32, bf16 = jnp.float32, jnp.bfloat16
LINKS = (
    (1, 2, 4, 3, 5, 0),
    (3, 4, 1, 2, 5, 0),
    (0, 5, 1, 2, 4, 3),
    (0, 5, 3, 4, 2, 1),
    (4, 3, 2, 1, 0, 5),
    (2, 1, 5, 0, 3, 4),
)
GRAM_PAIRS = ((2, 3), (5, 0))
PAIRS = tuple(sorted({tuple(sorted(links[i : i + 2])) for links in LINKS + GRAM_PAIRS for i in range(0, len(links), 2)}))
ORDER = (
    ("products", 0), ("p", 0), ("products", 1), ("p", 1), ("p", 0), ("products", 2), ("p", 2), ("p", 1),
    ("p", 2), ("p", 0), ("p", 0), ("terms", 0), ("p", 1), ("sum", 0), ("terms", 1), ("sum", 1), ("gram", 0),
    ("p", 1), ("terms", 2), ("p", 2), ("sum", 2), ("sum", 0), ("sum", 1), ("terms", 3), ("sum", 3),
    ("gram", 1), ("p", 2), ("terms", 4), ("sum", 4), ("sum", 2), ("terms", 5), ("sum", 5), ("sum", 3),
    ("gram", 2), ("gram", 0), ("sum", 4), ("sum", 5), ("sum", 0), ("gram", 1), ("sum", 1), ("gram", 2),
    ("sum", 2), ("sum", 5), ("sum", 4), ("sum", 3), ("sum", 0), ("sum", 1), ("gram", 0), ("gram", 1),
    ("sum", 2), ("gram", 2), ("sum", 4), ("sum", 5), ("gram", 0), ("sum", 3), ("gram", 1), ("sum", 0),
    ("gram", 2), ("sum", 1), ("gram", 0), ("sum", 2), ("gram", 1), ("gram", 2), ("factor", 1), ("factor", 1),
    ("sum", 4), ("sum", 3), ("sum", 5), ("factor", 1), ("sum", 0), ("sum", 1), ("sum", 2), ("factor", 1),
    ("factor", 1), ("factor", 1), ("sum", 4), ("factor", 1), ("sum", 3), ("sum", 5), ("factor", 1),
    ("factor", 1), ("sum", 0), ("factor", 1), ("factor", 1), ("sum", 1), ("sum", 2), ("sum", 0),
    ("factor", 1), ("factor", 1), ("sum", 1), ("factor", 1), ("sum", 4), ("sum", 5), ("sum", 2),
    ("factor", 1), ("sum", 3), ("factor", 1), ("factor", 1), ("factor", 1), ("factor", 1), ("sum", 4),
    ("sum", 5), ("sum", 3),
)
NT = (((1,), (1,)), ((), ()))


def dot(a, b):
    return jnp.dot(a, b, preferred_element_type=f32)


def dot_nt(a, b):
    return lax.dot_general(a, b, NT, preferred_element_type=f32)


def split(x):
    hi = x.astype(bf16)
    return hi, (x - hi.astype(f32)).astype(bf16)


def eliminate(grams, y_ref, p_ref, lhs_err, lhs_q):
    row = lax.broadcasted_iota(jnp.int32, (R, 2 * R), 0)
    lane = lax.broadcasted_iota(jnp.int32, (R, 2 * R), 1)
    eye = jnp.where(lane == row + 64, 1.0, 0.0)
    unit = jnp.where(lane == row, 1.0, 0.0)
    for m in range(8):
        if m < MATS:
            gram = grams[m // 2]
            gram = pltpu.roll(gram, 64, axis=1) if m % 2 else gram
        else:
            gram = unit
        y_ref[pl.ds(m, R, stride=8), :] = jnp.where(lane < 64, gram, eye)
    rows = [y_ref[8 * i : 8 * i + 8] for i in range(R)]

    def at(r, k):
        return jnp.broadcast_to(r[:, k : k + 1], (8, 128))

    for k in range(0, R, 4):
        r0, r1, r2, r3 = rows[k : k + 4]
        s00, s01, s02, s03 = (at(r0, k + i) for i in range(4))
        s11, s12, s13 = (at(r1, k + i) for i in range(1, 4))
        s22, s23, s33 = at(r2, k + 2), at(r2, k + 3), at(r3, k + 3)
        i0 = 1.0 / s00
        l10, l20, l30 = s01 * i0, s02 * i0, s03 * i0
        d1 = s11 - l10 * s01
        t12, t13 = s12 - l10 * s02, s13 - l10 * s03
        i1 = 1.0 / d1
        l21, l31 = t12 * i1, t13 * i1
        d2 = s22 - l20 * s02 - l21 * t12
        t23 = s23 - l20 * s03 - l21 * t13
        i2 = 1.0 / d2
        l32 = t23 * i2
        d3 = s33 - l30 * s03 - l31 * t13 - l32 * t23
        i3 = 1.0 / d3
        r1 = r1 - l10 * r0
        r2 = r2 - l20 * r0 - l21 * r1
        r3 = r3 - l30 * r0 - l31 * r1 - l32 * r2
        q0, q1, q2, q3 = r0 * i0, r1 * i1, r2 * i2, r3 * i3
        for i in range(k + 4, R):
            if i < k + 8:
                c0, c1, c2, c3 = (at(rows[i], k + j) for j in range(4))
                c1 = c1 - l10 * c0
                c2 = c2 - l20 * c0 - l21 * c1
                c3 = c3 - l30 * c0 - l31 * c1 - l32 * c2
            else:
                c0, c1, c2, c3 = at(r0, i), at(r1, i), at(r2, i), at(r3, i)
            rows[i] = rows[i] - (c0 * q0 + c1 * q1) - (c2 * q2 + c3 * q3)
        for i, (r, d) in enumerate(((r0, s00), (r1, d1), (r2, d2), (r3, d3))):
            y_ref[8 * (k + i) : 8 * (k + i) + 8] = r * (1.0 / jnp.sqrt(d))
        yield
    wide_lane = lax.broadcasted_iota(jnp.int32, (ROWS, 2 * R), 1)
    for m in range(MATS):
        side = jnp.where(lane >= 64, y_ref[pl.ds(m, R, stride=8), :], 0.0)
        other = pltpu.roll(side, 64, axis=1)
        inverse = side if m % 2 else other
        bh, bl = split(jnp.concatenate([inverse, inverse], axis=0))
        ph, pl_ = split(p_ref[m // 2])
        ortho = dot_nt(ph, bh) + (dot_nt(ph, bl) + dot_nt(pl_, bh))
        oh, ol = split(ortho)
        lhs_err[m] = jnp.concatenate([jnp.where(wide_lane < 64, oh, ol), oh], axis=1)
        lh, ll = split(side + other)
        lhs_q[m] = jnp.concatenate([jnp.where(lane < 64, lh, ll), lh], axis=1)
        if m % 2:
            yield


def comm_kernel(
    g_hbm, e_hbm, q_hbm, g_sum, lhs_err, lhs_q, ebuf,
    p_out, y_out, gbuf, qbuf, mh, ml, qst, p_own, p_recv, p_chip, p_far, g_acc,
    core_recv, recv1, q_acc, x_acc, recv2, recv3, gram_own, gram_half, gram_recv, gram_out,
    load_sem, p_send, p_arrive, c_send, c_arrive, a_send, a_arrive,
    gram_send, gram_arrive,
):
    dp, mp = lax.axis_index("dp"), lax.axis_index("mp")
    y_hi, core = lax.div(dp, 2), lax.rem(dp, 2)
    x = lax.rem(mp, 4)
    z = lax.rem(lax.div(mp, 4), 4)
    y = y_hi * 2 + lax.div(mp, 16)

    def device(xx, yy, zz, cc):
        return (lax.div(yy, 2) * 2 + cc, lax.rem(yy, 2) * 16 + zz * 4 + xx)

    def flip(v):
        return v + 1 - 2 * lax.rem(v, 2)

    def side0(v):
        hi = lax.div(v, 2)
        lo = lax.rem(v, 2)
        return hi + lo - 2 * hi * lo

    def side1(v):
        return lax.div(v, 2)

    def over(*links):
        xx, yy, zz = x, y, z
        for link in links:
            if link % 3 == 0:
                xx = flip(x) if link == 0 else 3 - x
            elif link % 3 == 1:
                yy = flip(y) if link == 1 else 3 - y
            else:
                zz = flip(z) if link == 2 else 3 - z
        return device(xx, yy, zz, core)

    near = tuple(over(link) for link in range(6))
    corner = {pair: over(*pair) for pair in PAIRS}
    sides = (side0(x), side0(y), side0(z), side1(x), side1(y), side1(z))
    twin = device(x, y, z, 1 - core)
    far = device(x, lax.rem(y + 2, 4), z, core)

    def loads(m):
        return (
            pltpu.make_async_copy(q_hbm.at[m], qbuf.at[m], load_sem.at[m, 0]),
            pltpu.make_async_copy(g_hbm.at[0, m], gbuf.at[m], load_sem.at[m, 1]),
            pltpu.make_async_copy(e_hbm.at[0, m], ebuf.at[m], load_sem.at[m, 2]),
        )

    def begin(m, _):
        for copy in loads(m):
            copy.start()
        return 0

    lax.fori_loop(0, MATS, begin, 0)
    barrier = pltpu.get_barrier_semaphore()
    everyone = near + tuple(corner.values()) + (twin, far)
    for other in everyone:
        pl.semaphore_signal(barrier, inc=1, device_id=other, device_id_type=MESH)

    sent = []
    step = 0

    def remote(src, dst, send, arrive, target):
        copy = pltpu.make_async_remote_copy(
            src_ref=src, dst_ref=dst, send_sem=send, recv_sem=arrive,
            device_id=target, device_id_type=MESH,
        )
        copy.start()
        sent.append((step, copy))
        return copy

    mine = pl.multiple_of(core * HALF, 8)
    theirs = pl.multiple_of((1 - core) * HALF, 8)
    q_acc[...] = jnp.zeros_like(q_acc)

    def arrive(m):
        for copy in loads(m):
            copy.wait()

    def merge(m):
        for r in range(0, ROWS, 32):
            rows = slice(r, r + 32)
            merged = gbuf[m, rows].astype(f32) + ebuf[m, rows]
            ebuf[m, rows] = merged
            hi, lo = split(merged)
            mh[m, rows] = hi
            ml[m, rows] = lo
        b = m % 2
        hi, lo = split(qbuf[m])
        qst[b, 0:64] = hi
        qst[b, 64:128] = lo
        qst[b, 128:192] = hi
        qst[b, 192:256] = hi

    def local_p(j):
        if j == 0:
            arrive(0)
            merge(0)
        parts = []
        for m in (2 * j, 2 * j + 1):
            if m + 1 < MATS:
                arrive(m + 1)
            wide = dot_nt(mh[m], qst[m % 2, :128])
            parts.append(wide + pltpu.roll(wide, 64, axis=1) + dot_nt(ml[m], qst[m % 2, 128:]))
            if m + 1 < MATS:
                merge(m + 1)
        lane = lax.broadcasted_iota(jnp.int32, (ROWS, 2 * R), 1)
        p_own[j] = jnp.where(lane < 64, parts[0], parts[1])

    def p_copy(s, j):
        if s == 0:
            src, dst, target = p_own.at[j, pl.ds(theirs, HALF)], p_recv.at[j], twin
        elif s == 1:
            src, dst, target = p_chip.at[j], p_far.at[j], far
        else:
            src = dst = p_out.at[j, pl.ds(mine, HALF)]
            target = twin
        return pltpu.make_async_remote_copy(
            src_ref=src, dst_ref=dst, send_sem=p_send.at[s, j], recv_sem=p_arrive.at[s, j],
            device_id=target, device_id_type=MESH,
        )

    def p_step(s, j):
        if s > 0:
            p_copy(s - 1, j).wait_recv()
        if s == 1:
            p_chip[j] = p_own[j, pl.ds(mine, HALF)] + p_recv[j]
        if s == 2:
            p_out[j, pl.ds(mine, HALF)] = (p_chip[j] + p_far[j]) * 0.25
        if s < 3:
            p_copy(s, j).start()

    halves = {}

    def transposed(j):
        if j not in halves:
            halves[j] = split(p_out[j].T)
        return halves[j]

    def three(src, dst, send, arrive, a, b):
        targets = (near[b], near[a], corner[min(a, b), max(a, b)])
        return [remote(src(f), dst(f), send.at[f], arrive.at[f], targets[f]) for f in range(3)]

    def gram_chain(j):
        hi, lo = transposed(j)
        square = dot_nt(hi, hi) + (dot_nt(hi, lo) + dot_nt(lo, hi))
        lane = lax.broadcasted_iota(jnp.int32, (R, 2 * R), 1)
        gram_own[j] = jnp.where(lane < 64, square[:64], square[64:])
        rows = pl.ds(pl.multiple_of(core * 32, 32), 32)
        gram_half[j, 0] = gram_own[j, rows]
        for s, (one, two) in enumerate(GRAM_PAIRS if j % 2 == 0 else GRAM_PAIRS[::-1]):
            copies = three(
                lambda f: gram_half.at[j, s], lambda f: gram_recv.at[j, s, f], gram_send.at[j, s], gram_arrive.at[j, s],
                one, two,
            )
            yield
            for copy in copies:
                copy.wait_recv()
            got = gram_recv.at[j, s]
            gram_half[j, s + 1] = (gram_half[j, s] + got[1]) + (got[0] + got[2])
        copy = remote(
            gram_half.at[j, 2], gram_recv.at[j, 2, 0], gram_send.at[j, 2, 0], gram_arrive.at[j, 2, 0], near[1],
        )
        yield
        copy.wait_recv()
        gram_out[j, rows] = gram_half[j, 2] + gram_recv[j, 2, 0]
        part = gram_out.at[j, rows]
        copy = remote(part, part, gram_send.at[j, 2, 1], gram_arrive.at[j, 2, 1], twin)
        yield
        copy.wait_recv()

    def local_g(m):
        j, b = divmod(m, 2)
        hi, lo = transposed(j)
        top = hi[64 * b : 64 * b + 64]
        both = jnp.concatenate([top, lo[64 * b : 64 * b + 64]], axis=0)
        for start, size in COLS:
            cols = slice(start, start + size)
            wide = dot(both, mh[m, :, cols])
            g_acc[m, :, cols] = wide[:64] + wide[64:] + dot(top, ml[m, :, cols])

    def g_chain(m):
        link = LINKS[m]
        keep = pl.multiple_of(core * 32, 32)
        give = pl.multiple_of((1 - core) * 32, 32)

        def both_ways(place, i):
            hi, lo = sides[link[i]], sides[link[i + 1]]
            return place(hi, lo), (place(hi, 1 - lo), place(1 - hi, lo), place(1 - hi, 1 - lo))

        def tile(h, l):
            return pl.ds(pl.multiple_of(core * 32 + (2 * h + l) * 8, 8), 8)

        def block(h, l):
            return pl.ds(pl.multiple_of((2 * h + l) * BLOCK, 128), BLOCK)

        rows, other_rows = both_ways(tile, 0)
        own, others = both_ways(block, 2)

        def send(s, src, dst, i):
            return three(src, dst, a_send.at[s, m], a_arrive.at[s, m], link[i], link[i + 1])

        def wait(copies):
            for copy in copies:
                copy.wait_recv()

        copy = remote(g_acc.at[m, pl.ds(give, 32)], core_recv.at[m], c_send.at[0, m], c_arrive.at[0, m], twin)
        yield
        copy.wait_recv()
        g_acc[m, pl.ds(keep, 32)] += core_recv[m]
        copies = send(0, lambda f: g_acc.at[m, other_rows[f]], lambda f: recv1.at[m, f], 0)
        yield
        wait(copies)
        q_acc[m, :, :D] = (g_acc[m, rows] + recv1[m, 1]) + (recv1[m, 0] + recv1[m, 2])
        copies = send(1, lambda f: q_acc.at[m, :, others[f]], lambda f: recv2.at[m, f], 2)
        yield
        wait(copies)
        x_acc[m] = (q_acc[m, :, own] + recv2[m, 1]) + (recv2[m, 0] + recv2[m, 2])
        copies = send(2, lambda f: x_acc.at[m], lambda f: recv3.at[m, f], 4)
        yield
        wait(copies)
        g_sum[m, rows, own] = (x_acc[m] + recv3[m, 1]) + (recv3[m, 0] + recv3[m, 2])
        part = g_sum.at[m, rows, own]
        copies = send(3, lambda f: part, lambda f: part, 2)
        yield
        wait(copies)
        whole = g_sum.at[m, rows, pl.ds(0, D)]
        copies = send(4, lambda f: whole, lambda f: whole, 0)
        yield
        wait(copies)
        half = g_sum.at[m, pl.ds(keep, 32), pl.ds(0, D)]
        copy = remote(half, half, c_send.at[1, m], c_arrive.at[1, m], twin)
        yield
        copy.wait_recv()

    gc = [gram_chain(j) for j in range(3)]
    ac = [g_chain(m) for m in range(MATS)]
    factor = None

    p_stage = [0, 0, 0]
    for step, (what, i) in enumerate(ORDER):
        while sent and sent[0][0] <= step - LAG:
            sent.pop(0)[1].wait_send()
        if what == "products":
            local_p(i)
            if i == 0:
                pl.semaphore_wait(barrier, len(everyone))
        elif what == "p":
            p_step(p_stage[i], i)
            p_stage[i] += 1
            if p_stage[i] == 4:
                for k in range(3):
                    p_copy(k, i).wait_send()
        elif what == "gram":
            next(gc[i], None)
        elif what == "terms":
            local_g(i)
        elif what == "sum":
            next(ac[i], None)
        else:
            if factor is None:
                factor = eliminate([gram_out[j] for j in range(3)], y_out, p_out, lhs_err, lhs_q)
            for _ in range(i):
                next(factor, None)
    for _ in factor:
        pass
    for _, copy in sent:
        copy.wait_send()


def finish_kernel(g_sum, lhs_err, lhs_q, m_ref, err_hbm, q_out, ebuf, new_q, wst, store_sem, q_sem):
    stores = []
    for m in range(MATS):
        gh, gl = split(g_sum[m, :, :D] * 0.25)
        wst[0, 0:64] = gh
        wst[0, 64:128] = gh
        wst[0, 128:192] = gl
        fresh = dot(lhs_q[m, :, :192], wst[0])
        new_q[m] = fresh
        store = pltpu.make_async_copy(new_q.at[m], q_out.at[m], q_sem.at[m])
        store.start()
        stores.append(store)
        nh, nl = split(fresh)
        wst[1, 0:64] = nh
        wst[1, 64:128] = nh
        wst[1, 128:192] = nl
        for i, (start, size) in enumerate(COLS):
            cols = slice(start, start + size)
            ebuf[m, :, cols] = m_ref[m, :, cols] - dot(lhs_err[m, :, :192], wst[1, :, cols])
            place = pl.ds(start, size)
            store = pltpu.make_async_copy(
                ebuf.at[m, :, place], err_hbm.at[0, m, :, place], store_sem.at[m, i]
            )
            store.start()
            stores.append(store)
    for store in stores:
        store.wait()


def body(gradients, errors, previous_q):
    vmem = pl.BlockSpec(memory_space=pltpu.VMEM)
    far_hbm = pl.BlockSpec(memory_space=pltpu.HBM)
    sem = pltpu.SemaphoreType.DMA
    g_sum, lhs_err, lhs_q, merged = pl.pallas_call(
        comm_kernel,
        out_shape=(
            jax.ShapeDtypeStruct((MATS, R, 4 * BLOCK), f32),
            jax.ShapeDtypeStruct((MATS, ROWS, 256), bf16),
            jax.ShapeDtypeStruct((MATS, R, 256), bf16),
            jax.ShapeDtypeStruct((MATS, ROWS, D), f32),
        ),
        in_specs=[far_hbm, far_hbm, far_hbm],
        out_specs=(vmem, vmem, vmem, vmem),
        scratch_shapes=[
            pltpu.VMEM((MATS // 2, ROWS, 2 * R), f32),
            pltpu.VMEM((8 * R, 2 * R), f32),
            pltpu.VMEM((MATS, ROWS, D), bf16),
            pltpu.VMEM((MATS, R, D), f32),
            pltpu.VMEM((MATS, ROWS, D), bf16),
            pltpu.VMEM((MATS, ROWS, D), bf16),
            pltpu.VMEM((2, 256, D), bf16),
            pltpu.VMEM((MATS // 2, ROWS, 128), f32),
            pltpu.VMEM((MATS // 2, HALF, 128), f32),
            pltpu.VMEM((MATS // 2, HALF, 128), f32),
            pltpu.VMEM((MATS // 2, HALF, 128), f32),
            pltpu.VMEM((MATS, R, D), f32),
            pltpu.VMEM((MATS, 32, D), f32),
            pltpu.VMEM((MATS, 3, 8, D), f32),
            pltpu.VMEM((MATS, 8, 4 * BLOCK), f32),
            pltpu.VMEM((MATS, 8, BLOCK), f32),
            pltpu.VMEM((MATS, 3, 8, BLOCK), f32),
            pltpu.VMEM((MATS, 3, 8, BLOCK), f32),
            pltpu.VMEM((MATS // 2, R, 2 * R), f32),
            pltpu.VMEM((MATS // 2, 3, R // 2, 2 * R), f32),
            pltpu.VMEM((MATS // 2, 3, 3, R // 2, 2 * R), f32),
            pltpu.VMEM((MATS // 2, R, 2 * R), f32),
            sem((MATS, 3)),
            sem((3, 3)),
            sem((3, 3)),
            sem((2, MATS)),
            sem((2, MATS)),
            sem((5, MATS, 3)),
            sem((5, MATS, 3)),
            sem((3, 3, 3)),
            sem((3, 3, 3)),
        ],
        compiler_params=pltpu.CompilerParams(
            collective_id=0, has_side_effects=True, vmem_limit_bytes=40 * 2**20
        ),
        name="compress_and_sum",
    )(*[pltpu.with_memory_space_constraint(v, pltpu.HBM) for v in (gradients, errors, previous_q)])
    return pl.pallas_call(
        finish_kernel,
        out_shape=(
            jax.ShapeDtypeStruct((1, MATS, ROWS, D), f32),
            jax.ShapeDtypeStruct((MATS, R, D), f32),
        ),
        in_specs=[vmem, vmem, vmem, vmem],
        out_specs=(far_hbm, far_hbm),
        scratch_shapes=[
            pltpu.VMEM((MATS, ROWS, D), f32),
            pltpu.VMEM((MATS, R, D), f32),
            pltpu.VMEM((2, ROWS, D), bf16),
            sem((MATS, 3)),
            sem((MATS,)),
        ],
        compiler_params=pltpu.CompilerParams(vmem_limit_bytes=24 * 2**20),
        name="new_q_and_errors",
    )(g_sum, lhs_err, lhs_q, merged)


def solution(mesh):
    in_specs = (P("dp", None, "mp", None), P("dp", None, "mp", None), P())
    out_specs = (P("dp", None, "mp", None), P())
    return jax.shard_map(body, mesh=mesh, in_specs=in_specs, out_specs=out_specs, check_vma=False)
```
